32 devices in a mesh: pair: 8 (over y, x, core), view: 4 (over z).
Axes of the slice: x: 2, y: 2, z: 4, core: 2. Of those that a mesh axis runs over, the one named last changes fastest.
Arguments:
- tokens: bfloat16 [8, 1536, 1024], P('pair', 'view'), may hold values from -6 to 6
- out_grad: bfloat16 [8, 1536, 768], P('pair', 'view'), may hold values from -6 to 6
- masks: int32 [8, 1536], P('pair', 'view'), may hold values from 0 to 1, as said below
- coords: int32 [2, 8, 1536], P(None, 'pair'), may hold values from 0 to 38, as said below
- enc_qkv: bfloat16 [1024, 3072], replicated, may hold values from -0.1875 to 0.1875
- enc_out: bfloat16 [1024, 1024], replicated, may hold values from -1.5 to 1.5
- enc_up: bfloat16 [1024, 4096], replicated, may hold values from -0.1875 to 0.1875
- enc_down: bfloat16 [4096, 1024], replicated, may hold values from -0.09375 to 0.09375
- enc_gains: bfloat16 [2048], replicated, may hold values from 0.25 to 1.75
- enc_biases: bfloat16 [12032], replicated, may hold values from -1.1953125 to 1.1953125
- proj: bfloat16 [1024, 768], replicated, may hold values from -0.1875 to 0.1875
- dec_in: bfloat16 [768, 15360], P(None, 'view'), may hold values from -0.21875 to 0.21875
- dec_outs: bfloat16 [768, 3072], P(None, 'view'), may hold values from -1.75 to 1.75
- dec_down: bfloat16 [3072, 1536], P(None, 'view'), may hold values from -0.109375 to 0.109375
- dec_gains: bfloat16 [6144], P('view'), may hold values from 0.25 to 1.75
- dec_biases: bfloat16 [26112], P('view'), may hold values from -1.1953125 to 1.1953125
Outputs:
- mixed: bfloat16 [8, 1536, 768], P('pair', 'view')
- tokens_grad: float32 [8, 1536, 1024], P('pair', 'view')
- enc_qkv_grad: float32 [1024, 3072], P('pair', 'view')
- enc_out_grad: float32 [1024, 1024], P('pair', 'view')
- enc_up_grad: float32 [1024, 4096], P('pair', 'view')
- enc_down_grad: float32 [4096, 1024], P('pair', 'view')
- enc_gains_grad: float32 [2048], replicated
- enc_biases_grad: float32 [12032], replicated
- proj_grad: float32 [1024, 768], P('pair', 'view')
- dec_in_grad: float32 [768, 15360], P('pair', 'view')
- dec_outs_grad: float32 [768, 3072], P('pair', 'view')
- dec_down_grad: float32 [3072, 1536], P('pair', 'view')
- dec_gains_grad: float32 [6144], P('view')
- dec_biases_grad: float32 [26112], P('view')
The draws below stay inside these ranges and needn't reach their ends.
Inputs may be any that keep to these rules, and one draw needn't show every extreme that they name: `masks`: each view's patches are valid (1) with a probability of its own, drawn from 10 to 100 percent. `coords`: each view's coordinates are the cells of a 24 x 32 grid in an order drawn from the seed, shifted by an offset of 0 to 7 in each direction, drawn for each view.
All inputs are finite; a program needn't handle non-finite values.
Results may differ from the reference program's by a relative error of at most 0.02.
Values may be sent and summed in bfloat16 or wider, within the bound.
A program may use at most 320 MiB of HBM per device.

```python
import jax
import jax.numpy as jnp
from jax import lax

DE = 1024
HE = 16
FE = 4096
DD = 768
HD = 12
FD = 3072
GRID_W = 32
VIEWLEN = 768
PAIRS = 8


def draw_masks(key, part):
    key = jax.random.fold_in(key, 11)
    share_key, cell_key = jax.random.split(key)
    percent = jax.random.randint(share_key, (PAIRS, 2, 1), 10, 101)
    ticket = jax.random.randint(cell_key, (PAIRS, 2, VIEWLEN), 0, 100)
    return (ticket < percent).astype(jnp.int32).reshape(PAIRS, 2 * VIEWLEN)


def draw_coords(key, part):
    key = jax.random.fold_in(key, 23)
    order_key, shift_key = jax.random.split(key)
    cell_ids = jnp.arange(VIEWLEN, dtype=jnp.int32)
    orders = jax.vmap(lambda sub_key: jax.random.permutation(sub_key, cell_ids))(jax.random.split(order_key, PAIRS * 2))
    shifts = jax.random.randint(shift_key, (2, PAIRS * 2, 1), 0, 8)
    row_pos = orders // GRID_W + shifts[0]
    col_pos = orders % GRID_W + shifts[1]
    return jnp.stack([row_pos, col_pos]).reshape(2, PAIRS, 2 * VIEWLEN).astype(jnp.int32)


def with_spikes(drawn, own_key, source, target, shards_of, factor):
    owner, partner = [(jnp.arange(drawn.shape[dim]) // (drawn.shape[dim] // shards_of)).reshape([-1 if axis == dim else 1 for axis in range(drawn.ndim)]) for dim in (source, target)]
    chosen = jax.random.permutation(own_key, shards_of)[partner]
    strong = (owner == chosen) | (owner == (partner + shards_of // 2) % shards_of)
    return jnp.where(strong, factor * drawn, drawn)


def levels(own_key, extent, cuts, least, largest):
    gain, own = 1.0, jax.random.fold_in(own_key, 6)
    for dim, parts in cuts:
        draws = jnp.exp(jax.random.uniform(jax.random.fold_in(own, dim), (parts,), jnp.float32, least / len(cuts), largest / len(cuts)))
        gain = gain * jnp.repeat(draws, extent[dim] // parts).reshape([-1 if axis == dim else 1 for axis in range(len(extent))])
    return gain


def noise(stream_key, extent, scale, limit, shards=(), kind=jnp.bfloat16):
    drawn = scale * jax.random.normal(stream_key, extent, jnp.float32)
    if shards:
        drawn = drawn * levels(stream_key, extent, shards, -0.22, 0.18)
    return jnp.clip(drawn, -limit, limit).astype(kind)


def heavy_noise(key, extent, deviation, bound, cuts, heavy, held_as=jnp.bfloat16):
    array = deviation * jax.random.normal(key, extent, jnp.float32)
    if cuts:
        array = array * levels(key, extent, cuts, -0.22, 0.18)
    return jnp.clip(with_spikes(array, jax.random.fold_in(key, 3), *heavy), -bound, bound).astype(held_as)


def setup_inputs(seed: int = 0) -> dict:
    streams_of = jax.random.split(jax.random.key(seed), 17)
    return {
        "tokens": heavy_noise(streams_of[0], (PAIRS, 2 * VIEWLEN, DE), 1.0, 6.0, ((0, 8), (1, 4)), (0, 2, 8, 2.0)),
        "out_grad": noise(streams_of[1], (PAIRS, 2 * VIEWLEN, DD), 1.0, 6.0, ((0, 8), (1, 4))),
        "masks": draw_masks(jax.random.fold_in(streams_of[16], 71), 0),
        "coords": draw_coords(jax.random.fold_in(streams_of[16], 71), 0),
        "enc_qkv": noise(streams_of[4], (DE, 3 * DE), DE ** -0.5, 0.1875),
        "enc_out": noise(streams_of[5], (DE, DE), (DE // 64) ** -0.5, 1.5),
        "enc_up": noise(streams_of[6], (DE, FE), DE ** -0.5, 0.1875),
        "enc_down": noise(streams_of[7], (FE, DE), FE ** -0.5, 0.09375),
        "enc_gains": jnp.clip(1.0 + 0.15 * jax.random.normal(streams_of[8], (2 * DE,), jnp.float32), 0.25, 1.75).astype(jnp.bfloat16),
        "enc_biases": noise(streams_of[9], (7 * DE + FE + DD,), 0.2, 1.1953125),
        "proj": noise(streams_of[10], (DE, DD), DE ** -0.5, 0.1875),
        "dec_in": noise(streams_of[11], (DD, 2 * (6 * DD + FD)), DD ** -0.5, 0.21875, ((1, 4),)),
        "dec_outs": noise(streams_of[12], (DD, 4 * DD), (DD // 64) ** -0.5, 1.75, ((1, 4),)),
        "dec_down": noise(streams_of[13], (FD, 2 * DD), FD ** -0.5, 0.109375, ((1, 4),)),
        "dec_gains": jnp.clip(1.0 + 0.15 * jax.random.normal(streams_of[14], (8 * DD,), jnp.float32), 0.25, 1.75).astype(jnp.bfloat16),
        "dec_biases": noise(streams_of[15], (2 * (13 * DD + FD),), 0.2, 1.1953125, ((0, 4),)),
    }


@jax.custom_vjp
def low(v):
    return lax.optimization_barrier(v.astype(jnp.bfloat16)).astype(jnp.float32)

@jax.custom_vjp
def low_back(v):
    return v

def low_keep(v):
    return (low(v), None)

def low_pass(kept, grad):
    return (grad,)

def back_keep(v):
    return (v, None)

def back_low(kept, grad):
    return (low(grad),)
low.defvjp(low_keep, low_pass)
low_back.defvjp(back_keep, back_low)
norm_eps = 1e-06

def mat_mul(left, right):
    return jnp.dot(left, right, precision=lax.Precision.HIGHEST)

def norm_rows(inputs, scale_row, shift_row):
    average = lax.optimization_barrier(jnp.mean(inputs, axis=-1, keepdims=True))
    centred = inputs - average
    spread = lax.optimization_barrier(jnp.mean(centred * centred, axis=-1, keepdims=True))
    return centred * lax.rsqrt(spread + norm_eps) * scale_row + shift_row

def rotary(tensor, row_pos, col_pos):
    half_size = tensor.shape[-1] // 2
    frequency = 100.0 ** (-jnp.arange(0, half_size, 2).astype(jnp.float32) / half_size)

    def turn_part(segment, position):
        angles = position[..., None] * frequency
        angles = jnp.concatenate([angles, angles], axis=-1)[..., None, :]
        first_half, second_half = jnp.split(segment, 2, axis=-1)
        rolled = jnp.concatenate([-second_half, first_half], axis=-1)
        return segment * jnp.cos(angles) + rolled * jnp.sin(angles)
    return jnp.concatenate([turn_part(tensor[..., :half_size], row_pos), turn_part(tensor[..., half_size:], col_pos)], axis=-1)

def to_heads(tensor, head_count):
    return tensor.reshape(tensor.shape[0], head_count, tensor.shape[1] // head_count)

def unpack_cols(view_cols, widths):
    blocks = jnp.split(view_cols, 2, axis=-1)
    pieces = []
    offset = 0
    for width in widths:
        pieces.append(blocks[0][:, offset:offset + width // 2])
        pieces.append(blocks[1][:, offset:offset + width // 2])
        offset += width // 2
    return jnp.concatenate(pieces, axis=-1)

def attend(queries, key_rows, value_rows):
    factor = queries.shape[-1] ** (-0.5)
    scores = low_back(jnp.einsum('qhd,khd->hqk', queries, key_rows, precision=lax.Precision.HIGHEST) * factor)
    chances = jax.nn.softmax(scores, axis=-1)
    mixed_rows = jnp.einsum('hqk,khd->qhd', low(chances), value_rows, precision=lax.Precision.HIGHEST)
    return low(low_back(mixed_rows)).reshape(mixed_rows.shape[0], -1)

def exact_gelu(values):
    return jax.nn.gelu(values, approximate=False)

def encode(inputs, row_pos, col_pos, qkv_w, out_w, up_w, down_w, scales, shifts, proj_w):
    start = 4 * DE + FE
    b_qkv = shifts[:3 * DE]
    b_out = shifts[3 * DE:4 * DE]
    b_up = shifts[4 * DE:start]
    b_down = shifts[start:start + DE]
    shift_one = shifts[start + DE:start + 2 * DE]
    shift_two = shifts[start + 2 * DE:start + 3 * DE]
    b_proj = shifts[start + 3 * DE:start + 3 * DE + DD]
    normed = norm_rows(inputs, scales[:DE], shift_one)
    joined = low_back(mat_mul(low(normed), qkv_w) + b_qkv)
    query_lin, key_lin, value_lin = jnp.split(joined, 3, axis=-1)
    queries = low(rotary(to_heads(query_lin, HE), row_pos, col_pos))
    key_rows = low(rotary(to_heads(key_lin, HE), row_pos, col_pos))
    value_rows = low(to_heads(value_lin, HE))
    after_attn = inputs + low_back(mat_mul(attend(queries, key_rows, value_rows), out_w) + b_out)
    normed_two = norm_rows(after_attn, scales[DE:], shift_two)
    up_lin = low_back(mat_mul(low(normed_two), up_w) + b_up)
    after_mlp = after_attn + low_back(mat_mul(low(exact_gelu(up_lin)), down_w) + b_down)
    return low(low_back(mat_mul(low(after_mlp), proj_w) + b_proj))

def decode(own_input, other_input, own_rows, own_cols, other_rows, other_cols, in_w, outs_w, down_w, scales, shifts):
    normed_a = norm_rows(own_input, scales[:DD], shifts[:DD])
    self_lin = low_back(mat_mul(low(normed_a), in_w[:, :3 * DD]) + shifts[4 * DD:7 * DD])
    query_lin, key_lin, value_lin = jnp.split(self_lin, 3, axis=-1)
    queries = low(rotary(to_heads(query_lin, HD), own_rows, own_cols))
    key_rows = low(rotary(to_heads(key_lin, HD), own_rows, own_cols))
    value_rows = low(to_heads(value_lin, HD))
    after_self = own_input + low_back(mat_mul(attend(queries, key_rows, value_rows), outs_w[:, :DD]) + shifts[7 * DD:8 * DD])
    normed_b = norm_rows(after_self, scales[DD:2 * DD], shifts[DD:2 * DD])
    cross_q_lin = low_back(mat_mul(low(normed_b), in_w[:, 3 * DD:4 * DD]) + shifts[8 * DD:9 * DD])
    normed_c = norm_rows(other_input, scales[2 * DD:3 * DD], shifts[2 * DD:3 * DD])
    cross_lin = low_back(mat_mul(low(normed_c), in_w[:, 4 * DD:6 * DD]) + shifts[9 * DD:11 * DD])
    cross_queries = low(rotary(to_heads(cross_q_lin, HD), own_rows, own_cols))
    cross_keys = low(rotary(to_heads(cross_lin[:, :DD], HD), other_rows, other_cols))
    cross_values = low(to_heads(cross_lin[:, DD:], HD))
    after_cross = after_self + low_back(mat_mul(attend(cross_queries, cross_keys, cross_values), outs_w[:, DD:]) + shifts[11 * DD:12 * DD])
    normed_d = norm_rows(after_cross, scales[3 * DD:], shifts[3 * DD:4 * DD])
    up_lin = low_back(mat_mul(low(normed_d), in_w[:, 6 * DD:]) + shifts[12 * DD:12 * DD + FD])
    return after_cross + low_back(mat_mul(low(exact_gelu(up_lin)), down_w) + shifts[12 * DD + FD:])

def pair_layer(params, inputs, row_pos, col_pos):
    qkv_w, out_w, up_w, down_w, enc_scale, enc_shift, proj_w, in_w, outs_w, dec_down_w, dec_scale, dec_shift = params
    in_width = 6 * DD + FD
    bias_width = 13 * DD + FD
    encoded = []
    for which_view in range(2):
        row_range = slice(which_view * VIEWLEN, (which_view + 1) * VIEWLEN)
        encoded.append(encode(inputs[row_range], row_pos[row_range], col_pos[row_range], qkv_w, out_w, up_w, down_w, enc_scale, enc_shift, proj_w))
    results = []
    for which_view in range(2):
        own_range = slice(which_view * VIEWLEN, (which_view + 1) * VIEWLEN)
        other_range = slice((1 - which_view) * VIEWLEN, (2 - which_view) * VIEWLEN)
        results.append(decode(encoded[which_view], encoded[1 - which_view], row_pos[own_range], col_pos[own_range], row_pos[other_range], col_pos[other_range], unpack_cols(in_w[:, which_view * in_width:(which_view + 1) * in_width], (3 * DD, DD, 2 * DD, FD)), unpack_cols(outs_w[:, which_view * 2 * DD:(which_view + 1) * 2 * DD], (DD, DD)), dec_down_w[:, which_view * DD:(which_view + 1) * DD], dec_scale[which_view * 4 * DD:(which_view + 1) * 4 * DD], dec_shift[which_view * bias_width:(which_view + 1) * bias_width]))
    return jnp.concatenate(results, axis=0)

def reference(tokens, out_grad, masks, coords, enc_qkv, enc_out, enc_up, enc_down, enc_gains, enc_biases, proj, dec_in, dec_outs, dec_down, dec_gains, dec_biases):
    params = tuple((weight.astype(jnp.float32) for weight in (enc_qkv, enc_out, enc_up, enc_down, enc_gains, enc_biases, proj, dec_in, dec_outs, dec_down, dec_gains, dec_biases)))

    def one_pair(totals, pieces):
        inputs, cotangent, valid, places = pieces
        row_pos = places[0].astype(jnp.float32)
        col_pos = places[1].astype(jnp.float32)
        outputs, pull_back = jax.vjp(lambda weights, acts: pair_layer(weights, acts, row_pos, col_pos), params, inputs.astype(jnp.float32))
        weight_grads, input_grad = pull_back(cotangent.astype(jnp.float32) * valid.astype(jnp.float32)[:, None])
        totals = jax.tree.map(jnp.add, totals, weight_grads)
        return (totals, (outputs.astype(jnp.bfloat16), input_grad))
    zeros_start = jax.tree.map(jnp.zeros_like, params)
    totals, (outputs, input_grads) = lax.scan(one_pair, zeros_start, (tokens, out_grad, masks, jnp.moveaxis(coords, 1, 0)))
    return (outputs, input_grads, totals[0], totals[1], totals[2], totals[3], totals[4], totals[5], totals[6], totals[7], totals[8], totals[9], totals[10], totals[11])
```

```python
from functools import partial

import jax
import jax.numpy as jnp
from jax import lax
from jax.experimental import pallas as pl
from jax.experimental.pallas import tpu as pltpu
from jax.sharding import PartitionSpec as P

DE = 1024
HE = 16
FE = 4096
DD = 768
HD = 12
FD = 3072

norm_eps = 1e-06
BF = jnp.bfloat16
F32 = jnp.float32
VMEM = 58 * 1024 * 1024

NN = (((1,), (0,)), ((), ()))
NT = (((1,), (1,)), ((), ()))
TN = (((0,), (0,)), ((), ()))


def mm(a, b, dims=NN):
    return lax.dot_general(a, b, dims, preferred_element_type=F32)


def full(shape):
    zeros = (0,) * len(shape)
    return pl.BlockSpec(shape, lambda *_: zeros)


def sds(shape, dtype):
    return jax.ShapeDtypeStruct(shape, dtype)


def call(body, name, grid, in_specs, out_specs, out_shape, scratch=(), flops=0, nbytes=0):
    return pl.pallas_call(
        body,
        grid=grid,
        in_specs=in_specs,
        out_specs=out_specs,
        out_shape=out_shape,
        scratch_shapes=list(scratch),
        name=name,
        compiler_params=pltpu.CompilerParams(vmem_limit_bytes=VMEM),
        cost_estimate=pl.CostEstimate(flops=flops, bytes_accessed=nbytes, transcendentals=0),
    )


def norm_parts(x):
    centred = x - jnp.mean(x, axis=-1, keepdims=True)
    rstd = lax.rsqrt(jnp.mean(centred * centred, axis=-1, keepdims=True) + norm_eps)
    return centred * rstd, rstd


def norm_back(dy, x, gain):
    xhat, rstd = norm_parts(x)
    dgain = jnp.sum(dy * xhat, axis=0, keepdims=True)
    dshift = jnp.sum(dy, axis=0, keepdims=True)
    dxh = dy * gain
    mean_one = jnp.mean(dxh, axis=-1, keepdims=True)
    mean_two = jnp.mean(dxh * xhat, axis=-1, keepdims=True)
    return rstd * (dxh - mean_one - xhat * mean_two), dgain, dshift


def turn(u, cos, sin):
    lane = lax.broadcasted_iota(jnp.int32, u.shape, 1)
    other = jnp.where(lane % 32 < 16, pltpu.roll(u, 112, 1), pltpu.roll(u, 16, 1))
    return u * cos + other * sin


def turn_cols(y, cos, sin):
    return jnp.concatenate(
        [turn(y[:, i : i + 128], cos, sin) for i in range(0, y.shape[1], 128)], axis=1
    )


def gelu_parts(u):
    z = jnp.abs(u) * 0.7071067811865476
    t = 1.0 / (1.0 + 0.3275911 * z)
    e = jnp.exp(-0.5 * u * u)
    poly = t * (
        0.254829592
        + t * (-0.284496736 + t * (1.421413741 + t * (-1.453152027 + t * 1.061405429)))
    )
    tail = 0.5 * poly * e
    phi = jnp.where(u >= 0, 1.0 - tail, tail)
    return u * phi, phi + u * e * 0.3989422804014327


def col_sum(g):
    return jnp.sum(g.astype(F32), axis=0, keepdims=True)


def lnproj(x, gain, shift, w, b, cos, sin, n_q, n_turn, n_all, name):
    rows, width = x.shape
    bn = w.shape[1] // n_all
    has_q = n_q > 0

    def body(x_ref, g_ref, s_ref, w_ref, b_ref, c_ref, sn_ref, *rest):
        if has_q:
            q_ref, kv_ref, t_ref, nrm = rest
        else:
            kv_ref, t_ref, nrm = rest
        j = pl.program_id(0)

        @pl.when(j == 0)
        def _():
            xhat, _ = norm_parts(x_ref[...].astype(F32))
            low = (xhat * g_ref[...] + s_ref[...]).astype(BF)
            nrm[...] = low
            t_ref[...] = low.T

        y = mm(nrm[...], w_ref[...]) + b_ref[...]

        @pl.when(j < n_turn)
        def _():
            out = turn_cols(y, c_ref[...], sn_ref[...]).astype(BF)
            if has_q:

                @pl.when(j < n_q)
                def _():
                    q_ref[...] = out

                @pl.when(j >= n_q)
                def _():
                    kv_ref[...] = out

            else:
                kv_ref[...] = out

        @pl.when(j >= n_turn)
        def _():
            kv_ref[...] = y.astype(BF)

    outs = [
        sds((rows, bn * (n_all - n_q)), BF),
        sds((width, rows), BF),
    ]
    specs = [
        pl.BlockSpec((rows, bn), lambda j: (0, jnp.maximum(j - n_q, 0))),
        full((width, rows)),
    ]
    if has_q:
        outs.insert(0, sds((rows, bn * n_q), BF))
        specs.insert(0, pl.BlockSpec((rows, bn), lambda j: (0, jnp.minimum(j, n_q - 1))))
    return call(
        body,
        name,
        (n_all,),
        [
            full((rows, width)),
            full((1, width)),
            full((1, width)),
            pl.BlockSpec((width, bn), lambda j: (0, j)),
            pl.BlockSpec((1, bn), lambda j: (0, j)),
            full((rows, 128)),
            full((rows, 128)),
        ],
        specs,
        outs,
        [pltpu.VMEM((rows, width), BF)],
        2 * rows * width * w.shape[1],
        2 * width * w.shape[1] + 4 * rows * w.shape[1],
    )(x, gain, shift, w, b, cos, sin)


def two_heads(block):
    first = lax.broadcasted_iota(jnp.int32, block.shape, 1) < 64
    zero = jnp.zeros_like(block)
    return jnp.concatenate(
        [jnp.where(first, block, zero), jnp.where(first, zero, block)], axis=0
    )


def pick_heads(tall, rows):
    return jnp.concatenate([tall[:64, :rows], tall[64:, rows:]], axis=0)


def attend(q, kv, kvf, name):
    rows, width = q.shape
    pairs = width // 128
    keys = 2 * rows

    def body(q_ref, ko_ref, vo_ref, kf_ref, vf_ref, p_ref, o_ref, t_ref):
        q2 = two_heads(q_ref[...] * jnp.asarray(0.125, BF))
        k = jnp.concatenate([ko_ref[...], kf_ref[...]], axis=0)
        v = jnp.concatenate([vo_ref[...], vf_ref[...]], axis=0)
        vt = v.T
        pieces = []
        for c in range(0, 2 * rows, 256):
            s = mm(k, q2[c : c + 256], NT)
            e = jnp.exp(s - jnp.max(s, axis=0, keepdims=True))
            p = (e * (1.0 / jnp.sum(e, axis=0, keepdims=True))).astype(BF)
            p_ref[0, :, c : c + 256] = p
            pieces.append(mm(vt, p))
        t = pick_heads(jnp.concatenate(pieces, axis=1), rows)
        t_ref[...] = t.astype(BF)
        o_ref[...] = t.T.astype(BF)

    col = lambda j: (0, j)
    val = lambda j: (0, pairs + j)
    return call(
        body,
        name,
        (pairs,),
        [
            pl.BlockSpec((rows, 128), col),
            pl.BlockSpec((rows, 128), col),
            pl.BlockSpec((rows, 128), val),
            pl.BlockSpec((rows, 128), col),
            pl.BlockSpec((rows, 128), val),
        ],
        [
            pl.BlockSpec((1, keys, 2 * rows), lambda j: (j, 0, 0)),
            pl.BlockSpec((rows, 128), col),
            pl.BlockSpec((128, rows), lambda j: (j, 0)),
        ],
        [
            sds((pairs, keys, 2 * rows), BF),
            sds((rows, width), BF),
            sds((width, rows), BF),
        ],
        (),
        4 * rows * keys * width,
        pairs * keys * rows * 4,
    )(q, kv, kv, kvf, kvf)


def attend_back(q, kv, kvf, p, o, do, cos, sin, cos_all, sin_all, name):
    rows, width = q.shape
    pairs = width // 128
    keys = 2 * rows

    def body(
        q_ref, ko_ref, vo_ref, kf_ref, vf_ref, p_ref, o_ref, do_ref, c_ref, s_ref, ca_ref, sa_ref,
        gq_ref, own_ref, far_ref,
    ):
        q2 = two_heads(q_ref[...] * jnp.asarray(0.125, BF))
        k = jnp.concatenate([ko_ref[...], kf_ref[...]], axis=0)
        v = jnp.concatenate([vo_ref[...], vf_ref[...]], axis=0)
        kt = k.T
        do_low = do_ref[...]
        do2 = two_heads(do_low)
        prod = two_heads(do_low.astype(F32) * o_ref[...].astype(F32))
        inner = lax.dot_general(
            jnp.ones((8, 128), F32), prod, NT, precision=lax.Precision.HIGHEST,
            preferred_element_type=F32,
        )[:1]
        dk = jnp.zeros((keys, 128), F32)
        dv = jnp.zeros((keys, 128), F32)
        pieces = []
        for c in range(0, 2 * rows, 256):
            dp = mm(v, do2[c : c + 256], NT)
            pc = p_ref[0, :, c : c + 256]
            ds = (pc.astype(F32) * (dp - inner[:, c : c + 256])).astype(BF)
            dk += mm(ds, q2[c : c + 256])
            dv += mm(pc, do2[c : c + 256])
            pieces.append(mm(kt, ds))
        dq = pick_heads(jnp.concatenate(pieces, axis=1), rows).T * 0.125
        gq_ref[...] = turn(dq, c_ref[...], s_ref[...]).astype(BF)
        dk = turn(dk, ca_ref[...], sa_ref[...])
        own_ref[0] = dk[:rows]
        own_ref[1] = dv[:rows]
        far_ref[0] = dk[rows:].astype(BF)
        far_ref[1] = dv[rows:].astype(BF)

    col = lambda j: (0, j)
    val = lambda j: (0, pairs + j)
    both = pl.BlockSpec((2, rows, 128), lambda j: (0, 0, j))
    return call(
        body,
        name,
        (pairs,),
        [
            pl.BlockSpec((rows, 128), col),
            pl.BlockSpec((rows, 128), col),
            pl.BlockSpec((rows, 128), val),
            pl.BlockSpec((rows, 128), col),
            pl.BlockSpec((rows, 128), val),
            pl.BlockSpec((1, keys, 2 * rows), lambda j: (j, 0, 0)),
            pl.BlockSpec((rows, 128), col),
            pl.BlockSpec((rows, 128), col),
            full((rows, 128)),
            full((rows, 128)),
            full((keys, 128)),
            full((keys, 128)),
        ],
        [pl.BlockSpec((rows, 128), col), both, both],
        [
            sds((rows, width), BF),
            sds((2, rows, width), F32),
            sds((2, rows, width), BF),
        ],
        (),
        8 * rows * keys * width,
        pairs * keys * rows * 4,
    )(q, kv, kv, kvf, kvf, p, o, do, cos, sin, cos_all, sin_all)


def ffn_forward(o, resid, wo, bo, gain, shift, w_up, b_up, w_down, b_down, head, bn, name):
    rows, width = o.shape
    hidden = w_up.shape[1]
    steps = hidden // bn

    def body(o_ref, r_ref, wo_ref, bo_ref, g_ref, s_ref, up_ref, bu_ref, dn_ref, bd_ref, *rest):
        if head:
            pj_ref, bp_ref, x1_ref, nt_ref, at_ref, gp_ref, z_ref, xt_ref, nrm, acc = rest
        else:
            x1_ref, nt_ref, at_ref, gp_ref, z_ref, nrm, acc = rest
        j = pl.program_id(0)

        @pl.when(j == 0)
        def _():
            x1 = r_ref[...].astype(F32) + mm(o_ref[...], wo_ref[...]) + bo_ref[...]
            x1_ref[...] = x1
            xhat, _ = norm_parts(x1)
            low = (xhat * g_ref[...] + s_ref[...]).astype(BF)
            nrm[...] = low
            nt_ref[...] = low.T
            acc[...] = x1 + bd_ref[...]

        u = mm(nrm[...], up_ref[...]) + bu_ref[...]
        act, slope = gelu_parts(u)
        act = act.astype(BF)
        gp_ref[...] = slope.astype(BF)
        at_ref[...] = act.T
        acc[...] += mm(act, dn_ref[...])

        @pl.when(j == steps - 1)
        def _():
            low = acc[...].astype(BF)
            if head:
                xt_ref[...] = low.T
                z_ref[...] = (mm(low, pj_ref[...]) + bp_ref[...]).astype(BF)
            else:
                z_ref[...] = low

    vec = full((1, width))
    in_specs = [
        full((rows, width)),
        full((rows, width)),
        full((width, width)),
        vec,
        vec,
        vec,
        pl.BlockSpec((width, bn), lambda j: (0, j)),
        pl.BlockSpec((1, bn), lambda j: (0, j)),
        pl.BlockSpec((bn, width), lambda j: (j, 0)),
        vec,
    ]
    out_specs = [
        full((rows, width)),
        full((width, rows)),
        pl.BlockSpec((bn, rows), lambda j: (j, 0)),
        pl.BlockSpec((rows, bn), lambda j: (0, j)),
    ]
    outs = [
        sds((rows, width), F32),
        sds((width, rows), BF),
        sds((hidden, rows), BF),
        sds((rows, hidden), BF),
    ]
    args = [o, resid, wo, bo, gain, shift, w_up, b_up, w_down, b_down]
    if head:
        wide = head[0].shape[1]
        in_specs += [full((width, wide)), full((1, wide))]
        args += list(head)
        out_specs += [full((rows, wide)), full((width, rows))]
        outs += [sds((rows, wide), BF), sds((width, rows), BF)]
    else:
        out_specs += [full((rows, width))]
        outs += [sds((rows, width), BF)]
    return call(
        body,
        name,
        (steps,),
        in_specs,
        out_specs,
        outs,
        [pltpu.VMEM((rows, width), BF), pltpu.VMEM((rows, width), F32)],
        4 * rows * width * hidden + 2 * rows * width * width,
        4 * width * hidden + 4 * rows * hidden,
    )(*args)


def ffn_backward(source, w_down, slope, w_up, x, gain, wo, bn, name):
    rows, width = x.shape
    hidden = w_up.shape[1]
    steps = hidden // bn
    enc = len(source) == 3

    def body(*refs):
        src, refs = refs[: len(source)], refs[len(source) :]
        dn_ref, gp_ref, up_ref, x_ref, g_ref, wo_ref, *refs = refs
        gd_ref, gu_ref, go_ref, gx_ref, do_ref, bd_ref, bu_ref, dg_ref, ds_ref, bo_ref, *refs = refs
        if enc:
            gp_out, bp_ref, *refs = refs
        acc, start = refs
        j = pl.program_id(0)

        @pl.when(j == 0)
        def _():
            if enc:
                low = (src[0][...] + src[1][...].astype(F32)).astype(BF)
                gp_out[...] = low
                bp_ref[...] = col_sum(low)
                first = mm(low, src[2][...], NT)
            else:
                first = src[0][...].astype(F32) * src[1][...]
            start[...] = first
            gd = first.astype(BF)
            gd_ref[...] = gd
            bd_ref[...] = col_sum(gd)
            acc[...] = jnp.zeros_like(acc)

        gu = (mm(gd_ref[...], dn_ref[...], NT) * gp_ref[...].astype(F32)).astype(BF)
        gu_ref[...] = gu
        bu_ref[...] = col_sum(gu)
        acc[...] += mm(gu, up_ref[...], NT)

        @pl.when(j == steps - 1)
        def _():
            dx, dg, ds = norm_back(acc[...], x_ref[...], g_ref[...])
            dg_ref[...] = dg
            ds_ref[...] = ds
            total = start[...] + dx
            gx_ref[...] = total
            go = total.astype(BF)
            go_ref[...] = go
            bo_ref[...] = col_sum(go)
            do_ref[...] = mm(go, wo_ref[...], NT).astype(BF)

    vec = full((1, width))
    whole = full((rows, width))
    if enc:
        wide = source[2].shape[1]
        src_specs = [full((rows, wide)), full((rows, wide)), full((width, wide))]
    else:
        src_specs = [whole, full((rows, 1))]
    in_specs = src_specs + [
        pl.BlockSpec((bn, width), lambda j: (j, 0)),
        pl.BlockSpec((rows, bn), lambda j: (0, j)),
        pl.BlockSpec((width, bn), lambda j: (0, j)),
        whole,
        vec,
        full((width, width)),
    ]
    out_specs = [
        whole,
        pl.BlockSpec((rows, bn), lambda j: (0, j)),
        whole,
        whole,
        whole,
        vec,
        pl.BlockSpec((1, bn), lambda j: (0, j)),
        vec,
        vec,
        vec,
    ]
    row = sds((1, width), F32)
    outs = [
        sds((rows, width), BF),
        sds((rows, hidden), BF),
        sds((rows, width), BF),
        sds((rows, width), F32),
        sds((rows, width), BF),
        row,
        sds((1, hidden), F32),
        row,
        row,
        row,
    ]
    if enc:
        out_specs += [full((rows, wide)), full((1, wide))]
        outs += [sds((rows, wide), BF), sds((1, wide), F32)]
    return call(
        body,
        name,
        (steps,),
        in_specs,
        out_specs,
        outs,
        [pltpu.VMEM((rows, width), F32), pltpu.VMEM((rows, width), F32)],
        4 * rows * width * hidden + 2 * rows * width * width,
        4 * width * hidden + 4 * rows * hidden,
    )(*source, w_down, slope, w_up, x, gain, wo)


def mid_forward(o, resid, wo, bo, gain, shift, w, b, cos, sin, name):
    rows, width = o.shape

    def body(o_ref, r_ref, wo_ref, bo_ref, g_ref, s_ref, w_ref, b_ref, c_ref, sn_ref, y_ref, q_ref, t_ref):
        y = r_ref[...].astype(F32) + mm(o_ref[...], wo_ref[...]) + bo_ref[...]
        y_ref[...] = y
        xhat, _ = norm_parts(y)
        low = (xhat * g_ref[...] + s_ref[...]).astype(BF)
        t_ref[...] = low.T
        q = mm(low, w_ref[...]) + b_ref[...]
        q_ref[...] = turn_cols(q, c_ref[...], sn_ref[...]).astype(BF)

    whole, vec = full((rows, width)), full((1, width))
    square, table = full((width, width)), full((rows, 128))
    return call(
        body,
        name,
        (1,),
        [whole, whole, square, vec, vec, vec, square, vec, table, table],
        [whole, whole, full((width, rows))],
        [sds((rows, width), F32), sds((rows, width), BF), sds((width, rows), BF)],
        (),
        4 * rows * width * width,
        4 * width * width,
    )(o, resid, wo, bo, gain, shift, w, b, cos, sin)


def mid_backward(gq, w, x, gain, above, wo, name):
    rows, width = x.shape

    def body(gq_ref, w_ref, x_ref, g_ref, a_ref, wo_ref, gx_ref, go_ref, do_ref, bq_ref, dg_ref, ds_ref, bo_ref):
        low = gq_ref[...]
        bq_ref[...] = col_sum(low)
        dx, dg, ds = norm_back(mm(low, w_ref[...], NT), x_ref[...], g_ref[...])
        dg_ref[...] = dg
        ds_ref[...] = ds
        total = a_ref[...] + dx
        gx_ref[...] = total
        go = total.astype(BF)
        go_ref[...] = go
        bo_ref[...] = col_sum(go)
        do_ref[...] = mm(go, wo_ref[...], NT).astype(BF)

    whole, vec, square = full((rows, width)), full((1, width)), full((width, width))
    row = sds((1, width), F32)
    return call(
        body,
        name,
        (1,),
        [whole, square, whole, vec, whole, square],
        [whole, whole, whole, vec, vec, vec, vec],
        [sds((rows, width), F32), sds((rows, width), BF), sds((rows, width), BF), row, row, row, row],
        (),
        4 * rows * width * width,
        4 * width * width,
    )(gq, w, x, gain, above, wo)


def proj_backward(gq, own, back, w, x, gain, above, name):
    rows, width = x.shape
    parts = w.shape[1] // width
    has_q, has_above = gq is not None, above is not None

    def body(*refs):
        if has_q:
            gq_ref, *refs = refs
        own_ref, back_ref, w_ref, x_ref, g_ref, *refs = refs
        if has_above:
            a_ref, *refs = refs
        g_out, b_ref, gx_ref, dg_ref, ds_ref, acc = refs
        j = pl.program_id(0)
        summed = (own_ref[0] + back_ref[0].astype(F32)).astype(BF)
        if has_q:
            low = jnp.where(j == 0, gq_ref[...], summed)
        else:
            low = summed
        g_out[...] = low
        b_ref[...] = col_sum(low)
        piece = mm(low, w_ref[...], NT)

        @pl.when(j == 0)
        def _():
            acc[...] = piece

        @pl.when(j > 0)
        def _():
            acc[...] += piece

        @pl.when(j == parts - 1)
        def _():
            dx, dg, ds = norm_back(acc[...], x_ref[...].astype(F32), g_ref[...])
            dg_ref[...] = dg
            ds_ref[...] = ds
            gx_ref[...] = (a_ref[...] + dx if has_above else dx).astype(gx_ref.dtype)

    whole, vec = full((rows, width)), full((1, width))
    skip = 1 if has_q else 0
    part = pl.BlockSpec((1, rows, width), lambda j: (jnp.maximum(j - skip, 0), 0, 0))
    in_specs = [part, part, pl.BlockSpec((width, width), lambda j: (0, j)), whole, vec]
    args = [own, back, w, x, gain]
    if has_q:
        in_specs.insert(0, whole)
        args.insert(0, gq)
    if has_above:
        in_specs.append(whole)
        args.append(above)
    row = sds((1, width), F32)
    return call(
        body,
        name,
        (parts,),
        in_specs,
        [
            pl.BlockSpec((rows, width), lambda j: (0, j)),
            pl.BlockSpec((1, width), lambda j: (0, j)),
            whole,
            vec,
            vec,
        ],
        [
            sds((rows, width * parts), BF),
            sds((1, width * parts), F32),
            sds((rows, width), F32 if has_above else BF),
            row,
            row,
        ],
        [pltpu.VMEM((rows, width), F32)],
        2 * rows * width * width * parts,
        2 * width * width * parts,
    )(*args)


def weight_blocks(place, at, g, nz, width, first, subs, bn, name):
    features, rows = at.shape
    rb = features // 8
    per = width // bn
    units = bn // 128

    def body(place_ref, a_ref, g_ref, keep_ref, send_ref, lhs):
        @pl.when((pl.program_id(0) == 0) & (pl.program_id(1) == 0))
        def _():
            for s in range(8):
                lhs[s * rb : (s + 1) * rb, :] = a_ref[place_ref[s]]

        grad = g_ref[...]
        for half, out in enumerate((keep_ref, send_ref)):
            for c in range(0, 4, max(1, 512 // rb) if rb < 512 else 1):
                n = min(4 - c, max(1, 512 // rb) if rb < 512 else 1)
                base = half * 4 + c
                y = mm(lhs[base * rb : (base + n) * rb, :], grad).astype(BF)
                for s in range(n):
                    for u in range(units):
                        out[c + s, 0, u] = y[s * rb : (s + 1) * rb, u * 128 : (u + 1) * 128]

    out = sds((4, nz, subs * units, rb, 128), BF)
    block = pl.BlockSpec((4, 1, units, rb, 128), lambda i, j, _: (0, i, j, 0, 0))
    spec = pltpu.PrefetchScalarGridSpec(
        num_scalar_prefetch=1,
        grid=(nz, subs),
        in_specs=[
            pl.BlockSpec((8, rb, rows), lambda i, j, _: (0, 0, 0)),
            pl.BlockSpec((rows, bn), lambda i, j, place_ref: (0, place_ref[8 + i] * per + first + j)),
        ],
        out_specs=[block, block],
        scratch_shapes=[pltpu.VMEM((features, rows), BF)],
    )
    return pl.pallas_call(
        body,
        grid_spec=spec,
        out_shape=[out, out],
        name=name,
        compiler_params=pltpu.CompilerParams(vmem_limit_bytes=VMEM),
        cost_estimate=pl.CostEstimate(
            flops=2 * rows * features * nz * subs * bn,
            bytes_accessed=2 * features * nz * subs * bn,
            transcendentals=0,
        ),
    )(place, at.reshape(8, rb, rows), g)


def swap(value, axis, distance):
    size = lax.axis_size(axis)
    return lax.ppermute(value, axis, [(i, i ^ distance) for i in range(size)])


def plus(a, b):
    return (a.astype(F32) + b.astype(F32)).astype(BF)


def reduce_stream(blocks, first, second):
    got = [swap(send, "pair", 1) for _, send in blocks]
    total = jnp.concatenate([plus(keep, r) for (keep, _), r in zip(blocks, got)], axis=2)
    total = plus(total[0:2], swap(total[2:4], "pair", first))
    total = plus(total[0], swap(total[1], "pair", second))
    nz = total.shape[0]
    if nz == 4:
        total = plus(total[0:2], swap(total[2:4], "view", 1))
        return total[0].astype(F32) + swap(total[1], "view", 2).astype(F32)
    return total[0].astype(F32) + swap(total[1], "view", 1).astype(F32)


def spread(units):
    return jnp.transpose(units, (1, 0, 2)).reshape(units.shape[1], -1)


def tables(place):
    lane = jnp.arange(128)
    frequency = 100.0 ** (-(lane % 16).astype(F32) * 2.0 / 32.0)
    position = jnp.where((lane % 64 < 32)[None, :], place[0][:, None], place[1][:, None])
    angle = position * frequency[None, :]
    sin = jnp.sin(angle)
    return jnp.cos(angle), jnp.where((lane % 32 < 16)[None, :], -sin, sin)


def joined(mine, theirs, half_id, start, stop):
    a, b = mine[:, start:stop], theirs[:, start:stop]
    return jnp.where(
        half_id == 0, jnp.concatenate([a, b], axis=1), jnp.concatenate([b, a], axis=1)
    )


def local(
    tokens,
    out_grad,
    masks,
    coords,
    enc_qkv,
    enc_out,
    enc_up,
    enc_down,
    enc_gains,
    enc_biases,
    proj,
    dec_in,
    dec_outs,
    dec_down,
    dec_gains,
    dec_biases,
):
    n_pair, n_view = lax.axis_size("pair"), lax.axis_size("view")
    quarter, pair_id = lax.axis_index("view"), lax.axis_index("pair")
    half_id, view_id, core = quarter % 2, quarter // 2, pair_id % 2
    rows = tokens.shape[1]
    tokens, out_grad, masks = tokens[0], out_grad[0], masks[0]

    def trade(value):
        moves = []
        for p in range(n_pair):
            for t in range(n_view):
                moves.append((p * n_view + t, (p - p % 2 + t % 2) * n_view + t - t % 2 + p % 2))
        return lax.ppermute(value, ("pair", "view"), moves)

    tokens = trade(tokens)
    far_coords = swap(coords[:, 0], "pair", 1)
    place = jnp.where(core == half_id, coords[:, 0], far_coords).astype(F32)
    out_grad, masks = trade((out_grad, masks))

    def fetch(array):
        if array.shape[0] % (16 * n_pair):
            return swap(array, "view", 1)
        share = array.shape[0] // n_pair
        piece = lax.dynamic_slice_in_dim(array, pair_id * share, share, 0)
        return lax.all_gather(swap(piece, "view", 1), "pair", axis=0, tiled=True)

    s1, s2, s3, s4 = 3 * DD // 2, 2 * DD, 3 * DD, 3 * DD + FD // 2
    far_gains, far_biases = swap((dec_gains, dec_biases), "view", 1)
    far_attn = fetch(dec_in[:, :s3])
    far_outs = fetch(dec_outs)
    far_up = fetch(dec_in[:, s3:])
    far_down = fetch(dec_down)

    def join_row(mine, theirs):
        return jnp.where(
            half_id == 0, jnp.concatenate([mine, theirs]), jnp.concatenate([theirs, mine])
        ).astype(F32)[None]

    dec_scale, dec_shift = join_row(dec_gains, far_gains), join_row(dec_biases, far_biases)
    enc_scale, enc_shift = enc_gains.astype(F32)[None], enc_biases.astype(F32)[None]
    w_sqkv = joined(dec_in, far_attn, half_id, 0, s1)
    w_cq = joined(dec_in, far_attn, half_id, s1, s2)
    w_ckv = joined(dec_in, far_attn, half_id, s2, s3)
    w_so = joined(dec_outs, far_outs, half_id, 0, DD // 2)
    w_co = joined(dec_outs, far_outs, half_id, DD // 2, DD)
    w_up = joined(dec_in[:, s3:], far_up, half_id, 0, FD // 2)
    w_down = joined(dec_down, far_down, half_id, 0, DD // 2)

    def seg(view, half):
        return lax.dynamic_slice_in_dim(place, (view * 2 + half) * rows, rows, 1)

    cos_own, sin_own = tables(seg(view_id, core))
    cos_far, sin_far = tables(seg(view_id, 1 - core))
    cos_ot, sin_ot = tables(seg(1 - view_id, core))
    cos_of, sin_of = tables(seg(1 - view_id, 1 - core))
    cos_all, back_all = jnp.concatenate([cos_own, cos_far]), -jnp.concatenate([sin_own, sin_far])
    cos_oth, back_oth = jnp.concatenate([cos_ot, cos_of]), -jnp.concatenate([sin_ot, sin_of])
    back_own = -sin_own

    start = 4 * DE + FE
    g1, g2 = enc_scale[:, :DE], enc_scale[:, DE:]
    sh1 = enc_shift[:, start + DE : start + 2 * DE]
    sh2 = enc_shift[:, start + 2 * DE : start + 3 * DE]
    e_q, e_kv, e_n1t = lnproj(
        tokens, g1, sh1, enc_qkv, enc_shift[:, : 3 * DE], cos_own, sin_own, 2, 4, 6, "enc_qkv"
    )
    e_kvf = swap(e_kv, "pair", 1)
    e_p, e_o, e_ot = attend(e_q, e_kv, e_kvf, "enc_attend")
    e_x1, e_n2t, e_at, e_slope, z, e_xt = ffn_forward(
        e_o, tokens, enc_out, enc_shift[:, 3 * DE : 4 * DE], g2, sh2, enc_up,
        enc_shift[:, 4 * DE : start], enc_down, enc_shift[:, start : start + DE],
        (proj, enc_shift[:, start + 3 * DE :]), 512, "enc_ffn",
    )
    other_z = swap(z, "view", 2)

    ga, gb, gc, gd = [dec_scale[:, i * DD : (i + 1) * DD] for i in range(4)]
    sa, sb, sc, sd = [dec_shift[:, i * DD : (i + 1) * DD] for i in range(4)]
    s_q, s_kv, s_nt = lnproj(
        z, ga, sa, w_sqkv, dec_shift[:, 4 * DD : 7 * DD], cos_own, sin_own, 2, 4, 6, "dec_qkv"
    )
    s_kvf = swap(s_kv, "pair", 1)
    c_kv, c_nt = lnproj(
        other_z, gc, sc, w_ckv, dec_shift[:, 9 * DD : 11 * DD], cos_ot, sin_ot, 0, 2, 4, "dec_ckv"
    )
    c_kvf = swap(c_kv, "pair", 1)
    s_p, s_o, s_ot = attend(s_q, s_kv, s_kvf, "self_attend")
    y1, c_q, b_nt = mid_forward(
        s_o, z, w_so, dec_shift[:, 7 * DD : 8 * DD], gb, sb, w_cq,
        dec_shift[:, 8 * DD : 9 * DD], cos_own, sin_own, "dec_mid",
    )
    c_p, c_o, c_ot = attend(c_q, c_kv, c_kvf, "cross_attend")
    y2, d_nt, d_at, d_slope, mixed = ffn_forward(
        c_o, y1, w_co, dec_shift[:, 11 * DD : 12 * DD], gd, sd, w_up,
        dec_shift[:, 12 * DD : 12 * DD + FD], w_down, dec_shift[:, 12 * DD + FD :],
        None, 512, "dec_ffn",
    )
    mixed = trade(mixed)

    mask = masks.astype(F32)[:, None]
    d_gd, d_gu, d_gco, grad_y2, d_doc, vb_down, vb_up, vg_d, vs_d, vb_co = ffn_backward(
        (out_grad, mask), w_down, d_slope, w_up, y2, gd, w_co, 512, "dec_ffn_back"
    )
    g_cq, c_own, c_far = attend_back(
        c_q, c_kv, c_kvf, c_p, c_o, d_doc, cos_own, back_own, cos_oth, back_oth, "cross_back"
    )
    c_back = swap(c_far, "pair", 1)
    grad_y1, d_gso, d_dos, vb_cq, vg_b, vs_b, vb_so = mid_backward(
        g_cq, w_cq, y1, gb, grad_y2, w_so, "mid_back"
    )
    g_ckv, vb_ckv, grad_other, vg_c, vs_c = proj_backward(
        None, c_own, c_back, w_ckv, other_z, gc, None, "ckv_back"
    )
    returned = swap(grad_other, "view", 2)
    g_sq, s_own, s_far = attend_back(
        s_q, s_kv, s_kvf, s_p, s_o, d_dos, cos_own, back_own, cos_all, back_all, "self_back"
    )
    s_back = swap(s_far, "pair", 1)
    g_sqkv, vb_sqkv, grad_own, vg_a, vs_a = proj_backward(
        g_sq, s_own, s_back, w_sqkv, z, ga, grad_y1, "qkv_back"
    )

    (
        e_gd, e_gu, e_go, grad_x1, e_do, ub_down, ub_up, ug_2, us_2, ub_out, e_gp, ub_proj,
    ) = ffn_backward(
        (grad_own, returned, proj), enc_down, e_slope, enc_up, e_x1, g2, enc_out, 512, "enc_ffn_back"
    )
    g_eq, e_own, e_far = attend_back(
        e_q, e_kv, e_kvf, e_p, e_o, e_do, cos_own, back_own, cos_all, back_all, "enc_back"
    )
    e_back = swap(e_far, "pair", 1)
    g_eqkv, ub_qkv, tokens_grad, ug_1, us_1 = proj_backward(
        g_eq, e_own, e_back, enc_qkv, tokens, g1, grad_x1, "enc_qkv_back"
    )
    tokens_grad = trade(tokens_grad.astype(BF)).astype(F32)

    if n_pair == 8 and n_view == 4:
        def order(high, low):
            blocks = []
            for dc in range(2):
                for a in range(2):
                    for b in range(2):
                        blocks.append(pair_id ^ (dc + a * high + b * low))
            return blocks

        enc_z = [quarter, quarter ^ 2, quarter ^ 1, quarter ^ 3]
        dec_z = [half_id, 1 - half_id]
        pack = lambda ids: jnp.stack(ids).astype(jnp.int32)
        dec_x, dec_y = pack(order(2, 4) + dec_z), pack(order(4, 2) + dec_z)
        enc_x, enc_y = pack(order(2, 4) + enc_z), pack(order(4, 2) + enc_z)

        t_down = reduce_stream(
            [weight_blocks(dec_x, d_at, d_gd, 2, 384, 0, 1, 384, "dw_dec_down")], 2, 4
        )
        t_up = reduce_stream(
            [weight_blocks(dec_y, d_nt, d_gu, 2, 1536, 0, 2, 768, "dw_dec_up")], 4, 2
        )
        t_cross = reduce_stream(
            [
                weight_blocks(dec_x, c_ot, d_gco, 2, 384, 0, 1, 384, "dw_co"),
                weight_blocks(dec_x, b_nt, g_cq, 2, 384, 0, 1, 384, "dw_cq"),
                weight_blocks(dec_x, c_nt, g_ckv, 2, 768, 0, 1, 768, "dw_ckv"),
            ],
            2,
            4,
        )
        t_self = reduce_stream(
            [
                weight_blocks(dec_y, s_ot, d_gso, 2, 384, 0, 1, 384, "dw_so"),
                weight_blocks(dec_y, s_nt, g_sqkv, 2, 1152, 0, 1, 1152, "dw_sqkv"),
            ],
            4,
            2,
        )
        e_gp_wide = jnp.pad(e_gp.reshape(rows, 4, DD // 4), ((0, 0), (0, 0), (0, 64))).reshape(rows, 1024)
        t_enc_down = reduce_stream(
            [weight_blocks(enc_x, e_at, e_gd, 4, 256, 0, 1, 256, "dw_enc_down")], 2, 4
        )
        t_enc_up = reduce_stream(
            [
                weight_blocks(enc_y, e_xt, e_gp_wide, 4, 256, 0, 1, 256, "dw_proj"),
                weight_blocks(enc_y, e_n2t, e_gu, 4, 1024, 0, 2, 512, "dw_enc_up"),
            ],
            4,
            2,
        )
        t_enc_one = reduce_stream(
            [weight_blocks(enc_x, e_n1t, g_eqkv, 4, 768, 0, 2, 256, "dw_qkv_one")], 2, 4
        )
        t_enc_two = reduce_stream(
            [
                weight_blocks(enc_y, e_ot, e_go, 4, 256, 0, 1, 256, "dw_out"),
                weight_blocks(enc_y, e_n1t, g_eqkv, 4, 768, 2, 1, 256, "dw_qkv_two"),
            ],
            4,
            2,
        )
        co, cq, ckv = t_cross[:3], t_cross[3:6], t_cross[6:]
        so, sqkv = t_self[:3], t_self[3:]
        dec_in_grad = spread(jnp.concatenate([sqkv, cq, ckv, t_up], axis=0))
        dec_outs_grad = spread(jnp.concatenate([so, co], axis=0))
        dec_down_grad = spread(t_down)
        enc_down_grad = spread(t_enc_down)
        proj_grad = spread(t_enc_up[:2])[:, : DD // 4]
        enc_up_grad = spread(t_enc_up[2:])
        enc_out_grad = spread(t_enc_two[:2])
        enc_qkv_grad = spread(jnp.concatenate([t_enc_one, t_enc_two[2:]], axis=0))
    else:
        def scatter(value, axis, dim):
            return lax.psum_scatter(value.astype(BF), axis, scatter_dimension=dim, tiled=True)

        def enc_sum(at, g):
            return scatter(scatter(mm(at, g), "pair", 0), "view", 1).astype(F32)

        def halves(value, which):
            width = value.shape[1] // 2
            return lax.dynamic_slice_in_dim(value, which * width, width, 1)

        def dec_sum(blocks):
            mine = jnp.concatenate([halves(b, half_id) for b in blocks], axis=1)
            other = jnp.concatenate([halves(b, 1 - half_id) for b in blocks], axis=1)
            both = mine + swap(other.astype(BF), "view", 1).astype(F32)
            return scatter(both, "pair", 0).astype(F32)

        dec_in_grad = dec_sum([mm(s_nt, g_sqkv), mm(b_nt, g_cq), mm(c_nt, g_ckv), mm(d_nt, d_gu)])
        dec_outs_grad = dec_sum([mm(s_ot, d_gso), mm(c_ot, d_gco)])
        dec_down_grad = dec_sum([mm(d_at, d_gd)])
        enc_qkv_grad, enc_out_grad = enc_sum(e_n1t, g_eqkv), enc_sum(e_ot, e_go)
        enc_up_grad, enc_down_grad = enc_sum(e_n2t, e_gu), enc_sum(e_at, e_gd)
        proj_grad = enc_sum(e_xt, e_gp)

    enc_vec = jnp.concatenate(
        [ug_1, ug_2, ub_qkv, ub_out, ub_up, ub_down, us_1, us_2, ub_proj], axis=1
    )[0]
    dec_vec = jnp.concatenate(
        [
            vg_a, vg_b, vg_c, vg_d, vs_a, vs_b, vs_c, vs_d,
            vb_sqkv, vb_so, vb_cq, vb_ckv, vb_co, vb_up, vb_down,
        ],
        axis=1,
    )[0]
    empty = jnp.zeros_like(dec_vec)
    enc_vec, dec_one, dec_two = lax.psum(
        (
            enc_vec,
            jnp.where(view_id == 0, dec_vec, empty),
            jnp.where(view_id == 0, empty, dec_vec),
        ),
        ("pair", "view"),
    )
    dec_vec = jnp.where(view_id == 0, dec_one, dec_two)
    gain_all, bias_all = dec_vec[: 4 * DD], dec_vec[4 * DD :]
    gain_part, bias_part = gain_all.shape[0] // 2, bias_all.shape[0] // 2
    dec_gains_grad = lax.dynamic_slice_in_dim(gain_all, half_id * gain_part, gain_part, 0)
    dec_biases_grad = lax.dynamic_slice_in_dim(bias_all, half_id * bias_part, bias_part, 0)
    return (
        mixed[None],
        tokens_grad[None],
        enc_qkv_grad,
        enc_out_grad,
        enc_up_grad,
        enc_down_grad,
        enc_vec[: 2 * DE],
        enc_vec[2 * DE :],
        proj_grad,
        dec_in_grad,
        dec_outs_grad,
        dec_down_grad,
        dec_gains_grad,
        dec_biases_grad,
    )


def solution(mesh):
    both = P("pair", "view")
    return jax.shard_map(
        local,
        mesh=mesh,
        in_specs=(
            P("pair", "view", None),
            P("pair", "view", None),
            both,
            P(None, "pair", None),
            P(),
            P(),
            P(),
            P(),
            P(),
            P(),
            P(),
            P(None, "view"),
            P(None, "view"),
            P(None, "view"),
            P("view"),
            P("view"),
        ),
        out_specs=(
            P("pair", "view", None),
            P("pair", "view", None),
            both,
            both,
            both,
            both,
            P(),
            P(),
            both,
            both,
            both,
            both,
            P("view"),
            P("view"),
        ),
        check_vma=False,
    )
```

```python
from functools import partial

import jax
import jax.numpy as jnp
from jax import lax
from jax.experimental import pallas as pl
from jax.experimental.pallas import tpu as pltpu
from jax.sharding import PartitionSpec as P

DE = 1024
HE = 16
FE = 4096
DD = 768
HD = 12
FD = 3072

norm_eps = 1e-06
BF = jnp.bfloat16
F32 = jnp.float32
VMEM = 58 * 1024 * 1024

NN = (((1,), (0,)), ((), ()))
NT = (((1,), (1,)), ((), ()))
TN = (((0,), (0,)), ((), ()))


def mm(a, b, dims=NN):
    return lax.dot_general(a, b, dims, preferred_element_type=F32)


def full(shape):
    zeros = (0,) * len(shape)
    return pl.BlockSpec(shape, lambda *_: zeros)


def sds(shape, dtype):
    return jax.ShapeDtypeStruct(shape, dtype)


def call(body, name, half, grid, in_specs, out_specs, out_shape, args, scratch=(), flops=0, nbytes=0):
    return pl.pallas_call(
        body,
        grid_spec=pltpu.PrefetchScalarGridSpec(
            num_scalar_prefetch=1,
            grid=grid,
            in_specs=in_specs,
            out_specs=out_specs,
            scratch_shapes=list(scratch),
        ),
        out_shape=out_shape,
        name=name,
        compiler_params=pltpu.CompilerParams(vmem_limit_bytes=VMEM),
        cost_estimate=cost(name),
    )(half, *args)


SCALE = 0.45e9

TIMES = {
    "enc_qkv": 8, "enc_attend": 19, "enc_ffn": 20, "dec_qkv": 8, "self_attend": 15, "dec_mid": 5,
    "dec_ckv": 7, "cross_attend": 15, "dec_ffn": 15, "dec_ffn_back": 13, "cross_back": 15,
    "mid_back": 5, "ckv_back": 7, "self_back": 15, "qkv_back": 10, "proj_back": 4,
    "enc_ffn_back": 18, "enc_back": 18, "enc_qkv_back": 11, "dw_dec_down": 6, "dw_dec_up": 6,
    "dw_co": 4, "dw_cq": 4, "dw_ckv": 4, "dw_so": 4, "dw_sqkv": 6, "dw_enc_down": 8, "dw_proj": 5,
    "dw_enc_up": 8, "dw_out": 5, "dw_enc_qkv": 7,
}


def cost(name):
    flops = int(TIMES[name] * SCALE)
    return pl.CostEstimate(flops=flops, bytes_accessed=0, transcendentals=0)


class Whole:
    def __init__(self, array):
        self.arrays, self.columns = [array], array.shape[1]
        self.rows = array.shape[0]

    def blocks(self, bn):
        return [pl.BlockSpec((self.rows, bn), lambda j, h: (0, j))]

    def whole(self, bn=None):
        if bn is None:
            return [full(self.arrays[0].shape)]
        return [pl.BlockSpec((bn, self.columns), lambda j, h: (j, 0))]

    def read(self, refs, h, j, bn):
        return refs[0][...]

    def read_whole(self, refs, h):
        return refs[0][...]


class Halves:
    def __init__(self, own, far, width):
        self.arrays = [own[0], far[0]]
        self.starts, self.width = (own[1], far[1]), width
        self.rows, self.columns = own[0].shape[0], 2 * width

    def blocks(self, bn):
        per = self.width // bn
        specs = []
        for which, start in enumerate(self.starts):

            def index(j, h, which=which, start=start):
                half = h[0] ^ which
                hold = jnp.where(half == 0, per - 1, 0)
                return 0, start // bn + jnp.where(j // per == half, j % per, hold)

            specs.append(pl.BlockSpec((self.rows, bn), index))
        return specs

    def whole(self, bn=None):
        specs = []
        for start in self.starts:
            col = start // self.width
            if bn is None:
                specs.append(pl.BlockSpec((self.rows, self.width), lambda j, h, col=col: (0, col)))
            else:
                specs.append(pl.BlockSpec((bn, self.width), lambda j, h, col=col: (j, col)))
        return specs

    def read(self, refs, h, j, bn):
        return jnp.where(j // (self.width // bn) == h[0], refs[0][...], refs[1][...])

    def read_whole(self, refs, h):
        own, far = refs[0][...], refs[1][...]
        first = h[0] == 0
        return jnp.concatenate([jnp.where(first, own, far), jnp.where(first, far, own)], axis=1)


def norm_parts(x):
    centred = x - jnp.mean(x, axis=-1, keepdims=True)
    rstd = lax.rsqrt(jnp.mean(centred * centred, axis=-1, keepdims=True) + norm_eps)
    return centred * rstd, rstd


def norm_back(dy, x, gain):
    xhat, rstd = norm_parts(x)
    dgain = jnp.sum(dy * xhat, axis=0, keepdims=True)
    dshift = jnp.sum(dy, axis=0, keepdims=True)
    dxh = dy * gain
    mean_one = jnp.mean(dxh, axis=-1, keepdims=True)
    mean_two = jnp.mean(dxh * xhat, axis=-1, keepdims=True)
    return rstd * (dxh - mean_one - xhat * mean_two), dgain, dshift


def turn(u, cos, sin):
    lane = lax.broadcasted_iota(jnp.int32, u.shape, 1)
    other = jnp.where(lane % 32 < 16, pltpu.roll(u, 112, 1), pltpu.roll(u, 16, 1))
    return u * cos + other * sin


def turn_cols(y, cos, sin):
    return jnp.concatenate(
        [turn(y[:, i : i + 128], cos, sin) for i in range(0, y.shape[1], 128)], axis=1
    )


def gelu_parts(u):
    z = jnp.abs(u) * 0.7071067811865476
    t = 1.0 / (1.0 + 0.3275911 * z)
    e = jnp.exp(-0.5 * u * u)
    poly = t * (
        0.254829592
        + t * (-0.284496736 + t * (1.421413741 + t * (-1.453152027 + t * 1.061405429)))
    )
    tail = 0.5 * poly * e
    phi = jnp.where(u >= 0, 1.0 - tail, tail)
    return u * phi, phi + u * e * 0.3989422804014327


def col_sum(g):
    return jnp.sum(g.astype(F32), axis=0, keepdims=True)


def deal(h, tall, mine, theirs, at=None):
    rb = mine.shape[1]
    for s in range(tall.shape[0] // (2 * rb)):
        even, odd = tall[2 * s * rb : (2 * s + 1) * rb], tall[(2 * s + 1) * rb : (2 * s + 2) * rb]
        first = h[1] == 0
        mine[s] = jnp.where(first, even, odd)
        theirs[s] = jnp.where(first, odd, even)


def dealt(width, rows):
    return [sds((4, width // 8, rows), BF)] * 2


def lnproj(half, x, gain, shift, w, b, cos, sin, n_q, n_turn, n_all, name):
    rows, width = x.shape
    bn = w.columns // n_all
    n_w = len(w.arrays)
    has_q = n_q > 0

    def body(h, x_ref, g_ref, s_ref, b_ref, c_ref, sn_ref, *rest):
        w_refs, rest = rest[:n_w], rest[n_w:]
        if has_q:
            q_ref, kv_ref, mine, theirs, nrm = rest
        else:
            kv_ref, mine, theirs, nrm = rest
        j = pl.program_id(0)

        @pl.when(j == 0)
        def _():
            xhat, _ = norm_parts(x_ref[...].astype(F32))
            low = (xhat * g_ref[...] + s_ref[...]).astype(BF)
            nrm[...] = low
            deal(h, low.T, mine, theirs)

        y = mm(nrm[...], w.read(w_refs, h, j, bn)) + b_ref[...]

        @pl.when(j < n_turn)
        def _():
            out = turn_cols(y, c_ref[...], sn_ref[...]).astype(BF)
            if has_q:

                @pl.when(j < n_q)
                def _():
                    q_ref[...] = out

                @pl.when(j >= n_q)
                def _():
                    kv_ref[...] = out

            else:
                kv_ref[...] = out

        @pl.when(j >= n_turn)
        def _():
            kv_ref[...] = y.astype(BF)

    outs = [
        sds((rows, bn * (n_all - n_q)), BF),
        *dealt(width, rows),
    ]
    specs = [
        pl.BlockSpec((rows, bn), lambda j, h: (0, jnp.maximum(j - n_q, 0))),
        full((4, width // 8, rows)),
        full((4, width // 8, rows)),
    ]
    if has_q:
        outs.insert(0, sds((rows, bn * n_q), BF))
        specs.insert(0, pl.BlockSpec((rows, bn), lambda j, h: (0, jnp.minimum(j, n_q - 1))))
    return call(
        body,
        name,
        half,
        (n_all,),
        [
            full((rows, width)),
            full((1, width)),
            full((1, width)),
            pl.BlockSpec((1, bn), lambda j, h: (0, j)),
            full((rows, 128)),
            full((rows, 128)),
        ]
        + w.blocks(bn),
        specs,
        outs,
        (x, gain, shift, b, cos, sin, *w.arrays),
        [pltpu.VMEM((rows, width), BF)],
        2 * rows * width * w.columns,
        2 * width * w.columns + 4 * rows * w.columns,
    )


def two_heads(block):
    first = lax.broadcasted_iota(jnp.int32, block.shape, 1) < 64
    zero = jnp.zeros_like(block)
    return jnp.concatenate(
        [jnp.where(first, block, zero), jnp.where(first, zero, block)], axis=0
    )


def pick_heads(tall, rows):
    return jnp.concatenate([tall[:64, :rows], tall[64:, rows:]], axis=0)


def attend(half, q, kv, kvf, name):
    rows, width = q.shape
    pairs = width // 128
    keys = 2 * rows

    def body(h, q_ref, ko_ref, vo_ref, kf_ref, vf_ref, p_ref, o_ref, mine, theirs, tall):
        q2 = two_heads(q_ref[...] * jnp.asarray(0.125, BF))
        k = jnp.concatenate([ko_ref[...], kf_ref[...]], axis=0)
        v = jnp.concatenate([vo_ref[...], vf_ref[...]], axis=0)
        vt = v.T
        pieces = []
        for c in range(0, 2 * rows, 256):
            s = mm(k, q2[c : c + 256], NT)
            e = jnp.exp(s - jnp.max(s, axis=0, keepdims=True))
            p = (e * (1.0 / jnp.sum(e, axis=0, keepdims=True))).astype(BF)
            p_ref[0, :, c : c + 256] = p
            pieces.append(mm(vt, p))
        t = pick_heads(jnp.concatenate(pieces, axis=1), rows)
        j = pl.program_id(0)
        tall[pl.ds(pl.multiple_of(j * 128, 128), 128), :] = t.astype(BF)
        o_ref[...] = t.T.astype(BF)

        @pl.when(j == pairs - 1)
        def _():
            deal(h, tall[...], mine, theirs)

    col = lambda j, h: (0, j)
    val = lambda j, h: (0, pairs + j)
    return call(
        body,
        name,
        half,
        (pairs,),
        [
            pl.BlockSpec((rows, 128), col),
            pl.BlockSpec((rows, 128), col),
            pl.BlockSpec((rows, 128), val),
            pl.BlockSpec((rows, 128), col),
            pl.BlockSpec((rows, 128), val),
        ],
        [
            pl.BlockSpec((1, keys, 2 * rows), lambda j, h: (j, 0, 0)),
            pl.BlockSpec((rows, 128), col),
            full((4, width // 8, rows)),
            full((4, width // 8, rows)),
        ],
        [
            sds((pairs, keys, 2 * rows), BF),
            sds((rows, width), BF),
            *dealt(width, rows),
        ],
        (q, kv, kv, kvf, kvf),
        [pltpu.VMEM((width, rows), BF)],
        4 * rows * keys * width,
        pairs * keys * rows * 4,
    )


def attend_back(half, q, kv, kvf, p, o, do, cos, sin, cos_all, sin_all, name):
    rows, width = q.shape
    pairs = width // 128
    keys = 2 * rows

    def body(
        h, q_ref, ko_ref, vo_ref, kf_ref, vf_ref, p_ref, o_ref, do_ref, c_ref, s_ref, ca_ref, sa_ref,
        own_ref, ship_ref,
    ):
        q2 = two_heads(q_ref[...] * jnp.asarray(0.125, BF))
        k = jnp.concatenate([ko_ref[...], kf_ref[...]], axis=0)
        v = jnp.concatenate([vo_ref[...], vf_ref[...]], axis=0)
        kt = k.T
        do_low = do_ref[...]
        do2 = two_heads(do_low)
        prod = two_heads(do_low.astype(F32) * o_ref[...].astype(F32))
        inner = lax.dot_general(
            jnp.ones((8, 128), F32), prod, NT, precision=lax.Precision.HIGHEST,
            preferred_element_type=F32,
        )[:1]
        dk = jnp.zeros((keys, 128), F32)
        dv = jnp.zeros((keys, 128), F32)
        pieces = []
        for c in range(0, 2 * rows, 256):
            dp = mm(v, do2[c : c + 256], NT)
            pc = p_ref[0, :, c : c + 256]
            ds = (pc.astype(F32) * (dp - inner[:, c : c + 256])).astype(BF)
            dk += mm(ds, q2[c : c + 256])
            dv += mm(pc, do2[c : c + 256])
            pieces.append(mm(kt, ds))
        dq = pick_heads(jnp.concatenate(pieces, axis=1), rows).T * 0.125
        ship_ref[2] = turn(dq, c_ref[...], s_ref[...]).astype(BF)
        dk = turn(dk, ca_ref[...], sa_ref[...])
        own_ref[0] = dk[:rows]
        own_ref[1] = dv[:rows]
        ship_ref[0] = dk[rows:].astype(BF)
        ship_ref[1] = dv[rows:].astype(BF)

    col = lambda j, h: (0, j)
    val = lambda j, h: (0, pairs + j)
    return call(
        body,
        name,
        half,
        (pairs,),
        [
            pl.BlockSpec((rows, 128), col),
            pl.BlockSpec((rows, 128), col),
            pl.BlockSpec((rows, 128), val),
            pl.BlockSpec((rows, 128), col),
            pl.BlockSpec((rows, 128), val),
            pl.BlockSpec((1, keys, 2 * rows), lambda j, h: (j, 0, 0)),
            pl.BlockSpec((rows, 128), col),
            pl.BlockSpec((rows, 128), col),
            full((rows, 128)),
            full((rows, 128)),
            full((keys, 128)),
            full((keys, 128)),
        ],
        [
            pl.BlockSpec((2, rows, 128), lambda j, h: (0, 0, j)),
            pl.BlockSpec((3, rows, 128), lambda j, h: (0, 0, j)),
        ],
        [sds((2, rows, width), F32), sds((3, rows, width), BF)],
        (q, kv, kv, kvf, kvf, p, o, do, cos, sin, cos_all, sin_all),
        (),
        8 * rows * keys * width,
        pairs * keys * rows * 4,
    )


def ffn_forward(half, o, resid, wo, bo, gain, shift, w_up, b_up, w_down, b_down, head, bn, name):
    rows, width = o.shape
    hidden = w_up.columns
    steps = hidden // bn
    n_w = len(wo.arrays)

    def body(h, o_ref, r_ref, bo_ref, g_ref, s_ref, bu_ref, bd_ref, *rest):
        wo_refs, up_refs, dn_refs, rest = rest[:n_w], rest[n_w : 2 * n_w], rest[2 * n_w : 3 * n_w], rest[3 * n_w :]
        if head:
            pj_ref, bp_ref, x1_ref, n_mine, n_theirs, a_mine, a_theirs, gp_ref, z_ref, *rest = rest
            x_mine, x_theirs, nrm, acc = rest
        else:
            x1_ref, n_mine, n_theirs, a_mine, a_theirs, gp_ref, z_ref, nrm, acc = rest
        j = pl.program_id(0)

        @pl.when(j == 0)
        def _():
            x1 = r_ref[...].astype(F32) + mm(o_ref[...], wo.read_whole(wo_refs, h)) + bo_ref[...]
            x1_ref[...] = x1
            xhat, _ = norm_parts(x1)
            low = (xhat * g_ref[...] + s_ref[...]).astype(BF)
            nrm[...] = low
            deal(h, low.T, n_mine, n_theirs)
            acc[...] = x1 + bd_ref[...]

        u = mm(nrm[...], w_up.read(up_refs, h, j, bn)) + bu_ref[...]
        act, slope = gelu_parts(u)
        act = act.astype(BF)
        gp_ref[...] = slope.astype(BF)
        deal(h, act.T, a_mine, a_theirs)
        acc[...] += mm(act, w_down.read_whole(dn_refs, h))

        @pl.when(j == steps - 1)
        def _():
            low = acc[...].astype(BF)
            if head:
                deal(h, low.T, x_mine, x_theirs)
                z_ref[...] = (mm(low, pj_ref[...]) + bp_ref[...]).astype(BF)
            else:
                z_ref[...] = low

    vec, whole = full((1, width)), full((rows, width))
    in_specs = (
        [whole, whole, vec, vec, vec, pl.BlockSpec((1, bn), lambda j, h: (0, j)), vec]
        + wo.whole()
        + w_up.blocks(bn)
        + w_down.whole(bn)
    )
    out_specs = [
        whole,
        full((4, width // 8, rows)),
        full((4, width // 8, rows)),
        pl.BlockSpec((bn * 4 // hidden, hidden // 8, rows), lambda j, h: (j, 0, 0)),
        pl.BlockSpec((bn * 4 // hidden, hidden // 8, rows), lambda j, h: (j, 0, 0)),
        pl.BlockSpec((rows, bn), lambda j, h: (0, j)),
    ]
    outs = [
        sds((rows, width), F32),
        *dealt(width, rows),
        *dealt(hidden, rows),
        sds((rows, hidden), BF),
    ]
    args = [o, resid, bo, gain, shift, b_up, b_down, *wo.arrays, *w_up.arrays, *w_down.arrays]
    if head:
        wide = head[0].shape[1]
        in_specs += [full((width, wide)), full((1, wide))]
        args += list(head)
        out_specs += [full((rows, wide)), full((4, width // 8, rows)), full((4, width // 8, rows))]
        outs += [sds((rows, wide), BF), *dealt(width, rows)]
    else:
        out_specs += [whole]
        outs += [sds((rows, width), BF)]
    return call(
        body,
        name,
        half,
        (steps,),
        in_specs,
        out_specs,
        outs,
        args,
        [pltpu.VMEM((rows, width), BF), pltpu.VMEM((rows, width), F32)],
        4 * rows * width * hidden + 2 * rows * width * width,
        4 * width * hidden + 4 * rows * hidden,
    )


def head_backward(half, grad, returned, proj, name):
    rows, wide = grad.shape
    width = proj.shape[0]

    part = wide // 4
    slot = -(-part // 128) * 128

    def body(h, g_ref, r_ref, w_ref, low_ref, b_ref, gx_ref, gd_ref):
        low = (g_ref[...] + r_ref[...].astype(F32)).astype(BF)
        pad = jnp.zeros((rows, slot - part), BF)
        for t in range(4):
            piece = low[:, t * part : (t + 1) * part]
            low_ref[:, t * slot : (t + 1) * slot] = jnp.concatenate([piece, pad], axis=1)
        b_ref[...] = col_sum(low)
        gx = mm(low, w_ref[...], NT)
        gx_ref[...] = gx
        gd_ref[...] = gx.astype(BF)

    inside, outside = full((rows, wide)), full((rows, width))
    return call(
        body,
        name,
        half,
        (1,),
        [inside, inside, full((width, wide))],
        [full((rows, 4 * slot)), full((1, wide)), outside, outside],
        [sds((rows, 4 * slot), BF), sds((1, wide), F32), sds((rows, width), F32), sds((rows, width), BF)],
        (grad, returned, proj),
        (),
        2 * rows * wide * width,
        2 * wide * width,
    )


def ffn_backward(half, gd, base, w_down, slope, w_up, x, gain, wo, bn, name):
    rows, width = x.shape
    hidden = w_up.columns
    steps = hidden // bn
    n_w = len(wo.arrays)
    has_base = base is not None

    def body(h, gd_ref, gp_ref, x_ref, g_ref, *refs):
        wo_refs, up_refs, dn_refs, refs = refs[:n_w], refs[n_w : 2 * n_w], refs[2 * n_w : 3 * n_w], refs[3 * n_w :]
        if has_base:
            base_ref, *refs = refs
        gu_ref, go_ref, gx_ref, do_ref, bd_ref, bu_ref, dg_ref, ds_ref, bo_ref, acc = refs
        j = pl.program_id(0)

        @pl.when(j == 0)
        def _():
            bd_ref[...] = col_sum(gd_ref[...])
            acc[...] = jnp.zeros_like(acc)

        da = mm(gd_ref[...], w_down.read_whole(dn_refs, h), NT)
        gu = (da * gp_ref[...].astype(F32)).astype(BF)
        gu_ref[...] = gu
        bu_ref[...] = col_sum(gu)
        acc[...] += mm(gu, w_up.read(up_refs, h, j, bn), NT)

        @pl.when(j == steps - 1)
        def _():
            dx, dg, ds = norm_back(acc[...], x_ref[...], g_ref[...])
            dg_ref[...] = dg
            ds_ref[...] = ds
            total = (base_ref[...] if has_base else gd_ref[...].astype(F32)) + dx
            gx_ref[...] = total
            go = total.astype(BF)
            go_ref[...] = go
            bo_ref[...] = col_sum(go)
            do_ref[...] = mm(go, wo.read_whole(wo_refs, h), NT).astype(BF)

    vec, whole = full((1, width)), full((rows, width))
    row = sds((1, width), F32)
    return call(
        body,
        name,
        half,
        (steps,),
        [whole, pl.BlockSpec((rows, bn), lambda j, h: (0, j)), whole, vec]
        + wo.whole()
        + w_up.blocks(bn)
        + w_down.whole(bn)
        + ([whole] if has_base else []),
        [
            pl.BlockSpec((rows, bn), lambda j, h: (0, j)),
            whole,
            whole,
            whole,
            vec,
            pl.BlockSpec((1, bn), lambda j, h: (0, j)),
            vec,
            vec,
            vec,
        ],
        [
            sds((rows, hidden), BF),
            sds((rows, width), BF),
            sds((rows, width), F32),
            sds((rows, width), BF),
            row,
            sds((1, hidden), F32),
            row,
            row,
            row,
        ],
        [gd, slope, x, gain, *wo.arrays, *w_up.arrays, *w_down.arrays] + ([base] if has_base else []),
        [pltpu.VMEM((rows, width), F32)],
        4 * rows * width * hidden + 2 * rows * width * width,
        4 * width * hidden + 4 * rows * hidden,
    )


def mid_forward(half, o, resid, wo, bo, gain, shift, w, b, cos, sin, name):
    rows, width = o.shape

    def body(
        h, o_ref, r_ref, bo_ref, g_ref, s_ref, b_ref, c_ref, sn_ref, wo_own, wo_far, w_own, w_far,
        y_ref, q_ref, mine, theirs,
    ):
        y = r_ref[...].astype(F32) + mm(o_ref[...], wo.read_whole((wo_own, wo_far), h)) + bo_ref[...]
        y_ref[...] = y
        xhat, _ = norm_parts(y)
        low = (xhat * g_ref[...] + s_ref[...]).astype(BF)
        deal(h, low.T, mine, theirs)
        q = mm(low, w.read_whole((w_own, w_far), h)) + b_ref[...]
        q_ref[...] = turn_cols(q, c_ref[...], sn_ref[...]).astype(BF)

    whole, vec, table = full((rows, width)), full((1, width)), full((rows, 128))
    return call(
        body,
        name,
        half,
        (1,),
        [whole, whole, vec, vec, vec, vec, table, table] + wo.whole() + w.whole(),
        [whole, whole, full((4, width // 8, rows)), full((4, width // 8, rows))],
        [sds((rows, width), F32), sds((rows, width), BF), *dealt(width, rows)],
        (o, resid, bo, gain, shift, b, cos, sin, *wo.arrays, *w.arrays),
        (),
        4 * rows * width * width,
        4 * width * width,
    )


def mid_backward(half, gq, w, x, gain, above, wo, name):
    rows, width = x.shape

    def body(
        h, gq_ref, x_ref, g_ref, a_ref, w_own, w_far, wo_own, wo_far,
        gx_ref, go_ref, do_ref, bq_ref, dg_ref, ds_ref, bo_ref,
    ):
        low = gq_ref[0]
        bq_ref[...] = col_sum(low)
        dx, dg, ds = norm_back(mm(low, w.read_whole((w_own, w_far), h), NT), x_ref[...], g_ref[...])
        dg_ref[...] = dg
        ds_ref[...] = ds
        total = a_ref[...] + dx
        gx_ref[...] = total
        go = total.astype(BF)
        go_ref[...] = go
        bo_ref[...] = col_sum(go)
        do_ref[...] = mm(go, wo.read_whole((wo_own, wo_far), h), NT).astype(BF)

    whole, vec = full((rows, width)), full((1, width))
    row = sds((1, width), F32)
    return call(
        body,
        name,
        half,
        (1,),
        [pl.BlockSpec((1, rows, width), lambda j, h: (2, 0, 0)), whole, vec, whole]
        + w.whole()
        + wo.whole(),
        [whole, whole, whole, vec, vec, vec, vec],
        [sds((rows, width), F32), sds((rows, width), BF), sds((rows, width), BF), row, row, row, row],
        (gq, x, gain, above, *w.arrays, *wo.arrays),
        (),
        4 * rows * width * width,
        4 * width * width,
    )


def proj_backward(half, gq, own, back, w, x, gain, above, bn, name):
    rows, width = x.shape
    steps, per = w.columns // bn, width // bn
    has_q, has_above = gq is not None, above is not None
    n_w = len(w.arrays)
    skip = per if has_q else 0

    def body(h, *refs):
        if has_q:
            gq_ref, *refs = refs
        own_ref, back_ref, x_ref, g_ref, *refs = refs
        w_refs, refs = refs[:n_w], refs[n_w:]
        if has_above:
            a_ref, *refs = refs
        g_out, b_ref, gx_ref, dg_ref, ds_ref, acc = refs
        j = pl.program_id(0)
        low = (own_ref[0] + back_ref[0].astype(F32)).astype(BF)
        if has_q:
            low = jnp.where(j < per, gq_ref[0], low)
        g_out[...] = low
        b_ref[...] = col_sum(low)
        piece = mm(low, w.read(w_refs, h, j, bn), NT)

        @pl.when(j == 0)
        def _():
            acc[...] = piece

        @pl.when(j > 0)
        def _():
            acc[...] += piece

        @pl.when(j == steps - 1)
        def _():
            dx, dg, ds = norm_back(acc[...], x_ref[...].astype(F32), g_ref[...])
            dg_ref[...] = dg
            ds_ref[...] = ds
            gx_ref[...] = (a_ref[...] + dx if has_above else dx).astype(gx_ref.dtype)

    whole, vec = full((rows, width)), full((1, width))

    def part_index(j, h):
        i = jnp.maximum(j - skip, 0)
        return i // per, 0, i % per

    part = pl.BlockSpec((1, rows, bn), part_index)
    in_specs = [part, part, whole, vec] + w.blocks(bn)
    args = [own, back, x, gain, *w.arrays]
    if has_q:
        in_specs.insert(0, pl.BlockSpec((1, rows, bn), lambda j, h: (2, 0, jnp.minimum(j, per - 1))))
        args.insert(0, gq)
    if has_above:
        in_specs.append(whole)
        args.append(above)
    row = sds((1, width), F32)
    return call(
        body,
        name,
        half,
        (steps,),
        in_specs,
        [
            pl.BlockSpec((rows, bn), lambda j, h: (0, j)),
            pl.BlockSpec((1, bn), lambda j, h: (0, j)),
            whole,
            vec,
            vec,
        ],
        [
            sds((rows, w.columns), BF),
            sds((1, w.columns), F32),
            sds((rows, width), F32 if has_above else BF),
            row,
            row,
        ],
        args,
        [pltpu.VMEM((rows, width), F32)],
        2 * rows * width * w.columns,
        2 * width * w.columns,
    )


def weight_blocks(place, mine, far, g, g_far, nz, width, bn, name, base=None, at=0, total=None, apart=False):
    _, rb, rows = mine.shape
    per = width // bn
    units = bn // 128
    total = total or width // 128
    group = max(1, 512 // rb)

    def body(place_ref, a_ref, b_ref, g_ref, gf_ref, *rest):
        *outs, lhs = rest[1:] if base is not None else rest

        @pl.when((pl.program_id(0) == 0) & (pl.program_id(1) == 0))
        def _():
            for s in range(4):
                lhs[s * rb : (s + 1) * rb, :rows] = a_ref[place_ref[nz + s]]
                lhs[s * rb : (s + 1) * rb, rows:] = b_ref[place_ref[nz + s]]

        grad = jnp.concatenate([g_ref[...].reshape(rows, bn), gf_ref[...].reshape(rows, bn)], axis=0)
        for c in range(0, 4, group):
            n = min(4 - c, group)
            y = mm(lhs[c * rb : (c + n) * rb, :], grad).astype(BF)
            for s in range(n):
                for u in range(units):
                    piece = y[s * rb : (s + 1) * rb, u * 128 : (u + 1) * 128]
                    if apart:
                        outs[c + s][0, u] = piece
                    else:
                        outs[0][c + s, 0, u] = piece

    if g.ndim == 3:
        columns = pl.BlockSpec((1, rows, bn), lambda i, j, z: (2, 0, z[i] * per + j))
    else:
        columns = pl.BlockSpec((rows, bn), lambda i, j, z: (0, z[i] * per + j))
    skip = at // units
    if apart:
        shape = [sds((nz, total, rb, 128), BF)] * 4
        specs = [pl.BlockSpec((1, units, rb, 128), lambda i, j, z: (i, skip + j, 0, 0))] * 4
    else:
        shape = [sds((4, nz, total, rb, 128), BF)]
        specs = [pl.BlockSpec((4, 1, units, rb, 128), lambda i, j, z: (0, i, skip + j, 0, 0))]
    in_specs = [full((4, rb, rows)), full((4, rb, rows)), columns, columns]
    args, aliases = [mine, far, g, g_far], {}
    if base is not None:
        for k, array in enumerate(base):
            in_specs.append(pl.BlockSpec(memory_space=pl.ANY))
            args.append(array)
            aliases[5 + k] = k

    def shell(place_ref, a_ref, b_ref, g_ref, gf_ref, *rest):
        kept = rest[len(base) - 1 :] if base is not None else rest
        body(place_ref, a_ref, b_ref, g_ref, gf_ref, *kept)

    return pl.pallas_call(
        shell,
        grid_spec=pltpu.PrefetchScalarGridSpec(
            num_scalar_prefetch=1,
            grid=(nz, per),
            in_specs=in_specs,
            out_specs=specs,
            scratch_shapes=[pltpu.VMEM((4 * rb, 2 * rows), BF)],
        ),
        out_shape=shape,
        name=name,
        input_output_aliases=aliases,
        compiler_params=pltpu.CompilerParams(vmem_limit_bytes=VMEM),
        cost_estimate=cost(name),
    )(place, *args)


def swap(value, axis, distance):
    size = lax.axis_size(axis)
    return lax.ppermute(value, axis, [(i, i ^ distance) for i in range(size)])


def plus(a, b):
    return (a.astype(F32) + b.astype(F32)).astype(BF)


def chip_sum(blocks):
    groups = [[0, 2, 4, 6], [1, 3, 5, 7]]
    flat = blocks.reshape(-1, 128)
    out = lax.psum_scatter(flat, "pair", scatter_dimension=0, axis_index_groups=groups, tiled=True)
    return out.reshape(blocks.shape[1:])


MESH = pl.DeviceIdType.MESH
CHUNK = 256


def final_sums(mains, stacks, halves, vector, vector_enc):
    chunks = []
    for k, array in enumerate(mains):
        for row in range(0, array.shape[2], CHUNK):
            chunks.append((k, row))
    n = len(chunks)
    l_main = n * CHUNK
    l_stack = sum(array.shape[1] for array in stacks)
    l_half = sum(array.shape[1] for array in halves)
    rows = vector.shape[0]

    def body(*refs):
        m_refs, refs = refs[: len(mains)], refs[len(mains) :]
        s_refs, refs = refs[: len(stacks)], refs[len(stacks) :]
        h_refs, refs = refs[: len(halves)], refs[len(halves) :]
        (
            v_ref, main_out, stack_out, half_out, v_out,
            keep, got1, got2, got3, got4, s_keep, s_got3, s_got4, h_keep, h_got, v_got,
            in_sem, send1, recv1, send2, recv2, send3, recv3, send4, recv4,
            s_in, s_send, s_recv, h_in, h_send, h_recv, v_send, v_recv,
        ) = refs
        p, t = lax.axis_index("pair"), lax.axis_index("view")

        def across(axis, bit):
            here = p if axis == "pair" else t
            return {axis: here + bit - 2 * bit * ((here // bit) % 2)}

        core, x, y = across("pair", 1), across("pair", 2), across("pair", 4)
        z1, z2 = across("view", 1), across("view", 2)

        barrier = pltpu.get_barrier_semaphore()
        for device in (core, x, y, z1, z2):
            pl.semaphore_signal(barrier, inc=1, device_id=device, device_id_type=MESH)
        pl.semaphore_wait(barrier, 5)

        sent = []

        def send(src, dst, send_sem, recv_sem, device, late=True):
            copy = pltpu.make_async_remote_copy(
                src_ref=src, dst_ref=dst, send_sem=send_sem, recv_sem=recv_sem,
                device_id=device, device_id_type=MESH,
            )
            copy.start()
            if late:
                sent.append(copy)
            return copy

        def fetch(src, dst, sem):
            copy = pltpu.make_async_copy(src, dst, sem)
            copy.start()
            return copy

        def at(i):
            return pl.ds(i * CHUNK, CHUNK)

        one, two, three, four, loads = {}, {}, {}, {}, {}

        def start_one(i):
            k, row = chunks[i]
            src = m_refs[k]
            first, away = (x, (1, 3)) if i % 2 == 0 else (y, (2, 3))
            one[i] = [
                send(
                    src.at[slot, :, pl.ds(row, CHUNK), :], got1.at[q, :, at(i), :],
                    send1.at[i, q], recv1.at[i, q], first,
                )
                for q, slot in enumerate(away)
            ]

        def start_load(i):
            k, row = chunks[i]
            stay = (0, 2) if i % 2 == 0 else (0, 1)
            loads[i] = [
                fetch(m_refs[k].at[slot, :, pl.ds(row, CHUNK), :], keep.at[q, :, at(i), :], in_sem.at[i, q])
                for q, slot in enumerate(stay)
            ]

        def start_two(i):
            second = y if i % 2 == 0 else x
            two[i] = send(keep.at[1, :, at(i), :], got2.at[:, at(i), :], send2.at[i], recv2.at[i], second)

        def start_three(i):
            three[i] = [
                send(keep.at[0, slot, at(i), :], got3.at[q, at(i), :], send3.at[i, q], recv3.at[i, q], z1)
                for q, slot in enumerate((1, 3))
            ]

        def start_four(i):
            four[i] = send(keep.at[0, 2, at(i), :], got4.at[at(i), :], send4.at[i], recv4.at[i], z2)

        ahead = 4
        for i in range(min(ahead, n)):
            start_one(i)
        v_out[...] = v_ref[...]
        v_axes = (core, x, y, z1, z2)

        def start_vector(r):
            count = vector_enc if r == 4 else rows
            return send(
                v_out.at[pl.ds(0, count), :], v_got.at[r, pl.ds(0, count), :],
                v_send.at[r], v_recv.at[r], v_axes[r], late=False,
            )

        flying = start_vector(0)
        offset, h_moves = 0, []
        for k, ref in enumerate(h_refs):
            size = ref.shape[1]
            where = pl.ds(offset, size)
            h_moves.append(
                (
                    send(ref.at[1], h_got.at[where, :], h_send.at[k], h_recv.at[k], z1),
                    fetch(ref.at[0], h_keep.at[where, :], h_in.at[k]),
                    where,
                )
            )
            offset += size
        offset, s_moves = 0, []
        for k, ref in enumerate(s_refs):
            size = ref.shape[1]
            where = pl.ds(offset, size)
            s_moves.append(
                (
                    [
                        send(ref.at[slot], s_got3.at[q, where, :], s_send.at[k, q], s_recv.at[k, q], z1)
                        for q, slot in enumerate((1, 3))
                    ],
                    [
                        fetch(ref.at[slot], s_keep.at[q, where, :], s_in.at[k, q])
                        for q, slot in enumerate((0, 2))
                    ],
                    where,
                )
            )
            offset += size
        for i in range(n):
            start_load(i)

        s_last = []
        for i in range(n + 6):
            if i < n:
                if i + ahead < n:
                    start_one(i + ahead)
                for copy in loads[i]:
                    copy.wait()
                for copy in one[i]:
                    copy.wait_recv()
                keep[:, :, at(i), :] = keep[:, :, at(i), :] + got1[:, :, at(i), :]
                start_two(i)
            j = i - 2
            if 0 <= j < n:
                two[j].wait_recv()
                keep[0, :, at(j), :] = keep[0, :, at(j), :] + got2[:, at(j), :]
                start_three(j)
            j = i - 4
            if 0 <= j < n:
                for copy in three[j]:
                    copy.wait_recv()
                keep[0, 0, at(j), :] = keep[0, 0, at(j), :] + got3[0, at(j), :]
                keep[0, 2, at(j), :] = keep[0, 2, at(j), :] + got3[1, at(j), :]
                start_four(j)
            j = i - 6
            if 0 <= j < n:
                four[j].wait_recv()
                main_out[at(j), :] = keep[0, 0, at(j), :].astype(F32) + got4[at(j), :].astype(F32)
            if i % 2 == 1 and i // 2 < 5:
                r = i // 2
                flying.wait()
                count = vector_enc if r == 4 else rows
                v_out[pl.ds(0, count), :] = v_out[pl.ds(0, count), :] + v_got[r, pl.ds(0, count), :]
                if r < 4:
                    flying = start_vector(r + 1)
            if i == n // 2:
                for k, (moves, reads, where) in enumerate(s_moves):
                    for copy in reads:
                        copy.wait()
                    for copy in moves:
                        copy.wait_recv()
                    for q in range(2):
                        s_keep[q, where, :] = s_keep[q, where, :] + s_got3[q, where, :]
                    s_last.append(
                        send(s_keep.at[1, where, :], s_got4.at[where, :], s_send.at[k, 2], s_recv.at[k, 2], z2)
                    )
            if i == n:
                for move, read, where in h_moves:
                    read.wait()
                    move.wait_recv()
                    half_out[where, :] = h_keep[where, :].astype(F32) + h_got[where, :].astype(F32)
            if i == n + 2:
                for copy, (_, _, where) in zip(s_last, s_moves):
                    copy.wait_recv()
                    stack_out[where, :] = s_keep[0, where, :].astype(F32) + s_got4[where, :].astype(F32)
        for copy in sent:
            copy.wait_send()

    def vmem(*shape, dtype=BF):
        return pltpu.VMEM(shape, dtype)

    dma = pltpu.SemaphoreType.DMA
    ns, nh = len(stacks), len(halves)
    hbm = pl.BlockSpec(memory_space=pl.ANY)
    inside = pl.BlockSpec(memory_space=pltpu.VMEM)
    return pl.pallas_call(
        body,
        in_specs=[hbm] * (len(mains) + ns + nh) + [inside],
        out_specs=[inside] * 4,
        out_shape=[
            sds((l_main, 128), F32),
            sds((l_stack, 128), F32),
            sds((l_half, 128), F32),
            sds((rows, 128), F32),
        ],
        scratch_shapes=[
            vmem(2, 4, l_main, 128),
            vmem(2, 4, l_main, 128),
            vmem(4, l_main, 128),
            vmem(2, l_main, 128),
            vmem(l_main, 128),
            vmem(2, l_stack, 128),
            vmem(2, l_stack, 128),
            vmem(l_stack, 128),
            vmem(l_half, 128),
            vmem(l_half, 128),
            vmem(5, rows, 128, dtype=F32),
            dma((n, 2)),
            dma((n, 2)),
            dma((n, 2)),
            dma((n,)),
            dma((n,)),
            dma((n, 2)),
            dma((n, 2)),
            dma((n,)),
            dma((n,)),
            dma((ns, 2)),
            dma((ns, 3)),
            dma((ns, 3)),
            dma((nh,)),
            dma((nh,)),
            dma((nh,)),
            dma((5,)),
            dma((5,)),
        ],
        name="final_sums",
        compiler_params=pltpu.CompilerParams(
            vmem_limit_bytes=VMEM, collective_id=1, has_side_effects=True
        ),
        cost_estimate=pl.CostEstimate(flops=int(100 * SCALE), bytes_accessed=0, transcendentals=0),
    )(*mains, *stacks, *halves, vector)


def after(value, *deps):
    return lax.optimization_barrier((value, *deps))[0]


def spread(units):
    return jnp.transpose(units, (1, 0, 2)).reshape(units.shape[1], -1)


def tables(place):
    lane = jnp.arange(128)
    frequency = 100.0 ** (-(lane % 16).astype(F32) * 2.0 / 32.0)
    position = jnp.where((lane % 64 < 32)[None, :], place[0][:, None], place[1][:, None])
    angle = position * frequency[None, :]
    sin = jnp.sin(angle)
    return jnp.cos(angle), jnp.where((lane % 32 < 16)[None, :], -sin, sin)


def local(
    tokens,
    out_grad,
    masks,
    coords,
    enc_qkv,
    enc_out,
    enc_up,
    enc_down,
    enc_gains,
    enc_biases,
    proj,
    dec_in,
    dec_outs,
    dec_down,
    dec_gains,
    dec_biases,
):
    n_pair, n_view = lax.axis_size("pair"), lax.axis_size("view")
    quarter, pair_id = lax.axis_index("view"), lax.axis_index("pair")
    half_id, view_id, core = quarter % 2, quarter // 2, pair_id % 2
    half = jnp.stack([half_id, core]).astype(jnp.int32)
    rows = tokens.shape[1]
    tokens, out_grad, masks = tokens[0], out_grad[0], masks[0]
    chip_plan = n_pair == 8 and n_view == 4

    def trade(value):
        moves = []
        for p in range(n_pair):
            for t in range(n_view):
                moves.append((p * n_view + t, (p - p % 2 + t % 2) * n_view + t - t % 2 + p % 2))
        return lax.ppermute(value, ("pair", "view"), moves)

    far_coords = swap(coords[:, 0], "pair", 1)
    place = jnp.where(core == half_id, coords[:, 0], far_coords).astype(F32)
    tokens = trade(tokens)

    s3 = 3 * DD

    def share(array):
        if not chip_plan:
            return array
        count = array.shape[0] // n_pair
        return lax.dynamic_slice_in_dim(array, pair_id * count, count, 0)

    def gather(array):
        return lax.all_gather(array, "pair", axis=0, tiled=True) if chip_plan else array

    first_piece = jnp.concatenate([share(dec_in)[:, :s3], share(dec_outs)], axis=1)
    up_piece, down_piece = share(dec_in)[:, s3:], share(dec_down)
    first_piece = swap(after(first_piece, tokens), "view", 1)
    up_piece = swap(after(up_piece, tokens), "view", 1)
    down_piece = swap(after(down_piece, tokens), "view", 1)
    far_gains, far_biases = swap(after((dec_gains, dec_biases), tokens), "view", 1)

    def join_row(mine, theirs):
        return jnp.where(
            half_id == 0, jnp.concatenate([mine, theirs]), jnp.concatenate([theirs, mine])
        ).astype(F32)[None]

    def seg(points, view, part):
        return lax.dynamic_slice_in_dim(points, (view * 2 + part) * rows, rows, 1)

    enc_scale, enc_shift = enc_gains.astype(F32)[None], enc_biases.astype(F32)[None]
    cos_own, sin_own = tables(seg(place, view_id, core))
    start = 4 * DE + FE
    g1, g2 = enc_scale[:, :DE], enc_scale[:, DE:]
    sh1 = enc_shift[:, start + DE : start + 2 * DE]
    sh2 = enc_shift[:, start + 2 * DE : start + 3 * DE]
    def given(dealt_pair, dep=None):
        mine, theirs = dealt_pair
        return mine, swap(theirs if dep is None else after(theirs, dep), "pair", 1), theirs

    e_q, e_kv, *e_n1t = lnproj(
        half, tokens, g1, sh1, Whole(enc_qkv), enc_shift[:, : 3 * DE], cos_own, sin_own, 1, 2, 3,
        "enc_qkv",
    )
    deps = []

    def pend(*values):
        deps.extend(values)

    def tie(value):
        out = after(value, *deps) if deps else value
        deps.clear()
        return out

    e_kvf = swap(e_kv, "pair", 1)
    far_first = gather(after(first_piece, e_q))
    late_place = after(place, e_q)
    out_grad, masks = trade(after((out_grad, masks), e_q))
    cos_far, sin_far = tables(seg(late_place, view_id, 1 - core))
    cos_ot, sin_ot = tables(seg(late_place, 1 - view_id, core))
    cos_of, sin_of = tables(seg(late_place, 1 - view_id, 1 - core))
    e_n1t = given(e_n1t)
    pend(e_n1t[1])
    e_p, e_o, *e_ot = attend(tie(half), e_q, e_kv, e_kvf, "enc_attend")
    far_up, far_down = gather(after(up_piece, e_o)), gather(after(down_piece, e_o))
    dec_scale, dec_shift = join_row(dec_gains, far_gains), join_row(dec_biases, far_biases)
    cos_all, back_all = jnp.concatenate([cos_own, cos_far]), -jnp.concatenate([sin_own, sin_far])
    cos_oth, back_oth = jnp.concatenate([cos_ot, cos_of]), -jnp.concatenate([sin_ot, sin_of])
    back_own = -sin_own
    e_ot = given(e_ot)
    e_x1, e_nm, e_nt, e_am, e_at, e_slope, z, e_xm, e_xt = ffn_forward(
        half, e_o, tokens, Whole(enc_out), enc_shift[:, 3 * DE : 4 * DE], g2, sh2, Whole(enc_up),
        enc_shift[:, 4 * DE : start], Whole(enc_down), enc_shift[:, start : start + DE],
        (proj, enc_shift[:, start + 3 * DE :]), 1024, "enc_ffn",
    )
    pend(e_ot[1])
    other_z = swap(z, "view", 2)
    d_gd = (out_grad.astype(F32) * masks.astype(F32)[:, None]).astype(BF)

    w_sqkv = Halves((dec_in, 0), (far_first, 0), 3 * DD // 2)
    w_cq = Halves((dec_in, 3 * DD // 2), (far_first, 3 * DD // 2), DD // 2)
    w_ckv = Halves((dec_in, 2 * DD), (far_first, 2 * DD), DD)
    w_so = Halves((dec_outs, 0), (far_first, s3), DD // 2)
    w_co = Halves((dec_outs, DD // 2), (far_first, s3 + DD // 2), DD // 2)
    w_up = Halves((dec_in, s3), (far_up, 0), FD // 2)
    w_down = Halves((dec_down, 0), (far_down, 0), DD // 2)
    ga, gb, gc, gd = [dec_scale[:, i * DD : (i + 1) * DD] for i in range(4)]
    sa, sb, sc, sd = [dec_shift[:, i * DD : (i + 1) * DD] for i in range(4)]
    s_q, s_kv, *s_nt = lnproj(
        tie(half), z, ga, sa, w_sqkv, dec_shift[:, 4 * DD : 7 * DD], cos_own, sin_own, 2, 4, 6,
        "dec_qkv",
    )
    s_kvf = swap(s_kv, "pair", 1)
    e_nt, s_nt = given((e_nm, e_nt), s_q), given(s_nt)
    s_p, s_o, *s_ot = attend(half, s_q, s_kv, s_kvf, "self_attend")
    pend(e_nt[1], s_nt[1], d_gd)
    e_at, e_xt, s_ot = given((e_am, e_at), s_o), given((e_xm, e_xt), s_o), given(s_ot)
    y1, c_q, *b_nt = mid_forward(
        tie(half), s_o, z, w_so, dec_shift[:, 7 * DD : 8 * DD], gb, sb, w_cq,
        dec_shift[:, 8 * DD : 9 * DD], cos_own, sin_own, "dec_mid",
    )
    pend(y1, e_at[1], s_ot[1])
    c_kv, *c_nt = lnproj(
        half, other_z, tie(gc), sc, w_ckv, dec_shift[:, 9 * DD : 11 * DD], cos_ot, sin_ot,
        0, 2, 4, "dec_ckv",
    )
    c_kvf = swap(c_kv, "pair", 1)
    b_nt, c_nt = given(b_nt), given(c_nt)
    pend(e_xt[1], b_nt[1])
    c_p, c_o, *c_ot = attend(tie(half), c_q, c_kv, c_kvf, "cross_attend")
    pend(c_nt[1])
    c_ot = given(c_ot)
    far_gd = swap(after(d_gd, c_o), "pair", 1)
    y2, d_nm, d_nt, d_am, d_at, d_slope, mixed = ffn_forward(
        tie(half), c_o, y1, w_co, dec_shift[:, 11 * DD : 12 * DD], gd, sd, w_up,
        dec_shift[:, 12 * DD : 12 * DD + FD], w_down, dec_shift[:, 12 * DD + FD :],
        None, 768, "dec_ffn",
    )
    pend(c_ot[1], far_gd)
    d_at, d_nt = given((d_am, d_at)), given((d_nm, d_nt))
    mixed = trade(mixed)

    chip = pair_id // 2
    pack = lambda *ids: jnp.stack([jnp.asarray(i, jnp.int32) for i in ids])
    dec_z = pack(half_id, 1 - half_id, 0, 1, 2, 3)
    enc_z = pack(quarter, quarter ^ 1, quarter ^ 2, quarter ^ 3, 0, 1, 2, 3)
    enc_near = pack(
        quarter, quarter ^ 1, quarter ^ 2, quarter ^ 3, chip, chip ^ 1, chip ^ 2, chip ^ 3
    )

    def blocks(plan, a, g, far, width, bn, name, **rest):
        if not chip_plan:
            return None
        nz = plan.shape[0] - 4
        out = weight_blocks(tie(plan), a[0], a[1], g, far, nz, width, bn, name, **rest)
        pend(out[0])
        return out

    def summed(out):
        return chip_sum(out[0]) if chip_plan else None

    d_gu, d_gco, grad_y2, d_doc, vb_down, vb_up, vg_d, vs_d, vb_co = ffn_backward(
        tie(half), d_gd, None, w_down, d_slope, w_up, y2, gd, w_co, 768, "dec_ffn_back"
    )
    pend(d_doc, d_at[1], d_nt[1])
    far_gu, far_gco = swap(d_gu, "pair", 1), swap(d_gco, "pair", 1)
    t_down = summed(blocks(dec_z, d_at, d_gd, far_gd, 384, 384, "dw_dec_down"))
    pend(far_gu, far_gco)
    c_own, c_ship = attend_back(
        tie(half), c_q, c_kv, c_kvf, c_p, c_o, d_doc, cos_own, back_own, cos_oth, back_oth,
        "cross_back",
    )
    c_back = swap(c_ship, "pair", 1)
    pend(c_own)
    t_up = summed(blocks(dec_z, d_nt, d_gu, far_gu, 1536, 768, "dw_dec_up"))
    pend(c_back)
    g_ckv, vb_ckv, grad_other, vg_c, vs_c = proj_backward(
        half, None, c_own, c_back, w_ckv, other_z, tie(gc), None, 384, "ckv_back"
    )
    returned = swap(grad_other, "view", 2)
    far_ckv = swap(g_ckv, "pair", 1)
    pend(g_ckv)
    grad_y1, d_gso, d_dos, vb_cq, vg_b, vs_b, vb_so = mid_backward(
        half, c_ship, w_cq, y1, tie(gb), grad_y2, w_so, "mid_back"
    )
    far_gso = swap(d_gso, "pair", 1)
    pend(d_dos, far_ckv)
    cross = blocks(dec_z, c_ot, d_gco, far_gco, 384, 384, "dw_co", total=12)
    cross = blocks(dec_z, b_nt, c_ship, c_back, 384, 384, "dw_cq", base=cross, at=3, total=12)
    pend(far_gso)
    t_cross = summed(
        blocks(dec_z, c_nt, g_ckv, far_ckv, 768, 768, "dw_ckv", base=cross, at=6, total=12)
    )
    s_own, s_ship = attend_back(
        tie(half), s_q, s_kv, s_kvf, s_p, s_o, d_dos, cos_own, back_own, cos_all, back_all, "self_back"
    )
    s_back = swap(s_ship, "pair", 1)
    pend(s_own)
    g_sqkv, vb_sqkv, grad_own, vg_a, vs_a = proj_backward(
        half, s_ship, s_own, s_back, w_sqkv, z, tie(ga), grad_y1, 384, "qkv_back"
    )
    far_sqkv = swap(g_sqkv, "pair", 1)
    e_gp, ub_proj, grad_x2, e_gd = head_backward(half, grad_own, returned, proj, "proj_back")
    far_egd, far_gp = swap(e_gd, "pair", 1), swap(e_gp, "pair", 1)
    pend(e_gd, far_sqkv)
    selfs = blocks(dec_z, s_ot, d_gso, far_gso, 384, 384, "dw_so", total=12)
    t_self = summed(
        blocks(dec_z, s_nt, g_sqkv, far_sqkv, 1152, 384, "dw_sqkv", base=selfs, at=3, total=12)
    )
    t_enc_down = summed(blocks(enc_z, e_at, e_gd, far_egd, 256, 256, "dw_enc_down"))
    pend(far_gp)
    e_gu, e_go, grad_x1, e_do, ub_down, ub_up, ug_2, us_2, ub_out = ffn_backward(
        half, e_gd, grad_x2, Whole(enc_down), e_slope, Whole(enc_up), e_x1, tie(g2), Whole(enc_out),
        1024, "enc_ffn_back",
    )
    far_egu, far_go = swap(e_gu, "pair", 1), swap(e_go, "pair", 1)
    pend(e_do, mixed)
    e_two = blocks(enc_near, e_xt, e_gp, far_gp, 256, 256, "dw_proj", at=8, total=10)
    pend(far_egu, far_go)

    e_two = blocks(enc_near, e_nt, e_gu, far_egu, 1024, 1024, "dw_enc_up", base=e_two, total=10)
    e_own, e_ship = attend_back(
        tie(half), e_q, e_kv, e_kvf, e_p, e_o, e_do, cos_own, back_own, cos_all, back_all, "enc_back"
    )
    e_back = swap(e_ship, "pair", 1)
    pend(e_own)
    e_three = blocks(enc_near, e_ot, e_go, far_go, 256, 256, "dw_out", at=6, total=8)
    pend(e_back)
    g_eqkv, ub_qkv, tokens_grad, ug_1, us_1 = proj_backward(
        half, e_ship, e_own, e_back, Whole(enc_qkv), tokens, tie(g1), grad_x1, 1024, "enc_qkv_back"
    )
    far_eqkv = swap(g_eqkv, "pair", 1)
    tokens_grad = trade(tokens_grad.astype(BF)).astype(F32)
    pend(g_eqkv)
    e_three = blocks(
        enc_near, e_n1t, g_eqkv, far_eqkv, 768, 768, "dw_enc_qkv", base=e_three, total=8
    )

    if chip_plan:
        def flat(array, lead):
            return array.reshape(*array.shape[:lead], -1, 128)

        def rows_of(vectors, count):
            joint = jnp.concatenate(vectors, axis=1)[0]
            return jnp.pad(joint, (0, count * 128 - joint.shape[0])).reshape(count, 128)

        enc_rows, dec_rows = 112, 128
        vector = jnp.concatenate(
            [
                rows_of([ug_1, ug_2, ub_qkv, ub_out, ub_up, ub_down, us_1, us_2, ub_proj], enc_rows),
                rows_of(
                    [
                        vg_a, vg_b, vg_c, vg_d, vs_a, vs_b, vs_c, vs_d,
                        vb_sqkv, vb_so, vb_cq, vb_ckv, vb_co, vb_up, vb_down,
                    ],
                    dec_rows,
                ),
            ]
        )
        mains = [flat(e_two[0], 2), flat(e_three[0], 2)]
        stacks, decs = [flat(t_enc_down, 1)], [flat(t, 1) for t in (t_down, t_up, t_cross, t_self)]
        main, t_enc_down, dec_all, vector = final_sums(mains, stacks, decs, vector, enc_rows)
        t_enc_up, t_last = main[:1280].reshape(10, 128, 128), main[1280:].reshape(8, 128, 128)
        t_enc_down = t_enc_down.reshape(2, 512, 128)
        t_down, t_up, t_cross, t_self = jnp.split(dec_all, 4)
        t_down = t_down.reshape(3, 384, 128)
        t_up, t_cross, t_self = [t.reshape(12, 96, 128) for t in (t_up, t_cross, t_self)]
        co, cq, ckv = jnp.split(t_cross, [3, 6])
        so, sqkv = jnp.split(t_self, [3])
        dec_in_grad = spread(jnp.concatenate([sqkv, cq, ckv, t_up], axis=0))
        dec_outs_grad = spread(jnp.concatenate([so, co], axis=0))
        dec_down_grad = spread(t_down)
        enc_down_grad, enc_up_grad = spread(t_enc_down), spread(t_enc_up[:8])
        proj_grad = spread(t_enc_up[8:])[:, : DD // 4]
        enc_qkv_grad, enc_out_grad = spread(t_last[:6]), spread(t_last[6:])
    else:
        def tall(pieces):
            mine, _, theirs = pieces
            even, odd = jnp.where(core == 0, mine, theirs), jnp.where(core == 0, theirs, mine)
            return jnp.stack([even, odd], axis=1).reshape(-1, rows)

        def scatter(value, axis, dim):
            return lax.psum_scatter(value.astype(BF), axis, scatter_dimension=dim, tiled=True)

        def enc_sum(a, g):
            return scatter(scatter(mm(tall(a), g), "pair", 0), "view", 1).astype(F32)

        def halves(value, which):
            width = value.shape[1] // 2
            return lax.dynamic_slice_in_dim(value, which * width, width, 1)

        def dec_sum(*pairs):
            blocks = [mm(tall(a), g) for a, g in pairs]
            mine = jnp.concatenate([halves(b, half_id) for b in blocks], axis=1)
            other = jnp.concatenate([halves(b, 1 - half_id) for b in blocks], axis=1)
            both = mine + swap(other.astype(BF), "view", 1).astype(F32)
            return scatter(both, "pair", 0).astype(F32)

        dec_in_grad = dec_sum((s_nt, g_sqkv), (b_nt, c_ship[2]), (c_nt, g_ckv), (d_nt, d_gu))
        dec_outs_grad = dec_sum((s_ot, d_gso), (c_ot, d_gco))
        dec_down_grad = dec_sum((d_at, d_gd))
        enc_qkv_grad, enc_out_grad = enc_sum(e_n1t, g_eqkv), enc_sum(e_ot, e_go)
        enc_up_grad, enc_down_grad = enc_sum(e_nt, e_gu), enc_sum(e_at, e_gd)
        proj_grad = enc_sum(e_xt, e_gp.reshape(rows, 4, -1)[:, :, : DD // 4].reshape(rows, DD))

    if chip_plan:
        enc_vec = vector[:enc_rows].reshape(-1)[: 9 * DE + FE + DD]
        dec_vec = vector[enc_rows:].reshape(-1)[: 17 * DD + FD]
    else:
        dec_vec = jnp.concatenate(
            [
                vg_a, vg_b, vg_c, vg_d, vs_a, vs_b, vs_c, vs_d,
                vb_sqkv, vb_so, vb_cq, vb_ckv, vb_co, vb_up, vb_down,
            ],
            axis=1,
        )[0]
        empty = jnp.zeros_like(dec_vec)
        enc_parts = [ug_1, ug_2, ub_qkv, ub_out, ub_up, ub_down, us_1, us_2, ub_proj]
        enc_vec, dec_one, dec_two = lax.psum(
            (
                jnp.concatenate(enc_parts, axis=1)[0],
                jnp.where(view_id == 0, dec_vec, empty),
                jnp.where(view_id == 0, empty, dec_vec),
            ),
            ("pair", "view"),
        )
        dec_vec = jnp.where(view_id == 0, dec_one, dec_two)
    enc_gains_grad, enc_biases_grad = enc_vec[: 2 * DE], enc_vec[2 * DE :]
    gain_all, bias_all = dec_vec[: 4 * DD], dec_vec[4 * DD :]
    gain_part, bias_part = gain_all.shape[0] // 2, bias_all.shape[0] // 2
    dec_gains_grad = lax.dynamic_slice_in_dim(gain_all, half_id * gain_part, gain_part, 0)
    dec_biases_grad = lax.dynamic_slice_in_dim(bias_all, half_id * bias_part, bias_part, 0)
    return (
        mixed[None],
        tokens_grad[None],
        enc_qkv_grad,
        enc_out_grad,
        enc_up_grad,
        enc_down_grad,
        enc_gains_grad,
        enc_biases_grad,
        proj_grad,
        dec_in_grad,
        dec_outs_grad,
        dec_down_grad,
        dec_gains_grad,
        dec_biases_grad,
    )


def solution(mesh):
    both = P("pair", "view")
    return jax.shard_map(
        local,
        mesh=mesh,
        in_specs=(
            P("pair", "view", None),
            P("pair", "view", None),
            both,
            P(None, "pair", None),
            P(),
            P(),
            P(),
            P(),
            P(),
            P(),
            P(),
            P(None, "view"),
            P(None, "view"),
            P(None, "view"),
            P("view"),
            P("view"),
        ),
        out_specs=(
            P("pair", "view", None),
            P("pair", "view", None),
            both,
            both,
            both,
            both,
            P(),
            P(),
            both,
            both,
            both,
            both,
            P("view"),
            P("view"),
        ),
        check_vma=False,
    )
```

```python
from functools import partial

import jax
import jax.numpy as jnp
from jax import lax
from jax.experimental import pallas as pl
from jax.experimental.pallas import tpu as pltpu
from jax.sharding import PartitionSpec as P

DE = 1024
HE = 16
FE = 4096
DD = 768
HD = 12
FD = 3072

norm_eps = 1e-06
BF = jnp.bfloat16
F32 = jnp.float32
VMEM = 58 * 1024 * 1024

NN = (((1,), (0,)), ((), ()))
NT = (((1,), (1,)), ((), ()))
TN = (((0,), (0,)), ((), ()))


def mm(a, b, dims=NN):
    return lax.dot_general(a, b, dims, preferred_element_type=F32)


def full(shape):
    zeros = (0,) * len(shape)
    return pl.BlockSpec(shape, lambda *_: zeros)


def sds(shape, dtype):
    return jax.ShapeDtypeStruct(shape, dtype)


MESH = pl.DeviceIdType.MESH


def across(axis, bit):
    here = lax.axis_index(axis)
    return {axis: here + bit - 2 * bit * ((here // bit) % 2)}


def greet(devices):
    barrier = pltpu.get_barrier_semaphore()
    for device in devices:
        pl.semaphore_signal(barrier, inc=1, device_id=device, device_id_type=MESH)
    pl.semaphore_wait(barrier, len(devices))


def carry(body, name, number, ride, grid, in_specs, out_specs, out_shape, args, scratch):
    landing, moves = [], []
    for k, (array, indices, axis, bit) in enumerate(ride):
        shape = jax.eval_shape(lambda a, i=indices[0]: a[i], array).shape if indices[0] else array.shape
        landing.append(sds((len(indices), *shape), array.dtype))
        moves += [(k, place, index, axis, bit) for place, index in enumerate(indices)]
    partners = sorted({(axis, bit) for _, _, axis, bit in ride})
    n_in, n_out, n_ride = len(in_specs), len(out_specs), len(ride)
    last = grid[0] - 1

    def plain(spec):
        return pl.BlockSpec(spec.block_shape, lambda j, index=spec.index_map: index(j, None))

    def shell(*refs):
        ins, refs = refs[:n_in], refs[n_in:]
        sources, refs = refs[:n_ride], refs[n_ride:]
        outs, refs = refs[:n_out], refs[n_out:]
        targets, refs = refs[:n_ride], refs[n_ride:]
        *rest, send_sem, recv_sem = refs
        j = pl.program_id(0)

        def copies():
            out = []
            for m, (k, place, index, axis, bit) in enumerate(moves):
                source = sources[k]
                if index:
                    source = source.at[
                        tuple(pl.ds(i.start, i.stop - i.start) if isinstance(i, slice) and i.stop else i for i in index)
                    ]
                out.append(
                    pltpu.make_async_remote_copy(
                        src_ref=source, dst_ref=targets[k].at[place], send_sem=send_sem.at[m],
                        recv_sem=recv_sem.at[m], device_id=across(axis, bit), device_id_type=MESH,
                    )
                )
            return out

        @pl.when(j == 0)
        def _():
            greet([across(axis, bit) for axis, bit in partners])
            for copy in copies():
                copy.start()

        body((lax.axis_index("view") % 2, lax.axis_index("pair") % 2), *ins, *outs, *rest)

        @pl.when(j == last)
        def _():
            for copy in copies():
                copy.wait()

    hbm = pl.BlockSpec(memory_space=pl.ANY)
    dma = pltpu.SemaphoreType.DMA((len(moves),))
    return pl.pallas_call(
        shell,
        grid=grid,
        in_specs=[plain(spec) for spec in in_specs] + [hbm] * n_ride,
        out_specs=[plain(spec) for spec in out_specs] + [hbm] * n_ride,
        out_shape=list(out_shape) + landing,
        scratch_shapes=list(scratch) + [dma, dma],
        name=name,
        compiler_params=pltpu.CompilerParams(
            vmem_limit_bytes=VMEM, collective_id=number, has_side_effects=True
        ),
        cost_estimate=cost(name),
    )(*args, *(array for array, *_ in ride))


def call(
    body, name, half, grid, in_specs, out_specs, out_shape, args, scratch=(), flops=0, nbytes=0,
    ride=None, number=0,
):
    if ride:
        return carry(body, name, number, ride, grid, in_specs, out_specs, out_shape, args, scratch)
    return pl.pallas_call(
        body,
        grid_spec=pltpu.PrefetchScalarGridSpec(
            num_scalar_prefetch=1,
            grid=grid,
            in_specs=in_specs,
            out_specs=out_specs,
            scratch_shapes=list(scratch),
        ),
        out_shape=out_shape,
        name=name,
        compiler_params=pltpu.CompilerParams(vmem_limit_bytes=VMEM),
        cost_estimate=cost(name),
    )(half, *args)


SCALE = 0.2e9

TIMES = {
    "enc_qkv": 8, "enc_attend": 19, "enc_ffn": 20, "dec_qkv": 8, "self_attend": 15, "dec_mid": 5,
    "dec_ckv": 7, "cross_attend": 15, "dec_ffn": 15, "dec_ffn_back": 13, "cross_back": 15,
    "mid_back": 5, "ckv_back": 7, "self_back": 15, "qkv_back": 10, "proj_back": 4,
    "enc_ffn_back": 18, "enc_back": 18, "enc_qkv_back": 11, "dw_dec_down": 6, "dw_dec_up": 6,
    "dw_co": 4, "dw_cq": 4, "dw_ckv": 4, "dw_so": 4, "dw_sqkv": 6, "dw_enc_down": 8, "dw_proj": 5,
    "dw_enc_up": 8, "dw_out": 5, "dw_enc_qkv": 7,
}


def cost(name):
    flops = int(TIMES[name] * SCALE)
    return pl.CostEstimate(flops=flops, bytes_accessed=0, transcendentals=0)


class Whole:
    def __init__(self, array):
        self.arrays, self.columns = [array], array.shape[1]
        self.rows = array.shape[0]

    def blocks(self, bn, fixed=False):
        return [pl.BlockSpec((self.rows, bn), lambda j, h: (0, j))]

    def whole(self, bn=None):
        if bn is None:
            return [full(self.arrays[0].shape)]
        return [pl.BlockSpec((bn, self.columns), lambda j, h: (j, 0))]

    def read(self, refs, h, j, bn):
        return refs[0][...]

    def read_whole(self, refs, h):
        return refs[0][...]


class Halves:
    def __init__(self, own, far, width):
        self.arrays = [own[0], far[0]]
        self.starts, self.width = (own[1], far[1]), width
        self.rows, self.columns = own[0].shape[0], 2 * width

    def blocks(self, bn, fixed=False):
        per = self.width // bn
        specs = []
        for which, start in enumerate(self.starts):

            def index(j, h, which=which, start=start):
                if fixed:
                    return 0, start // bn + j % per
                half = h[0] ^ which
                hold = jnp.where(half == 0, per - 1, 0)
                return 0, start // bn + jnp.where(j // per == half, j % per, hold)

            specs.append(pl.BlockSpec((self.rows, bn), index))
        return specs

    def whole(self, bn=None):
        specs = []
        for start in self.starts:
            col = start // self.width
            if bn is None:
                specs.append(pl.BlockSpec((self.rows, self.width), lambda j, h, col=col: (0, col)))
            else:
                specs.append(pl.BlockSpec((bn, self.width), lambda j, h, col=col: (j, col)))
        return specs

    def read(self, refs, h, j, bn):
        return jnp.where(j // (self.width // bn) == h[0], refs[0][...], refs[1][...])

    def read_whole(self, refs, h):
        own, far = refs[0][...], refs[1][...]
        first = h[0] == 0
        return jnp.concatenate([jnp.where(first, own, far), jnp.where(first, far, own)], axis=1)


def norm_parts(x):
    centred = x - jnp.mean(x, axis=-1, keepdims=True)
    rstd = lax.rsqrt(jnp.mean(centred * centred, axis=-1, keepdims=True) + norm_eps)
    return centred * rstd, rstd


def norm_back(dy, x, gain):
    xhat, rstd = norm_parts(x)
    dgain = jnp.sum(dy * xhat, axis=0, keepdims=True)
    dshift = jnp.sum(dy, axis=0, keepdims=True)
    dxh = dy * gain
    mean_one = jnp.mean(dxh, axis=-1, keepdims=True)
    mean_two = jnp.mean(dxh * xhat, axis=-1, keepdims=True)
    return rstd * (dxh - mean_one - xhat * mean_two), dgain, dshift


def turn(u, cos, sin):
    lane = lax.broadcasted_iota(jnp.int32, u.shape, 1)
    other = jnp.where(lane % 32 < 16, pltpu.roll(u, 112, 1), pltpu.roll(u, 16, 1))
    return u * cos + other * sin


def turn_cols(y, cos, sin):
    return jnp.concatenate(
        [turn(y[:, i : i + 128], cos, sin) for i in range(0, y.shape[1], 128)], axis=1
    )


def gelu_parts(u):
    z = jnp.abs(u) * 0.7071067811865476
    t = 1.0 / (1.0 + 0.3275911 * z)
    e = jnp.exp(-0.5 * u * u)
    poly = t * (
        0.254829592
        + t * (-0.284496736 + t * (1.421413741 + t * (-1.453152027 + t * 1.061405429)))
    )
    tail = 0.5 * poly * e
    phi = jnp.where(u >= 0, 1.0 - tail, tail)
    return u * phi, phi + u * e * 0.3989422804014327


def col_sum(g):
    return jnp.sum(g.astype(F32), axis=0, keepdims=True)


def deal(h, tall, mine, theirs, at=None):
    rb = mine.shape[1]
    for s in range(tall.shape[0] // (2 * rb)):
        even, odd = tall[2 * s * rb : (2 * s + 1) * rb], tall[(2 * s + 1) * rb : (2 * s + 2) * rb]
        first = h[1] == 0
        mine[s] = jnp.where(first, even, odd)
        theirs[s] = jnp.where(first, odd, even)


def dealt(width, rows):
    return [sds((4, width // 8, rows), BF)] * 2


def lnproj(half, x, gain, shift, w, b, cos, sin, n_q, n_turn, n_all, name, ride=None, number=0):
    rows, width = x.shape
    bn = w.columns // n_all
    n_w = len(w.arrays)
    has_q = n_q > 0

    def body(h, x_ref, g_ref, s_ref, b_ref, c_ref, sn_ref, *rest):
        w_refs, rest = rest[:n_w], rest[n_w:]
        if has_q:
            q_ref, kv_ref, mine, theirs, nrm = rest
        else:
            kv_ref, mine, theirs, nrm = rest
        j = pl.program_id(0)

        @pl.when(j == 0)
        def _():
            xhat, _ = norm_parts(x_ref[...].astype(F32))
            low = (xhat * g_ref[...] + s_ref[...]).astype(BF)
            nrm[...] = low
            deal(h, low.T, mine, theirs)

        y = mm(nrm[...], w.read(w_refs, h, j, bn)) + b_ref[...]

        @pl.when(j < n_turn)
        def _():
            out = turn_cols(y, c_ref[...], sn_ref[...]).astype(BF)
            if has_q:

                @pl.when(j < n_q)
                def _():
                    q_ref[...] = out

                @pl.when(j >= n_q)
                def _():
                    kv_ref[...] = out

            else:
                kv_ref[...] = out

        @pl.when(j >= n_turn)
        def _():
            kv_ref[...] = y.astype(BF)

    outs = [
        sds((rows, bn * (n_all - n_q)), BF),
        *dealt(width, rows),
    ]
    specs = [
        pl.BlockSpec((rows, bn), lambda j, h: (0, jnp.maximum(j - n_q, 0))),
        full((4, width // 8, rows)),
        full((4, width // 8, rows)),
    ]
    if has_q:
        outs.insert(0, sds((rows, bn * n_q), BF))
        specs.insert(0, pl.BlockSpec((rows, bn), lambda j, h: (0, jnp.minimum(j, n_q - 1))))
    return call(
        body,
        name,
        half,
        (n_all,),
        [
            full((rows, width)),
            full((1, width)),
            full((1, width)),
            pl.BlockSpec((1, bn), lambda j, h: (0, j)),
            full((rows, 128)),
            full((rows, 128)),
        ]
        + w.blocks(bn, bool(ride)),
        specs,
        outs,
        (x, gain, shift, b, cos, sin, *w.arrays),
        [pltpu.VMEM((rows, width), BF)],
        ride=ride,
        number=number,
    )


def two_heads(block):
    first = lax.broadcasted_iota(jnp.int32, block.shape, 1) < 64
    zero = jnp.zeros_like(block)
    return jnp.concatenate(
        [jnp.where(first, block, zero), jnp.where(first, zero, block)], axis=0
    )


def pick_heads(tall, rows):
    return jnp.concatenate([tall[:64, :rows], tall[64:, rows:]], axis=0)


def attend(half, q, kv, kvf, name, ride=None, number=0):
    rows, width = q.shape
    pairs = width // 128
    keys = 2 * rows

    def body(h, q_ref, ko_ref, vo_ref, kf_ref, vf_ref, p_ref, o_ref, mine, theirs, tall):
        q2 = two_heads(q_ref[...] * jnp.asarray(0.125, BF))
        k = jnp.concatenate([ko_ref[...], kf_ref[...]], axis=0)
        v = jnp.concatenate([vo_ref[...], vf_ref[...]], axis=0)
        vt = v.T
        pieces = []
        for c in range(0, 2 * rows, 256):
            s = mm(k, q2[c : c + 256], NT)
            e = jnp.exp(s - jnp.max(s, axis=0, keepdims=True))
            p = (e * (1.0 / jnp.sum(e, axis=0, keepdims=True))).astype(BF)
            p_ref[0, :, c : c + 256] = p
            pieces.append(mm(vt, p))
        t = pick_heads(jnp.concatenate(pieces, axis=1), rows)
        j = pl.program_id(0)
        tall[pl.ds(pl.multiple_of(j * 128, 128), 128), :] = t.astype(BF)
        o_ref[...] = t.T.astype(BF)

        @pl.when(j == pairs - 1)
        def _():
            deal(h, tall[...], mine, theirs)

    col = lambda j, h: (0, j)
    val = lambda j, h: (0, pairs + j)
    return call(
        body,
        name,
        half,
        (pairs,),
        [
            pl.BlockSpec((rows, 128), col),
            pl.BlockSpec((rows, 128), col),
            pl.BlockSpec((rows, 128), val),
            pl.BlockSpec((rows, 128), col),
            pl.BlockSpec((rows, 128), val),
        ],
        [
            pl.BlockSpec((1, keys, 2 * rows), lambda j, h: (j, 0, 0)),
            pl.BlockSpec((rows, 128), col),
            full((4, width // 8, rows)),
            full((4, width // 8, rows)),
        ],
        [
            sds((pairs, keys, 2 * rows), BF),
            sds((rows, width), BF),
            *dealt(width, rows),
        ],
        (q, kv, kv, kvf, kvf),
        [pltpu.VMEM((width, rows), BF)],
        ride=ride,
        number=number,
    )


def attend_back(half, q, kv, kvf, p, o, do, cos, sin, cos_all, sin_all, name, ride=None, number=0):
    rows, width = q.shape
    pairs = width // 128
    keys = 2 * rows

    def body(
        h, q_ref, ko_ref, vo_ref, kf_ref, vf_ref, p_ref, o_ref, do_ref, c_ref, s_ref, ca_ref, sa_ref,
        own_ref, ship_ref,
    ):
        q2 = two_heads(q_ref[...] * jnp.asarray(0.125, BF))
        k = jnp.concatenate([ko_ref[...], kf_ref[...]], axis=0)
        v = jnp.concatenate([vo_ref[...], vf_ref[...]], axis=0)
        kt = k.T
        do_low = do_ref[...]
        do2 = two_heads(do_low)
        prod = two_heads(do_low.astype(F32) * o_ref[...].astype(F32))
        inner = lax.dot_general(
            jnp.ones((8, 128), F32), prod, NT, precision=lax.Precision.HIGHEST,
            preferred_element_type=F32,
        )[:1]
        dk = jnp.zeros((keys, 128), F32)
        dv = jnp.zeros((keys, 128), F32)
        pieces = []
        for c in range(0, 2 * rows, 256):
            dp = mm(v, do2[c : c + 256], NT)
            pc = p_ref[0, :, c : c + 256]
            ds = (pc.astype(F32) * (dp - inner[:, c : c + 256])).astype(BF)
            dk += mm(ds, q2[c : c + 256])
            dv += mm(pc, do2[c : c + 256])
            pieces.append(mm(kt, ds))
        dq = pick_heads(jnp.concatenate(pieces, axis=1), rows).T * 0.125
        ship_ref[2] = turn(dq, c_ref[...], s_ref[...]).astype(BF)
        dk = turn(dk, ca_ref[...], sa_ref[...])
        own_ref[0] = dk[:rows]
        own_ref[1] = dv[:rows]
        ship_ref[0] = dk[rows:].astype(BF)
        ship_ref[1] = dv[rows:].astype(BF)

    col = lambda j, h: (0, j)
    val = lambda j, h: (0, pairs + j)
    return call(
        body,
        name,
        half,
        (pairs,),
        [
            pl.BlockSpec((rows, 128), col),
            pl.BlockSpec((rows, 128), col),
            pl.BlockSpec((rows, 128), val),
            pl.BlockSpec((rows, 128), col),
            pl.BlockSpec((rows, 128), val),
            pl.BlockSpec((1, keys, 2 * rows), lambda j, h: (j, 0, 0)),
            pl.BlockSpec((rows, 128), col),
            pl.BlockSpec((rows, 128), col),
            full((rows, 128)),
            full((rows, 128)),
            full((keys, 128)),
            full((keys, 128)),
        ],
        [
            pl.BlockSpec((2, rows, 128), lambda j, h: (0, 0, j)),
            pl.BlockSpec((3, rows, 128), lambda j, h: (0, 0, j)),
        ],
        [sds((2, rows, width), F32), sds((3, rows, width), BF)],
        (q, kv, kv, kvf, kvf, p, o, do, cos, sin, cos_all, sin_all),
        (),
        ride=ride,
        number=number,
    )


def ffn_forward(half, o, resid, wo, bo, gain, shift, w_up, b_up, w_down, b_down, head, bn, name):
    rows, width = o.shape
    hidden = w_up.columns
    steps = hidden // bn
    n_w = len(wo.arrays)

    def body(h, o_ref, r_ref, bo_ref, g_ref, s_ref, bu_ref, bd_ref, *rest):
        wo_refs, up_refs, dn_refs, rest = rest[:n_w], rest[n_w : 2 * n_w], rest[2 * n_w : 3 * n_w], rest[3 * n_w :]
        if head:
            pj_ref, bp_ref, x1_ref, n_mine, n_theirs, a_mine, a_theirs, gp_ref, z_ref, *rest = rest
            x_mine, x_theirs, nrm, acc = rest
        else:
            x1_ref, n_mine, n_theirs, a_mine, a_theirs, gp_ref, z_ref, nrm, acc = rest
        j = pl.program_id(0)

        @pl.when(j == 0)
        def _():
            x1 = r_ref[...].astype(F32) + mm(o_ref[...], wo.read_whole(wo_refs, h)) + bo_ref[...]
            x1_ref[...] = x1
            xhat, _ = norm_parts(x1)
            low = (xhat * g_ref[...] + s_ref[...]).astype(BF)
            nrm[...] = low
            deal(h, low.T, n_mine, n_theirs)
            acc[...] = x1 + bd_ref[...]

        u = mm(nrm[...], w_up.read(up_refs, h, j, bn)) + bu_ref[...]
        act, slope = gelu_parts(u)
        act = act.astype(BF)
        gp_ref[...] = slope.astype(BF)
        deal(h, act.T, a_mine, a_theirs)
        acc[...] += mm(act, w_down.read_whole(dn_refs, h))

        @pl.when(j == steps - 1)
        def _():
            low = acc[...].astype(BF)
            if head:
                deal(h, low.T, x_mine, x_theirs)
                z_ref[...] = (mm(low, pj_ref[...]) + bp_ref[...]).astype(BF)
            else:
                z_ref[...] = low

    vec, whole = full((1, width)), full((rows, width))
    in_specs = (
        [whole, whole, vec, vec, vec, pl.BlockSpec((1, bn), lambda j, h: (0, j)), vec]
        + wo.whole()
        + w_up.blocks(bn)
        + w_down.whole(bn)
    )
    out_specs = [
        whole,
        full((4, width // 8, rows)),
        full((4, width // 8, rows)),
        pl.BlockSpec((bn * 4 // hidden, hidden // 8, rows), lambda j, h: (j, 0, 0)),
        pl.BlockSpec((bn * 4 // hidden, hidden // 8, rows), lambda j, h: (j, 0, 0)),
        pl.BlockSpec((rows, bn), lambda j, h: (0, j)),
    ]
    outs = [
        sds((rows, width), F32),
        *dealt(width, rows),
        *dealt(hidden, rows),
        sds((rows, hidden), BF),
    ]
    args = [o, resid, bo, gain, shift, b_up, b_down, *wo.arrays, *w_up.arrays, *w_down.arrays]
    if head:
        wide = head[0].shape[1]
        in_specs += [full((width, wide)), full((1, wide))]
        args += list(head)
        out_specs += [full((rows, wide)), full((4, width // 8, rows)), full((4, width // 8, rows))]
        outs += [sds((rows, wide), BF), *dealt(width, rows)]
    else:
        out_specs += [whole]
        outs += [sds((rows, width), BF)]
    return call(
        body,
        name,
        half,
        (steps,),
        in_specs,
        out_specs,
        outs,
        args,
        [pltpu.VMEM((rows, width), BF), pltpu.VMEM((rows, width), F32)],
        4 * rows * width * hidden + 2 * rows * width * width,
        4 * width * hidden + 4 * rows * hidden,
    )


def head_backward(half, grad, returned, proj, name):
    rows, wide = grad.shape
    width = proj.shape[0]

    part = wide // 4
    slot = -(-part // 128) * 128

    def body(h, g_ref, r_ref, s_ref, w_ref, low_ref, b_ref, gx_ref, gd_ref):
        back = jnp.concatenate([r_ref[...], s_ref[...]], axis=0)
        low = (g_ref[...] + back.astype(F32)).astype(BF)
        pad = jnp.zeros((rows, slot - part), BF)
        for t in range(4):
            piece = low[:, t * part : (t + 1) * part]
            low_ref[:, t * slot : (t + 1) * slot] = jnp.concatenate([piece, pad], axis=1)
        b_ref[...] = col_sum(low)
        gx = mm(low, w_ref[...], NT)
        gx_ref[...] = gx
        gd_ref[...] = gx.astype(BF)

    inside, outside = full((rows, wide)), full((rows, width))
    return call(
        body,
        name,
        half,
        (1,),
        [inside, full(returned[0].shape), full(returned[1].shape), full((width, wide))],
        [full((rows, 4 * slot)), full((1, wide)), outside, outside],
        [sds((rows, 4 * slot), BF), sds((1, wide), F32), sds((rows, width), F32), sds((rows, width), BF)],
        (grad, *returned, proj),
        (),
        2 * rows * wide * width,
        2 * wide * width,
    )


def ffn_backward(half, gd, base, w_down, slope, w_up, x, gain, wo, bn, name, ride=None, number=0):
    rows, width = x.shape
    hidden = w_up.columns
    steps = hidden // bn
    n_w = len(wo.arrays)
    has_base = base is not None

    def body(h, gd_ref, gp_ref, x_ref, g_ref, *refs):
        wo_refs, up_refs, dn_refs, refs = refs[:n_w], refs[n_w : 2 * n_w], refs[2 * n_w : 3 * n_w], refs[3 * n_w :]
        if has_base:
            base_ref, *refs = refs
        gu_ref, go_ref, gx_ref, do_ref, bd_ref, bu_ref, dg_ref, ds_ref, bo_ref, acc = refs
        j = pl.program_id(0)

        @pl.when(j == 0)
        def _():
            bd_ref[...] = col_sum(gd_ref[...])
            acc[...] = jnp.zeros_like(acc)

        da = mm(gd_ref[...], w_down.read_whole(dn_refs, h), NT)
        gu = (da * gp_ref[...].astype(F32)).astype(BF)
        gu_ref[...] = gu
        bu_ref[...] = col_sum(gu)
        acc[...] += mm(gu, w_up.read(up_refs, h, j, bn), NT)

        @pl.when(j == steps - 1)
        def _():
            dx, dg, ds = norm_back(acc[...], x_ref[...], g_ref[...])
            dg_ref[...] = dg
            ds_ref[...] = ds
            total = (base_ref[...] if has_base else gd_ref[...].astype(F32)) + dx
            gx_ref[...] = total
            go = total.astype(BF)
            go_ref[...] = go
            bo_ref[...] = col_sum(go)
            do_ref[...] = mm(go, wo.read_whole(wo_refs, h), NT).astype(BF)

    vec, whole = full((1, width)), full((rows, width))
    row = sds((1, width), F32)
    return call(
        body,
        name,
        half,
        (steps,),
        [whole, pl.BlockSpec((rows, bn), lambda j, h: (0, j)), whole, vec]
        + wo.whole()
        + w_up.blocks(bn)
        + w_down.whole(bn)
        + ([whole] if has_base else []),
        [
            pl.BlockSpec((rows, bn), lambda j, h: (0, j)),
            whole,
            whole,
            whole,
            vec,
            pl.BlockSpec((1, bn), lambda j, h: (0, j)),
            vec,
            vec,
            vec,
        ],
        [
            sds((rows, hidden), BF),
            sds((rows, width), BF),
            sds((rows, width), F32),
            sds((rows, width), BF),
            row,
            sds((1, hidden), F32),
            row,
            row,
            row,
        ],
        [gd, slope, x, gain, *wo.arrays, *w_up.arrays, *w_down.arrays] + ([base] if has_base else []),
        [pltpu.VMEM((rows, width), F32)],
        ride=ride,
        number=number,
    )


def mid_forward(half, o, resid, wo, bo, gain, shift, w, b, cos, sin, name):
    rows, width = o.shape

    def body(
        h, o_ref, r_ref, bo_ref, g_ref, s_ref, b_ref, c_ref, sn_ref, wo_own, wo_far, w_own, w_far,
        y_ref, q_ref, mine, theirs,
    ):
        y = r_ref[...].astype(F32) + mm(o_ref[...], wo.read_whole((wo_own, wo_far), h)) + bo_ref[...]
        y_ref[...] = y
        xhat, _ = norm_parts(y)
        low = (xhat * g_ref[...] + s_ref[...]).astype(BF)
        deal(h, low.T, mine, theirs)
        q = mm(low, w.read_whole((w_own, w_far), h)) + b_ref[...]
        q_ref[...] = turn_cols(q, c_ref[...], sn_ref[...]).astype(BF)

    whole, vec, table = full((rows, width)), full((1, width)), full((rows, 128))
    return call(
        body,
        name,
        half,
        (1,),
        [whole, whole, vec, vec, vec, vec, table, table] + wo.whole() + w.whole(),
        [whole, whole, full((4, width // 8, rows)), full((4, width // 8, rows))],
        [sds((rows, width), F32), sds((rows, width), BF), *dealt(width, rows)],
        (o, resid, bo, gain, shift, b, cos, sin, *wo.arrays, *w.arrays),
        (),
        4 * rows * width * width,
        4 * width * width,
    )


def mid_backward(half, gq, w, x, gain, above, wo, name, ride=None, number=0):
    rows, width = x.shape

    def body(
        h, gq_ref, x_ref, g_ref, a_ref, w_own, w_far, wo_own, wo_far,
        gx_ref, go_ref, do_ref, bq_ref, dg_ref, ds_ref, bo_ref,
    ):
        low = gq_ref[0]
        bq_ref[...] = col_sum(low)
        dx, dg, ds = norm_back(mm(low, w.read_whole((w_own, w_far), h), NT), x_ref[...], g_ref[...])
        dg_ref[...] = dg
        ds_ref[...] = ds
        total = a_ref[...] + dx
        gx_ref[...] = total
        go = total.astype(BF)
        go_ref[...] = go
        bo_ref[...] = col_sum(go)
        do_ref[...] = mm(go, wo.read_whole((wo_own, wo_far), h), NT).astype(BF)

    whole, vec = full((rows, width)), full((1, width))
    row = sds((1, width), F32)
    return call(
        body,
        name,
        half,
        (1,),
        [pl.BlockSpec((1, rows, width), lambda j, h: (2, 0, 0)), whole, vec, whole]
        + w.whole()
        + wo.whole(),
        [whole, whole, whole, vec, vec, vec, vec],
        [sds((rows, width), F32), sds((rows, width), BF), sds((rows, width), BF), row, row, row, row],
        (gq, x, gain, above, *w.arrays, *wo.arrays),
        ride=ride,
        number=number,
    )


def proj_backward(half, gq, own, back, w, x, gain, above, bn, name, ride=None, number=0):
    rows, width = x.shape
    steps, per = w.columns // bn, width // bn
    has_q, has_above = gq is not None, above is not None
    n_w = len(w.arrays)
    skip = per if has_q else 0

    def body(h, *refs):
        if has_q:
            gq_ref, *refs = refs
        own_ref, back_ref, x_ref, g_ref, *refs = refs
        w_refs, refs = refs[:n_w], refs[n_w:]
        if has_above:
            a_ref, *refs = refs
        g_out, b_ref, gx_ref, dg_ref, ds_ref, acc = refs
        j = pl.program_id(0)
        low = (own_ref[0] + back_ref[0].astype(F32)).astype(BF)
        if has_q:
            low = jnp.where(j < per, gq_ref[0], low)
        g_out[...] = low
        b_ref[...] = col_sum(low)
        piece = mm(low, w.read(w_refs, h, j, bn), NT)

        @pl.when(j == 0)
        def _():
            acc[...] = piece

        @pl.when(j > 0)
        def _():
            acc[...] += piece

        @pl.when(j == steps - 1)
        def _():
            dx, dg, ds = norm_back(acc[...], x_ref[...].astype(F32), g_ref[...])
            dg_ref[...] = dg
            ds_ref[...] = ds
            gx_ref[...] = (a_ref[...] + dx if has_above else dx).astype(gx_ref.dtype)

    whole, vec = full((rows, width)), full((1, width))

    def part_index(j, h):
        i = jnp.maximum(j - skip, 0)
        return i // per, 0, i % per

    part = pl.BlockSpec((1, rows, bn), part_index)
    in_specs = [part, part, whole, vec] + w.blocks(bn, bool(ride))
    args = [own, back, x, gain, *w.arrays]
    if has_q:
        in_specs.insert(0, pl.BlockSpec((1, rows, bn), lambda j, h: (2, 0, jnp.minimum(j, per - 1))))
        args.insert(0, gq)
    if has_above:
        in_specs.append(whole)
        args.append(above)
    row = sds((1, width), F32)
    return call(
        body,
        name,
        half,
        (steps,),
        in_specs,
        [
            pl.BlockSpec((rows, bn), lambda j, h: (0, j)),
            pl.BlockSpec((1, bn), lambda j, h: (0, j)),
            whole,
            vec,
            vec,
        ],
        [
            sds((rows, w.columns), BF),
            sds((1, w.columns), F32),
            sds((rows, width), F32 if has_above and n_w == 2 else BF),
            row,
            row,
        ],
        args,
        [pltpu.VMEM((rows, width), F32)],
        ride=ride,
        number=number,
    )


def weight_blocks(place, mine, far, g, g_far, nz, width, bn, name, base=None, at=0, total=None, apart=False):
    _, rb, rows = mine.shape
    per = width // bn
    units = bn // 128
    total = total or width // 128
    group = max(1, 512 // rb)

    def body(place_ref, a_ref, b_ref, g_ref, gf_ref, *rest):
        *outs, lhs = rest[1:] if base is not None else rest

        @pl.when((pl.program_id(0) == 0) & (pl.program_id(1) == 0))
        def _():
            for s in range(4):
                lhs[s * rb : (s + 1) * rb, :rows] = a_ref[place_ref[nz + s]]
                lhs[s * rb : (s + 1) * rb, rows:] = b_ref[place_ref[nz + s]]

        grad = jnp.concatenate([g_ref[...].reshape(rows, bn), gf_ref[...].reshape(rows, bn)], axis=0)
        for c in range(0, 4, group):
            n = min(4 - c, group)
            y = mm(lhs[c * rb : (c + n) * rb, :], grad).astype(BF)
            for s in range(n):
                for u in range(units):
                    piece = y[s * rb : (s + 1) * rb, u * 128 : (u + 1) * 128]
                    if apart:
                        outs[c + s][0, u] = piece
                    else:
                        outs[0][c + s, 0, u] = piece

    if g.ndim == 3:
        columns = pl.BlockSpec((1, rows, bn), lambda i, j, z: (2, 0, z[i] * per + j))
    else:
        columns = pl.BlockSpec((rows, bn), lambda i, j, z: (0, z[i] * per + j))
    skip = at // units
    if apart:
        shape = [sds((nz, total, rb, 128), BF)] * 4
        specs = [pl.BlockSpec((1, units, rb, 128), lambda i, j, z: (i, skip + j, 0, 0))] * 4
    else:
        shape = [sds((4, nz, total, rb, 128), BF)]
        specs = [pl.BlockSpec((4, 1, units, rb, 128), lambda i, j, z: (0, i, skip + j, 0, 0))]
    in_specs = [full((4, rb, rows)), full((4, rb, rows)), columns, columns]
    args, aliases = [mine, far, g, g_far], {}
    if base is not None:
        for k, array in enumerate(base):
            in_specs.append(pl.BlockSpec(memory_space=pl.ANY))
            args.append(array)
            aliases[5 + k] = k

    def shell(place_ref, a_ref, b_ref, g_ref, gf_ref, *rest):
        kept = rest[len(base) - 1 :] if base is not None else rest
        body(place_ref, a_ref, b_ref, g_ref, gf_ref, *kept)

    return pl.pallas_call(
        shell,
        grid_spec=pltpu.PrefetchScalarGridSpec(
            num_scalar_prefetch=1,
            grid=(nz, per),
            in_specs=in_specs,
            out_specs=specs,
            scratch_shapes=[pltpu.VMEM((4 * rb, 2 * rows), BF)],
        ),
        out_shape=shape,
        name=name,
        input_output_aliases=aliases,
        compiler_params=pltpu.CompilerParams(vmem_limit_bytes=VMEM),
        cost_estimate=cost(name),
    )(place, *args)


def swap(value, axis, distance):
    size = lax.axis_size(axis)
    return lax.ppermute(value, axis, [(i, i ^ distance) for i in range(size)])


def plus(a, b):
    return (a.astype(F32) + b.astype(F32)).astype(BF)


def chip_sum(blocks):
    groups = [[0, 2, 4, 6], [1, 3, 5, 7]]
    flat = blocks.reshape(-1, 128)
    out = lax.psum_scatter(flat, "pair", scatter_dimension=0, axis_index_groups=groups, tiled=True)
    return out.reshape(blocks.shape[1:])


STAY = ((0, 2), (0, 1))
AWAY = ((1, 3), (2, 3))
BITS = (2, 4)


def final_sums(mains, stacks, pairs, added, layout, shapes, vectors, traded):
    arrays, chunks, base = [array for array, _ in mains], [], 0
    for k, (array, parts) in enumerate(mains):
        chunks += [(k, row, count, order, base + row, array.shape[1]) for row, count, order in parts]
        base += array.shape[2]
    n, l_main = len(chunks), base
    l_stack = sum(array.shape[1] for array in stacks)
    l_pair = sum(array.shape[1] for array in pairs)
    n_arr, ns, np, na = len(arrays), len(stacks), len(pairs), len(added)
    enc_vectors, dec_vectors = vectors
    nv = len(enc_vectors) + len(dec_vectors)
    enc_count, dec_count = [sum(v.shape[1] for v in group) // 128 for group in vectors]
    vector_enc = -(-enc_count // 8) * 8
    rows = vector_enc + -(-dec_count // 8) * 8
    gain_rows, dec_gain = 2 * DE // 128, 4 * DD // 128
    dec_bias = dec_count - dec_gain
    ahead = 4

    def body(*refs):
        m_refs, refs = refs[:n_arr], refs[n_arr:]
        s_refs, refs = refs[:ns], refs[ns:]
        p_refs, refs = refs[:np], refs[np:]
        a_refs, refs = refs[: 2 * na], refs[2 * na :]
        v_refs, refs = refs[:nv], refs[nv:]
        t_ref, *refs = refs
        outs, refs = refs[: len(shapes)], refs[len(shapes) :]
        (
            gains_out, biases_out, dec_gains_out, dec_biases_out, t_out, v_out, t_keep, t_in, t_send, t_recv,
            keep, got1, got2, got3, got4, s_keep, s_got3, s_got4, p_keep, p_got, v_got,
            in_sem, send1, recv1, send2, recv2, send3, recv3, send4, recv4,
            s_in, s_send, s_recv, p_in, p_send, p_recv, v_send, v_recv,
        ) = refs
        core, x, y = across("pair", 1), across("pair", 2), across("pair", 4)
        z1, z2 = across("view", 1), across("view", 2)
        axes = (x, y)
        slanted = {**core, **z1}
        greet((core, x, y, z1, z2, slanted))
        stays = lax.axis_index("pair") % 2 == lax.axis_index("view") % 2
        t_local = pltpu.make_async_copy(t_ref, t_keep, t_in)
        t_remote = pltpu.make_async_remote_copy(
            src_ref=t_ref, dst_ref=t_keep, send_sem=t_send, recv_sem=t_recv, device_id=slanted,
            device_id_type=MESH,
        )

        @pl.when(stays)
        def _():
            t_local.start()

        @pl.when(jnp.logical_not(stays))
        def _():
            t_remote.start()

        sent = []

        def send(src, dst, send_sem, recv_sem, device, late=True):
            copy = pltpu.make_async_remote_copy(
                src_ref=src, dst_ref=dst, send_sem=send_sem, recv_sem=recv_sem,
                device_id=device, device_id_type=MESH,
            )
            copy.start()
            if late:
                sent.append(copy)
            return copy

        def fetch(src, dst, sem):
            copy = pltpu.make_async_copy(src, dst, sem)
            copy.start()
            return copy

        def at(i):
            return pl.ds(chunks[i][4], chunks[i][2])

        def store(places, total):
            row = 0
            for count, out, column in places:
                outs[out][:, column : column + 128] = total[row : row + count]
                row += count

        one, two, three, four, loads = {}, {}, {}, {}, {}

        def start_one(i):
            k, row, count, order, _, nz = chunks[i]
            one[i] = [
                send(
                    m_refs[k].at[slot, :, pl.ds(row, count), :], got1.at[q, pl.ds(0, nz), at(i), :],
                    send1.at[i, q], recv1.at[i, q], axes[order],
                )
                for q, slot in enumerate(AWAY[order])
            ]

        def start_load(i):
            k, row, count, order, _, nz = chunks[i]
            loads[i] = [
                fetch(
                    m_refs[k].at[slot, :, pl.ds(row, count), :], keep.at[q, pl.ds(0, nz), at(i), :],
                    in_sem.at[i, q],
                )
                for q, slot in enumerate(STAY[order])
            ]

        def start_two(i):
            device = axes[1 - chunks[i][3]]
            nz = pl.ds(0, chunks[i][5])
            two[i] = send(
                keep.at[1, nz, at(i), :], got2.at[nz, at(i), :], send2.at[i], recv2.at[i], device
            )

        def start_three(i):
            three[i] = [
                send(keep.at[0, slot, at(i), :], got3.at[q, at(i), :], send3.at[i, q], recv3.at[i, q], z1)
                for q, slot in enumerate((1, 3)[: chunks[i][5] // 2])
            ]

        def start_four(i):
            four[i] = send(keep.at[0, 2, at(i), :], got4.at[at(i), :], send4.at[i], recv4.at[i], z2)

        for i in range(min(ahead, n)):
            start_one(i)
        for i in range(n):
            start_load(i)
        v_out[...] = jnp.zeros_like(v_out)
        row = 0
        for k, ref in enumerate(v_refs):
            row = vector_enc if k == len(enc_vectors) else row
            for u in range(ref.shape[1] // 128):
                v_out[row : row + 1, :] = ref[:, u * 128 : (u + 1) * 128]
                row += 1
        v_axes = (core, x, y, z1, z2)

        def start_vector(r):
            count = vector_enc if r == 4 else rows
            return send(
                v_out.at[pl.ds(0, count), :], v_got.at[r, pl.ds(0, count), :],
                v_send.at[r], v_recv.at[r], v_axes[r], late=False,
            )

        flying = start_vector(0)
        offset, s_moves = 0, []
        for k, ref in enumerate(s_refs):
            size = ref.shape[1]
            where = pl.ds(offset, size)
            s_moves.append(
                (
                    [
                        send(ref.at[slot], s_got3.at[q, where, :], s_send.at[k, q], s_recv.at[k, q], z1)
                        for q, slot in enumerate((1, 3))
                    ],
                    [
                        fetch(ref.at[slot], s_keep.at[q, where, :], s_in.at[k, q])
                        for q, slot in enumerate((0, 2))
                    ],
                    where,
                )
            )
            offset += size
        offset, p_moves = 0, []
        for k, ref in enumerate(p_refs):
            where = pl.ds(offset, ref.shape[1])
            p_moves.append(
                (
                    send(ref.at[1], p_got.at[where, :], p_send.at[k], p_recv.at[k], z2),
                    fetch(ref.at[0], p_keep.at[where, :], p_in.at[k]),
                    where,
                )
            )
            offset += ref.shape[1]

        mark = n // 2
        s_last = []
        for i in range(n + 6):
            if i < n:
                for copy in loads[i]:
                    copy.wait()
                for copy in one[i]:
                    copy.wait_recv()
                nz = pl.ds(0, chunks[i][5])
                keep[:, nz, at(i), :] = keep[:, nz, at(i), :] + got1[:, nz, at(i), :]
                start_two(i)
                if i + ahead < n:
                    start_one(i + ahead)
            j = i - 2
            if 0 <= j < n:
                two[j].wait_recv()
                nz = pl.ds(0, chunks[j][5])
                keep[0, nz, at(j), :] = keep[0, nz, at(j), :] + got2[nz, at(j), :]
                start_three(j)
            if i == mark:
                for k, (moves, reads, where) in enumerate(s_moves):
                    for copy in reads:
                        copy.wait()
                    for copy in moves:
                        copy.wait_recv()
                    for q in range(2):
                        s_keep[q, where, :] = s_keep[q, where, :] + s_got3[q, where, :]
                    s_last.append(
                        send(s_keep.at[1, where, :], s_got4.at[where, :], s_send.at[k, 2], s_recv.at[k, 2], z2)
                    )
            j = i - 4
            if 0 <= j < n:
                for copy in three[j]:
                    copy.wait_recv()
                if chunks[j][5] == 4:
                    keep[0, 0, at(j), :] = keep[0, 0, at(j), :] + got3[0, at(j), :]
                    keep[0, 2, at(j), :] = keep[0, 2, at(j), :] + got3[1, at(j), :]
                    start_four(j)
            j = i - 6
            if 0 <= j < n:
                row = chunks[j][4]
                if chunks[j][5] == 4:
                    four[j].wait_recv()
                    last = got4[at(j), :]
                else:
                    last = got3[0, at(j), :]
                total = keep[0, 0, at(j), :].astype(F32) + last.astype(F32)
                done = 0
                for count, out, column in main_places:
                    if done >= row and done < row + chunks[j][2]:
                        outs[out][:, column : column + 128] = total[done - row : done - row + count]
                    done += count
            if i % 2 == 1 and i // 2 < 5:
                r = i // 2
                flying.wait()
                count = vector_enc if r == 4 else rows
                v_out[pl.ds(0, count), :] = v_out[pl.ds(0, count), :] + v_got[r, pl.ds(0, count), :]
                if r < 4:
                    flying = start_vector(r + 1)
            if i == n - 1:
                for k in range(na):
                    total = a_refs[2 * k][...].astype(F32) + a_refs[2 * k + 1][...].astype(F32)
                    store(layout[len(mains) + ns + np + k], total)
                for k, (move, read, where) in enumerate(p_moves):
                    read.wait()
                    move.wait_recv()
                    total = p_keep[where, :].astype(F32) + p_got[where, :].astype(F32)
                    store(layout[len(mains) + ns + k], total)
            if i == n + 3:
                for k, (copy, (_, _, where)) in enumerate(zip(s_last, s_moves)):
                    copy.wait_recv()
                    total = s_keep[0, where, :].astype(F32) + s_got4[where, :].astype(F32)
                    store(layout[len(mains) + k], total)
        gains_out[...] = v_out[:gain_rows]
        biases_out[...] = v_out[gain_rows:enc_count]
        first = lax.axis_index("view") % 2 == 0
        for out, base, count in ((dec_gains_out, 0, dec_gain), (dec_biases_out, dec_gain, dec_bias)):
            start, half = vector_enc + base, count // 2
            one, two_ = v_out[start : start + half], v_out[start + half : start + count]
            out[...] = jnp.where(first, one, two_)

        @pl.when(stays)
        def _():
            t_local.wait()

        @pl.when(jnp.logical_not(stays))
        def _():
            t_remote.wait()

        t_out[...] = t_keep[...].astype(F32)
        for copy in sent:
            copy.wait_send()

    main_places = [place for part in layout[: len(mains)] for place in part]

    def vmem(*shape, dtype=BF):
        return pltpu.VMEM(shape, dtype)

    dma = pltpu.SemaphoreType.DMA
    hbm = pl.BlockSpec(memory_space=pl.ANY)
    inside = pl.BlockSpec(memory_space=pltpu.VMEM)
    return pl.pallas_call(
        body,
        in_specs=[hbm] * (n_arr + ns + np) + [inside] * (2 * na + nv) + [hbm],
        out_specs=[inside] * (len(shapes) + 5),
        out_shape=[sds(shape, F32) for shape in shapes]
        + [sds((count, 128), F32) for count in (gain_rows, enc_count - gain_rows, dec_gain // 2, dec_bias // 2)]
        + [sds(traded.shape, F32)],
        scratch_shapes=[
            pltpu.VMEM((rows, 128), F32),
            pltpu.VMEM(traded.shape, BF),
            pltpu.SemaphoreType.DMA,
            pltpu.SemaphoreType.DMA,
            pltpu.SemaphoreType.DMA,
            vmem(2, 4, l_main, 128),
            vmem(2, 4, l_main, 128),
            vmem(4, l_main, 128),
            vmem(2, l_main, 128),
            vmem(l_main, 128),
            vmem(2, l_stack, 128),
            vmem(2, l_stack, 128),
            vmem(l_stack, 128),
            vmem(l_pair, 128),
            vmem(l_pair, 128),
            vmem(5, rows, 128, dtype=F32),
            dma((n, 2)),
            dma((n, 2)),
            dma((n, 2)),
            dma((n,)),
            dma((n,)),
            dma((n, 2)),
            dma((n, 2)),
            dma((n,)),
            dma((n,)),
            dma((ns, 2)),
            dma((ns, 3)),
            dma((ns, 3)),
            dma((np,)),
            dma((np,)),
            dma((np,)),
            dma((5,)),
            dma((5,)),
        ],
        name="final_sums",
        compiler_params=pltpu.CompilerParams(
            vmem_limit_bytes=VMEM, collective_id=1, has_side_effects=True
        ),
        cost_estimate=pl.CostEstimate(flops=int(100 * SCALE), bytes_accessed=0, transcendentals=0),
    )(*arrays, *stacks, *pairs, *(a for pair in added for a in pair), *enc_vectors, *dec_vectors, traded)


def hand_over(arrays, vectors):
    ins = [*arrays, *vectors]
    shapes = [array.shape for array in ins]
    shapes[4] = (shapes[4][0], DD // 4)

    def body(*refs):
        for source, target in zip(refs[: len(ins)], refs[len(ins) :]):
            target[...] = source[:, : target.shape[1]]

    inside = pl.BlockSpec(memory_space=pltpu.VMEM)
    return pl.pallas_call(
        body,
        in_specs=[inside] * len(ins),
        out_specs=[inside] * len(ins),
        out_shape=[sds(shape, F32) for shape in shapes],
        name="hand_over",
        compiler_params=pltpu.CompilerParams(vmem_limit_bytes=VMEM),
    )(*ins)


def after(value, *deps):
    return lax.optimization_barrier((value, *deps))[0]


def spread(units):
    return jnp.transpose(units, (1, 0, 2)).reshape(units.shape[1], -1)


def tables(place):
    lane = jnp.arange(128)
    frequency = 100.0 ** (-(lane % 16).astype(F32) * 2.0 / 32.0)
    position = jnp.where((lane % 64 < 32)[None, :], place[0][:, None], place[1][:, None])
    angle = position * frequency[None, :]
    sin = jnp.sin(angle)
    return jnp.cos(angle), jnp.where((lane % 32 < 16)[None, :], -sin, sin)


def local(
    tokens,
    out_grad,
    masks,
    coords,
    enc_qkv,
    enc_out,
    enc_up,
    enc_down,
    enc_gains,
    enc_biases,
    proj,
    dec_in,
    dec_outs,
    dec_down,
    dec_gains,
    dec_biases,
):
    n_pair, n_view = lax.axis_size("pair"), lax.axis_size("view")
    quarter, pair_id = lax.axis_index("view"), lax.axis_index("pair")
    half_id, view_id, core = quarter % 2, quarter // 2, pair_id % 2
    half = jnp.stack([half_id, core]).astype(jnp.int32)
    rows = tokens.shape[1]
    tokens = tokens[0]
    d_gd = (out_grad[0].astype(F32) * masks[0].astype(F32)[:, None]).astype(BF)
    chip_plan = n_pair == 8 and n_view == 4

    def trade(value):
        moves = []
        for p in range(n_pair):
            for t in range(n_view):
                moves.append((p * n_view + t, (p - p % 2 + t % 2) * n_view + t - t % 2 + p % 2))
        return lax.ppermute(value, ("pair", "view"), moves)

    far_coords = swap(coords[:, 0], "pair", 1)
    place = jnp.where(core == half_id, coords[:, 0], far_coords).astype(F32)
    tokens = trade(tokens)

    s3 = 3 * DD

    def share(array):
        if not chip_plan:
            return array
        count = array.shape[0] // n_pair
        return lax.dynamic_slice_in_dim(array, pair_id * count, count, 0)

    def gather(array):
        return lax.all_gather(array, "pair", axis=0, tiled=True) if chip_plan else array

    first_piece = jnp.concatenate([share(dec_in)[:, :s3], share(dec_outs)], axis=1)
    up_piece, down_piece = share(dec_in)[:, s3:], share(dec_down)
    first_piece = swap(after(first_piece, tokens), "view", 1)
    far_small = swap(after(jnp.concatenate([dec_gains, dec_biases]), tokens), "view", 1)
    far_gains, far_biases = far_small[: dec_gains.shape[0]], far_small[dec_gains.shape[0] :]
    up_shape = up_piece.shape
    second_piece = jnp.concatenate([up_piece, down_piece.reshape(up_shape[0], -1)], axis=1)

    def join_row(mine, theirs):
        return jnp.where(
            half_id == 0, jnp.concatenate([mine, theirs]), jnp.concatenate([theirs, mine])
        ).astype(F32)[None]

    def seg(points, view, part):
        return lax.dynamic_slice_in_dim(points, (view * 2 + part) * rows, rows, 1)

    enc_scale, enc_shift = enc_gains.astype(F32)[None], enc_biases.astype(F32)[None]
    cos_own, sin_own = tables(seg(place, view_id, core))
    start = 4 * DE + FE
    g1, g2 = enc_scale[:, :DE], enc_scale[:, DE:]
    sh1 = enc_shift[:, start + DE : start + 2 * DE]
    sh2 = enc_shift[:, start + 2 * DE : start + 3 * DE]
    def given(dealt_pair, dep=None):
        mine, theirs = dealt_pair
        return mine, swap(theirs if dep is None else after(theirs, dep), "pair", 1), theirs

    e_q, e_kv, *e_n1t = lnproj(
        half, tokens, g1, sh1, Whole(enc_qkv), enc_shift[:, : 3 * DE], cos_own, sin_own, 1, 2, 3,
        "enc_qkv",
    )
    deps = []

    def pend(*values):
        deps.extend(values)

    def tie(value):
        out = after(value, *deps) if deps else value
        deps.clear()
        return out

    e_kvf = swap(e_kv, "pair", 1)
    far_first = gather(after(first_piece, e_q))
    second_piece = swap(after(second_piece, e_q), "view", 1)
    late_place = after(place, e_q)
    d_gd = trade(after(d_gd, e_q))
    cos_far, sin_far = tables(seg(late_place, view_id, 1 - core))
    cos_ot, sin_ot = tables(seg(late_place, 1 - view_id, core))
    cos_of, sin_of = tables(seg(late_place, 1 - view_id, 1 - core))
    e_n1t = given(e_n1t)
    e_p, e_o, *e_ot = attend(half, e_q, e_kv, e_kvf, "enc_attend")
    pend(e_n1t[1], second_piece)
    far_second = gather(after(second_piece, e_o))
    far_up, far_down = (far_second, 0), far_second[:, up_shape[1] :].reshape(dec_down.shape)
    dec_scale, dec_shift = join_row(dec_gains, far_gains), join_row(dec_biases, far_biases)
    cos_all, back_all = jnp.concatenate([cos_own, cos_far]), -jnp.concatenate([sin_own, sin_far])
    cos_oth, back_oth = jnp.concatenate([cos_ot, cos_of]), -jnp.concatenate([sin_ot, sin_of])
    back_own = -sin_own
    e_ot = given(e_ot)
    e_x1, e_nm, e_nt, e_am, e_at, e_slope, z, e_xm, e_xt = ffn_forward(
        tie(half), e_o, tokens, Whole(enc_out), enc_shift[:, 3 * DE : 4 * DE], g2, sh2, Whole(enc_up),
        enc_shift[:, 4 * DE : start], Whole(enc_down), enc_shift[:, start : start + DE],
        (proj, enc_shift[:, start + 3 * DE :]), 1024, "enc_ffn",
    )
    pend(e_ot[1], d_gd)
    cut = rows // 48 * 16 + 16
    upper, lower = (slice(0, cut),), (slice(cut, rows),)

    w_sqkv = Halves((dec_in, 0), (far_first, 0), 3 * DD // 2)
    w_cq = Halves((dec_in, 3 * DD // 2), (far_first, 3 * DD // 2), DD // 2)
    w_ckv = Halves((dec_in, 2 * DD), (far_first, 2 * DD), DD)
    w_so = Halves((dec_outs, 0), (far_first, s3), DD // 2)
    w_co = Halves((dec_outs, DD // 2), (far_first, s3 + DD // 2), DD // 2)
    w_up = Halves((dec_in, s3), far_up, FD // 2)
    w_down = Halves((dec_down, 0), (far_down, 0), DD // 2)
    ga, gb, gc, gd = [dec_scale[:, i * DD : (i + 1) * DD] for i in range(4)]
    sa, sb, sc, sd = [dec_shift[:, i * DD : (i + 1) * DD] for i in range(4)]
    s_q, s_kv, *s_nt, z_one = lnproj(
        half, z, tie(ga), sa, w_sqkv, dec_shift[:, 4 * DD : 7 * DD], cos_own, sin_own, 2, 4, 6,
        "dec_qkv", ride=[(z, [upper], "view", 2)], number=6,
    )
    s_kvf = swap(s_kv, "pair", 1)
    e_nt, s_nt = given((e_nm, e_nt), s_q), given(s_nt)
    s_p, s_o, *s_ot, z_two = attend(
        half, s_q, s_kv, s_kvf, "self_attend", ride=[(z, [lower], "view", 2)], number=7
    )
    other_z = jnp.concatenate([z_one[0], z_two[0]])
    pend(e_nt[1], s_nt[1])
    e_at, e_xt, s_ot = given((e_am, e_at), s_o), given((e_xm, e_xt), s_o), given(s_ot)
    y1, c_q, *b_nt = mid_forward(
        tie(half), s_o, z, w_so, dec_shift[:, 7 * DD : 8 * DD], gb, sb, w_cq,
        dec_shift[:, 8 * DD : 9 * DD], cos_own, sin_own, "dec_mid",
    )
    pend(y1, e_at[1], s_ot[1])
    c_kv, *c_nt = lnproj(
        half, other_z, tie(gc), sc, w_ckv, dec_shift[:, 9 * DD : 11 * DD], cos_ot, sin_ot,
        0, 2, 4, "dec_ckv",
    )
    c_kvf = swap(c_kv, "pair", 1)
    b_nt, c_nt = given(b_nt), given(c_nt)
    pend(e_xt[1], b_nt[1])
    c_p, c_o, *c_ot = attend(tie(half), c_q, c_kv, c_kvf, "cross_attend")
    pend(c_nt[1])
    c_ot = given(c_ot)
    far_gd = swap(after(d_gd, c_o), "pair", 1)
    y2, d_nm, d_nt, d_am, d_at, d_slope, mixed = ffn_forward(
        tie(half), c_o, y1, w_co, dec_shift[:, 11 * DD : 12 * DD], gd, sd, w_up,
        dec_shift[:, 12 * DD : 12 * DD + FD], w_down, dec_shift[:, 12 * DD + FD :],
        None, 768, "dec_ffn",
    )
    pend(c_ot[1], far_gd)
    d_at, d_nt = given((d_am, d_at)), given((d_nm, d_nt))
    mixed = trade(mixed)

    chip = pair_id // 2
    pack = lambda *ids: jnp.stack([jnp.asarray(i, jnp.int32) for i in ids])
    dec_z = pack(half_id, 1 - half_id, 0, 1, 2, 3)
    dec_near = pack(half_id, 1 - half_id, chip, chip ^ 1, chip ^ 2, chip ^ 3)
    enc_z = pack(quarter, quarter ^ 1, quarter ^ 2, quarter ^ 3, 0, 1, 2, 3)
    enc_near = pack(
        quarter, quarter ^ 1, quarter ^ 2, quarter ^ 3, chip, chip ^ 1, chip ^ 2, chip ^ 3
    )

    def blocks(plan, a, g, far, width, bn, name, **rest):
        if not chip_plan:
            return None
        nz = plan.shape[0] - 4
        out = weight_blocks(tie(plan), a[0], a[1], g, far, nz, width, bn, name, **rest)
        pend(out[0])
        return out

    def summed(out):
        return chip_sum(out[0]) if chip_plan else None

    pend(d_at[1])
    t_down = summed(blocks(dec_z, d_at, d_gd, far_gd, 384, 384, "dw_dec_down"))
    d_gu, d_gco, grad_y2, d_doc, vb_down, vb_up, vg_d, vs_d, vb_co = ffn_backward(
        tie(half), d_gd, None, w_down, d_slope, w_up, y2, gd, w_co, 768, "dec_ffn_back"
    )
    pend(d_doc, d_nt[1])
    far_gu, far_gco = swap(d_gu, "pair", 1), swap(d_gco, "pair", 1)
    pend(far_gu, far_gco)
    c_own, c_ship = attend_back(
        tie(half), c_q, c_kv, c_kvf, c_p, c_o, d_doc, cos_own, back_own, cos_oth, back_oth,
        "cross_back",
    )
    c_back = swap(c_ship, "pair", 1)
    pend(c_own)
    t_up = summed(blocks(dec_z, d_nt, d_gu, far_gu, 1536, 768, "dw_dec_up"))
    pend(c_back)
    g_ckv, vb_ckv, grad_other, vg_c, vs_c = proj_backward(
        half, None, c_own, c_back, w_ckv, other_z, tie(gc), None, 384, "ckv_back"
    )
    far_ckv = swap(g_ckv, "pair", 1)
    pend(g_ckv)
    grad_y1, d_gso, d_dos, vb_cq, vg_b, vs_b, vb_so = mid_backward(
        half, c_ship, w_cq, y1, tie(gb), grad_y2, w_so, "mid_back"
    )
    far_gso = swap(d_gso, "pair", 1)
    pend(d_dos, far_ckv)
    cross = blocks(dec_z, c_ot, d_gco, far_gco, 384, 384, "dw_co", total=12)
    cross = blocks(dec_z, b_nt, c_ship, c_back, 384, 384, "dw_cq", base=cross, at=3, total=12)
    pend(far_gso)
    t_cross = summed(
        blocks(dec_z, c_nt, g_ckv, far_ckv, 768, 768, "dw_ckv", base=cross, at=6, total=12)
    )
    s_own, s_ship, returned = attend_back(
        half, s_q, s_kv, s_kvf, s_p, s_o, tie(d_dos), cos_own, back_own, cos_all, back_all, "self_back",
        ride=[(grad_other, [lower], "view", 2)], number=2,
    )
    s_back = swap(s_ship, "pair", 1)
    pend(s_own)
    g_sqkv, vb_sqkv, grad_own, vg_a, vs_a, returned_up = proj_backward(
        half, s_ship, s_own, s_back, w_sqkv, z, tie(ga), grad_y1, 384, "qkv_back",
        ride=[(grad_other, [upper], "view", 2)], number=8,
    )
    returned = (returned_up[0], returned[0])
    far_sqkv = swap(g_sqkv, "pair", 1)
    e_gp, ub_proj, grad_x2, e_gd = head_backward(half, grad_own, returned, proj, "proj_back")
    far_egd, far_gp = swap(e_gd, "pair", 1), swap(e_gp, "pair", 1)
    pend(e_gd, far_sqkv)
    t_enc_down = summed(blocks(enc_z, e_at, e_gd, far_egd, 256, 256, "dw_enc_down"))
    selfs = blocks(dec_near, s_ot, d_gso, far_gso, 384, 384, "dw_so", total=12)
    selfs = blocks(dec_near, s_nt, g_sqkv, far_sqkv, 1152, 384, "dw_sqkv", base=selfs, at=3, total=12)
    pend(far_gp)
    e_gu, e_go, grad_x1, e_do, ub_down, ub_up, ug_2, us_2, ub_out, *dec_got = ffn_backward(
        half, e_gd, grad_x2, Whole(enc_down), e_slope, Whole(enc_up), e_x1, tie(g2), Whole(enc_out),
        1024, "enc_ffn_back", ride=[(t, [(1,)], "view", 1) for t in (t_down, t_up)] if chip_plan else None,
        number=3,
    )
    far_egu, far_go = swap(e_gu, "pair", 1), swap(e_go, "pair", 1)
    pend(e_do, mixed)
    e_two = blocks(enc_z, e_xt, e_gp, far_gp, 256, 256, "dw_proj", at=8, total=10)
    pend(far_egu, far_go)

    t_enc_up = summed(
        blocks(enc_z, e_nt, e_gu, far_egu, 1024, 1024, "dw_enc_up", base=e_two, total=10)
    )
    rides = [(t_cross, [(1,)], "view", 1)] if chip_plan else None
    e_own, e_ship, *rode = attend_back(
        half, e_q, e_kv, e_kvf, e_p, e_o, tie(e_do), cos_own, back_own, cos_all, back_all, "enc_back",
        ride=rides, number=4,
    )
    if chip_plan:
        down_got, up_got, cross_got = [got[0] for got in (*dec_got, *rode)]
    e_back = swap(e_ship, "pair", 1)
    pend(e_own)
    e_three = blocks(enc_near, e_ot, e_go, far_go, 256, 256, "dw_out", at=6, total=8)
    pend(e_back)
    rides = [(t_enc_down, [(1,), (3,)], "view", 1)] if chip_plan else None
    g_eqkv, ub_qkv, tokens_grad, ug_1, us_1, *rode = proj_backward(
        half, e_ship, e_own, e_back, Whole(enc_qkv), tokens, tie(g1), grad_x1, 1024, "enc_qkv_back",
        ride=rides, number=5,
    )
    far_eqkv = swap(g_eqkv, "pair", 1)
    pend(g_eqkv)
    e_three = blocks(
        enc_near, e_n1t, g_eqkv, far_eqkv, 768, 768, "dw_enc_qkv", base=e_three, total=8
    )

    if chip_plan:
        def flat(array, lead):
            return array.reshape(*array.shape[:lead], -1, 128)

        vectors = (
            [ug_1, ug_2, ub_qkv, ub_out, ub_up, ub_down, us_1, us_2, ub_proj],
            [
                vg_a, vg_b, vg_c, vg_d, vs_a, vs_b, vs_c, vs_d,
                vb_sqkv, vb_so, vb_cq, vb_ckv, vb_co, vb_up, vb_down,
            ],
        )
        t_enc_down = plus(jnp.stack([t_enc_down[0], t_enc_down[2]]), rode[0])
        mains = [
            (flat(selfs[0], 2), [(288 * c, 288, c % 2) for c in range(4)]),
            (flat(e_three[0], 2), [(128 * c, 128, c % 2) for c in range(8)]),
        ]
        stacks, pairs = [flat(t_enc_up, 1)], [flat(t_enc_down, 1)]
        added = [
            (flat(t_down[0], 0), flat(down_got, 0)),
            (flat(t_up[0], 0), flat(up_got, 0)),
            (flat(t_cross[0], 0), flat(cross_got, 0)),
        ]
        shapes = [
            (DE // 8, 3 * DE // 4), (DE // 8, DE // 4), (DE // 8, FE // 4), (FE // 8, DE // 4),
            (DE // 8, 256), (DD // 8, 3 * DD + FD // 2), (DD // 8, DD), (FD // 8, DD // 2),
        ]

        def run(count, units, out, column):
            return [(count, out, column + 128 * u) for u in range(units)]

        layout = [
            run(96, 3, 6, 0) + run(96, 9, 5, 0),
            run(128, 6, 0, 0) + run(128, 2, 1, 0),
            run(128, 8, 2, 0) + run(128, 2, 4, 0),
            run(512, 2, 3, 0),
            run(384, 3, 7, 0),
            run(96, 12, 5, 3 * DD),
            run(96, 3, 6, DD // 2) + run(96, 3, 5, 3 * DD // 2) + run(96, 6, 5, 2 * DD),
        ]
        results = final_sums(mains, stacks, pairs, added, layout, shapes, vectors, tokens_grad)
        (
            enc_qkv_grad, enc_out_grad, enc_up_grad, enc_down_grad, proj_grad, dec_in_grad,
            dec_outs_grad, dec_down_grad, tokens_grad, *vectors,
        ) = hand_over(results[:8] + results[12:], results[8:12])
        enc_gains_grad, enc_biases_grad, dec_gains_grad, dec_biases_grad = [
            v.reshape(-1) for v in vectors
        ]
    else:
        def tall(pieces):
            mine, _, theirs = pieces
            even, odd = jnp.where(core == 0, mine, theirs), jnp.where(core == 0, theirs, mine)
            return jnp.stack([even, odd], axis=1).reshape(-1, rows)

        def scatter(value, axis, dim):
            return lax.psum_scatter(value.astype(BF), axis, scatter_dimension=dim, tiled=True)

        def enc_sum(a, g):
            return scatter(scatter(mm(tall(a), g), "pair", 0), "view", 1).astype(F32)

        def halves(value, which):
            width = value.shape[1] // 2
            return lax.dynamic_slice_in_dim(value, which * width, width, 1)

        def dec_sum(*pairs):
            blocks = [mm(tall(a), g) for a, g in pairs]
            mine = jnp.concatenate([halves(b, half_id) for b in blocks], axis=1)
            other = jnp.concatenate([halves(b, 1 - half_id) for b in blocks], axis=1)
            both = mine + swap(other.astype(BF), "view", 1).astype(F32)
            return scatter(both, "pair", 0).astype(F32)

        dec_in_grad = dec_sum((s_nt, g_sqkv), (b_nt, c_ship[2]), (c_nt, g_ckv), (d_nt, d_gu))
        dec_outs_grad = dec_sum((s_ot, d_gso), (c_ot, d_gco))
        dec_down_grad = dec_sum((d_at, d_gd))
        enc_qkv_grad, enc_out_grad = enc_sum(e_n1t, g_eqkv), enc_sum(e_ot, e_go)
        enc_up_grad, enc_down_grad = enc_sum(e_nt, e_gu), enc_sum(e_at, e_gd)
        proj_grad = enc_sum(e_xt, e_gp.reshape(rows, 4, -1)[:, :, : DD // 4].reshape(rows, DD))

    if not chip_plan:
        tokens_grad = trade(tokens_grad).astype(F32)
        dec_vec = jnp.concatenate(
            [
                vg_a, vg_b, vg_c, vg_d, vs_a, vs_b, vs_c, vs_d,
                vb_sqkv, vb_so, vb_cq, vb_ckv, vb_co, vb_up, vb_down,
            ],
            axis=1,
        )[0]
        empty = jnp.zeros_like(dec_vec)
        enc_parts = [ug_1, ug_2, ub_qkv, ub_out, ub_up, ub_down, us_1, us_2, ub_proj]
        enc_vec, dec_one, dec_two = lax.psum(
            (
                jnp.concatenate(enc_parts, axis=1)[0],
                jnp.where(view_id == 0, dec_vec, empty),
                jnp.where(view_id == 0, empty, dec_vec),
            ),
            ("pair", "view"),
        )
        dec_vec = jnp.where(view_id == 0, dec_one, dec_two)
        enc_gains_grad, enc_biases_grad = enc_vec[: 2 * DE], enc_vec[2 * DE :]
        gain_all, bias_all = dec_vec[: 4 * DD], dec_vec[4 * DD :]
        gain_part, bias_part = gain_all.shape[0] // 2, bias_all.shape[0] // 2
        dec_gains_grad = lax.dynamic_slice_in_dim(gain_all, half_id * gain_part, gain_part, 0)
        dec_biases_grad = lax.dynamic_slice_in_dim(bias_all, half_id * bias_part, bias_part, 0)
    return (
        mixed[None],
        tokens_grad[None],
        enc_qkv_grad,
        enc_out_grad,
        enc_up_grad,
        enc_down_grad,
        enc_gains_grad,
        enc_biases_grad,
        proj_grad,
        dec_in_grad,
        dec_outs_grad,
        dec_down_grad,
        dec_gains_grad,
        dec_biases_grad,
    )


def solution(mesh):
    both = P("pair", "view")
    return jax.shard_map(
        local,
        mesh=mesh,
        in_specs=(
            P("pair", "view", None),
            P("pair", "view", None),
            both,
            P(None, "pair", None),
            P(),
            P(),
            P(),
            P(),
            P(),
            P(),
            P(),
            P(None, "view"),
            P(None, "view"),
            P(None, "view"),
            P("view"),
            P("view"),
        ),
        out_specs=(
            P("pair", "view", None),
            P("pair", "view", None),
            both,
            both,
            both,
            both,
            P(),
            P(),
            both,
            both,
            both,
            both,
            P("view"),
            P("view"),
        ),
        check_vma=False,
    )
```

```python
from functools import partial

import jax
import jax.numpy as jnp
from jax import lax
from jax.experimental import pallas as pl
from jax.experimental.pallas import tpu as pltpu
from jax.sharding import PartitionSpec as P

DE = 1024
HE = 16
FE = 4096
DD = 768
HD = 12
FD = 3072

norm_eps = 1e-06
BF = jnp.bfloat16
F32 = jnp.float32
VMEM = 58 * 1024 * 1024

NN = (((1,), (0,)), ((), ()))
NT = (((1,), (1,)), ((), ()))
TN = (((0,), (0,)), ((), ()))


def mm(a, b, dims=NN):
    return lax.dot_general(a, b, dims, preferred_element_type=F32)


def full(shape):
    zeros = (0,) * len(shape)
    return pl.BlockSpec(shape, lambda *_: zeros)


def sds(shape, dtype):
    return jax.ShapeDtypeStruct(shape, dtype)


MESH = pl.DeviceIdType.MESH


def across(axis, bit):
    here = lax.axis_index(axis)
    return {axis: here + bit - 2 * bit * ((here // bit) % 2)}


def greet(devices):
    barrier = pltpu.get_barrier_semaphore()
    for device in devices:
        pl.semaphore_signal(barrier, inc=1, device_id=device, device_id_type=MESH)
    pl.semaphore_wait(barrier, len(devices))


def slanted():
    return {**across("pair", 1), **across("view", 1)}


def stays():
    return lax.axis_index("pair") % 2 == lax.axis_index("view") % 2


def part(ref, index):
    if not index:
        return ref
    return ref.at[
        tuple(pl.ds(i.start, i.stop - i.start) if isinstance(i, slice) and i.stop else i for i in index)
    ]


def carry(body, name, number, ride, mirror, grid, in_specs, out_specs, out_shape, args, scratch):
    landing, moves = [], []
    for k, (array, indices, axis, bit) in enumerate(ride):
        shape = jax.eval_shape(lambda a, i=indices[0]: a[i], array).shape if indices[0] else array.shape
        landing.append(sds((len(indices), *shape), array.dtype))
        moves += [(k, place, index, axis, bit) for place, index in enumerate(indices)]
    partners = {(axis, bit) for _, _, axis, bit in ride}
    if mirror:
        partners.add(("pair", 1))
    partners = sorted(partners)
    landing += [out_shape[k] for k, _ in mirror]
    n_in, n_out, n_ride, n_mirror = len(in_specs), len(out_specs), len(ride), len(mirror)
    n_scratch = len(scratch)
    traded = [array for array, _, axis, _ in ride if axis == "trade"]
    n_trade = len(traded)
    last = grid[0] - 1

    def plain(spec):
        return pl.BlockSpec(spec.block_shape, lambda j, index=spec.index_map: index(j, None))

    def shell(*refs):
        ins, refs = refs[:n_in], refs[n_in:]
        sources, refs = refs[:n_ride], refs[n_ride:]
        outs, refs = refs[:n_out], refs[n_out:]
        targets, refs = refs[:n_ride], refs[n_ride:]
        fars, refs = refs[:n_mirror], refs[n_mirror:]
        rest, refs = refs[:n_scratch], refs[n_scratch:]
        held, refs = refs[:n_mirror], refs[n_mirror:]
        bounce, refs = refs[:n_trade], refs[n_trade:]
        sems = list(refs)
        j = pl.program_id(0)

        def device(axis, bit):
            return slanted() if axis == "trade" else across(axis, bit)

        def remote(source, target, send, recv, to):
            return pltpu.make_async_remote_copy(
                src_ref=source, dst_ref=target, send_sem=send, recv_sem=recv, device_id=to,
                device_id_type=MESH,
            )

        def rides(act):
            for m, (k, place, index, axis, bit) in enumerate(moves):
                source, target = part(sources[k], index), targets[k].at[place]
                send, recv = sems[0].at[m], sems[1].at[m]
                copy = remote(source, target, send, recv, device(axis, bit))
                if axis == "trade":
                    pl.when(jnp.logical_not(stays()))(lambda copy=copy: act(copy))
                else:
                    act(copy)

        def keeps(out):
            found = [m for m, (_, _, _, axis, _) in enumerate(moves) if axis == "trade"]
            for i, m in enumerate(found):
                if out:
                    yield pltpu.make_async_copy(bounce[i], targets[moves[m][0]].at[0], sems[0].at[m])
                else:
                    yield pltpu.make_async_copy(sources[moves[m][0]], bounce[i], sems[1].at[m])

        def mirrored(m, n, index):
            send, recv = sems[2 * (m + 1)].at[n], sems[2 * (m + 1) + 1].at[n]
            return remote(part(held[m], index), part(fars[m], index), send, recv, across("pair", 1))

        @pl.when(j == 0)
        def _():
            greet([device(axis, bit) for axis, bit in partners])
            rides(lambda copy: copy.start())
            if traded:

                @pl.when(stays())
                def _():
                    for copy in keeps(False):
                        copy.start()

        if traded:

            @pl.when((j == 1) & stays())
            def _():
                for copy in keeps(False):
                    copy.wait()
                for copy in keeps(True):
                    copy.start()

        body((lax.axis_index("view") % 2, lax.axis_index("pair") % 2), *ins, *outs, *rest)

        for m, (k, steps) in enumerate(mirror):
            for n, (step, index) in enumerate(steps):

                @pl.when(j == step)
                def _(m=m, n=n, k=k, index=index):
                    part(held[m], index)[...] = outs[k][...]
                    mirrored(m, n, index).start()

        @pl.when(j == last)
        def _():
            for m, (_, steps) in enumerate(mirror):
                for n, (_, index) in enumerate(steps):
                    mirrored(m, n, index).wait()
            rides(lambda copy: copy.wait())
            if traded:

                @pl.when(stays())
                def _():
                    for copy in keeps(True):
                        copy.wait()

    hbm = pl.BlockSpec(memory_space=pl.ANY)
    dma = pltpu.SemaphoreType.DMA
    counts = [max(1, len(moves))] + [len(steps) for _, steps in mirror]
    return pl.pallas_call(
        shell,
        grid=grid,
        in_specs=[plain(spec) for spec in in_specs] + [hbm] * n_ride,
        out_specs=[plain(spec) for spec in out_specs] + [hbm] * (n_ride + n_mirror),
        out_shape=list(out_shape) + landing,
        scratch_shapes=list(scratch)
        + [pltpu.VMEM(out_shape[k].shape, out_shape[k].dtype) for k, _ in mirror]
        + [pltpu.VMEM(array.shape, array.dtype) for array in traded]
        + [dma((count,)) for count in counts for _ in range(2)],
        name=name,
        compiler_params=pltpu.CompilerParams(
            vmem_limit_bytes=VMEM, collective_id=number, has_side_effects=True
        ),
        cost_estimate=cost(name),
    )(*args, *(array for array, *_ in ride))


def call(
    body, name, half, grid, in_specs, out_specs, out_shape, args, scratch=(), flops=0, nbytes=0,
    ride=(), number=0, mirror=(),
):
    if number:
        return carry(body, name, number, ride, mirror, grid, in_specs, out_specs, out_shape, args, scratch)
    return pl.pallas_call(
        body,
        grid_spec=pltpu.PrefetchScalarGridSpec(
            num_scalar_prefetch=1,
            grid=grid,
            in_specs=in_specs,
            out_specs=out_specs,
            scratch_shapes=list(scratch),
        ),
        out_shape=out_shape,
        name=name,
        compiler_params=pltpu.CompilerParams(vmem_limit_bytes=VMEM),
        cost_estimate=cost(name),
    )(half, *args)


SCALE = 0.2e9

TIMES = {
    "enc_qkv": 8, "enc_attend": 19, "enc_ffn": 20, "dec_qkv": 8, "self_attend": 15, "dec_mid": 5,
    "dec_ckv": 7, "cross_attend": 15, "dec_ffn": 15, "dec_ffn_back": 13, "cross_back": 15,
    "mid_back": 5, "ckv_back": 7, "self_back": 15, "qkv_back": 10, "proj_back": 4,
    "enc_ffn_back": 18, "enc_back": 18, "enc_qkv_back": 11, "dw_dec_down": 6, "dw_dec_up": 6,
    "dw_co": 4, "dw_cq": 4, "dw_ckv": 4, "dw_so": 4, "dw_sqkv": 6, "dw_enc_down": 8, "dw_proj": 5,
    "dw_enc_up": 8, "dw_out": 5, "dw_enc_qkv": 7,
}


def cost(name):
    flops = int(TIMES[name] * SCALE)
    return pl.CostEstimate(flops=flops, bytes_accessed=0, transcendentals=0)


class Row:
    def __init__(self, array, start, size):
        self.array, self.start, self.size = array, start, size

    @property
    def spec(self):
        return full(self.array.shape)

    def get(self, ref):
        return ref[:, self.start : self.start + self.size]

    def block(self, ref, j, bn):
        return ref[:, pl.ds(pl.multiple_of(self.start + j * bn, 128), bn)]


class Whole:
    def __init__(self, array):
        self.arrays, self.columns = [array], array.shape[1]
        self.rows = array.shape[0]

    def blocks(self, bn, fixed=False):
        return [pl.BlockSpec((self.rows, bn), lambda j, h: (0, j))]

    def whole(self, bn=None):
        if bn is None:
            return [full(self.arrays[0].shape)]
        return [pl.BlockSpec((bn, self.columns), lambda j, h: (j, 0))]

    def read(self, refs, h, j, bn):
        return refs[0][...]

    def read_whole(self, refs, h):
        return refs[0][...]


class Halves:
    def __init__(self, own, far, width):
        self.arrays = [own[0], far[0]]
        self.starts, self.width = (own[1], far[1]), width
        self.rows, self.columns = own[0].shape[0], 2 * width

    def blocks(self, bn, fixed=False):
        per = self.width // bn
        specs = []
        for which, start in enumerate(self.starts):

            def index(j, h, which=which, start=start):
                if fixed:
                    return 0, start // bn + j % per
                half = h[0] ^ which
                hold = jnp.where(half == 0, per - 1, 0)
                return 0, start // bn + jnp.where(j // per == half, j % per, hold)

            specs.append(pl.BlockSpec((self.rows, bn), index))
        return specs

    def whole(self, bn=None):
        specs = []
        for start in self.starts:
            col = start // self.width
            if bn is None:
                specs.append(pl.BlockSpec((self.rows, self.width), lambda j, h, col=col: (0, col)))
            else:
                specs.append(pl.BlockSpec((bn, self.width), lambda j, h, col=col: (j, col)))
        return specs

    def read(self, refs, h, j, bn):
        return jnp.where(j // (self.width // bn) == h[0], refs[0][...], refs[1][...])

    def read_whole(self, refs, h):
        own, far = refs[0][...], refs[1][...]
        first = h[0] == 0
        return jnp.concatenate([jnp.where(first, own, far), jnp.where(first, far, own)], axis=1)


def norm_parts(x):
    centred = x - jnp.mean(x, axis=-1, keepdims=True)
    rstd = lax.rsqrt(jnp.mean(centred * centred, axis=-1, keepdims=True) + norm_eps)
    return centred * rstd, rstd


def norm_back(dy, x, gain):
    xhat, rstd = norm_parts(x)
    dgain = jnp.sum(dy * xhat, axis=0, keepdims=True)
    dshift = jnp.sum(dy, axis=0, keepdims=True)
    dxh = dy * gain
    mean_one = jnp.mean(dxh, axis=-1, keepdims=True)
    mean_two = jnp.mean(dxh * xhat, axis=-1, keepdims=True)
    return rstd * (dxh - mean_one - xhat * mean_two), dgain, dshift


def turn(u, cos, sin):
    lane = lax.broadcasted_iota(jnp.int32, u.shape, 1)
    other = jnp.where(lane % 32 < 16, pltpu.roll(u, 112, 1), pltpu.roll(u, 16, 1))
    return u * cos + other * sin


def turn_cols(y, cos, sin):
    return jnp.concatenate(
        [turn(y[:, i : i + 128], cos, sin) for i in range(0, y.shape[1], 128)], axis=1
    )


def gelu_parts(u):
    z = jnp.abs(u) * 0.7071067811865476
    t = 1.0 / (1.0 + 0.3275911 * z)
    e = jnp.exp(-0.5 * u * u)
    poly = t * (
        0.254829592
        + t * (-0.284496736 + t * (1.421413741 + t * (-1.453152027 + t * 1.061405429)))
    )
    tail = 0.5 * poly * e
    phi = jnp.where(u >= 0, 1.0 - tail, tail)
    return u * phi, phi + u * e * 0.3989422804014327


def col_sum(g):
    return jnp.sum(g.astype(F32), axis=0, keepdims=True)


def deal(h, tall, mine, theirs, at=None):
    rb = mine.shape[1]
    for s in range(tall.shape[0] // (2 * rb)):
        even, odd = tall[2 * s * rb : (2 * s + 1) * rb], tall[(2 * s + 1) * rb : (2 * s + 2) * rb]
        first = h[1] == 0
        mine[s] = jnp.where(first, even, odd)
        theirs[s] = jnp.where(first, odd, even)


def dealt(width, rows):
    return [sds((4, width // 8, rows), BF)] * 2


def columns_at(i, bn):
    return slice(None), slice(i * bn, i * bn + bn)


def lnproj(half, x, gain, shift, w, b, cos, sin, n_q, n_turn, n_all, name, ride=(), number=0):
    rows, width = x.shape
    bn = w.columns // n_all
    n_w = len(w.arrays)
    has_q = n_q > 0

    def body(h, x_ref, g_ref, s_ref, b_ref, c_ref, sn_ref, *rest):
        w_refs, rest = rest[:n_w], rest[n_w:]
        if has_q:
            q_ref, kv_ref, mine, theirs, nrm = rest
        else:
            kv_ref, mine, theirs, nrm = rest
        j = pl.program_id(0)

        @pl.when(j == 0)
        def _():
            xhat, _ = norm_parts(x_ref[...].astype(F32))
            low = (xhat * gain.get(g_ref) + shift.get(s_ref)).astype(BF)
            nrm[...] = low
            deal(h, low.T, mine, theirs)

        y = mm(nrm[...], w.read(w_refs, h, j, bn)) + b.block(b_ref, j, bn)

        @pl.when(j < n_turn)
        def _():
            out = turn_cols(y, c_ref[...], sn_ref[...]).astype(BF)
            if has_q:

                @pl.when(j < n_q)
                def _():
                    q_ref[...] = out

                @pl.when(j >= n_q)
                def _():
                    kv_ref[...] = out

            else:
                kv_ref[...] = out

        @pl.when(j >= n_turn)
        def _():
            kv_ref[...] = y.astype(BF)

    outs = [
        sds((rows, bn * (n_all - n_q)), BF),
        *dealt(width, rows),
    ]
    specs = [
        pl.BlockSpec((rows, bn), lambda j, h: (0, jnp.maximum(j - n_q, 0))),
        full((4, width // 8, rows)),
        full((4, width // 8, rows)),
    ]
    if has_q:
        outs.insert(0, sds((rows, bn * n_q), BF))
        specs.insert(0, pl.BlockSpec((rows, bn), lambda j, h: (0, jnp.minimum(j, n_q - 1))))
    return call(
        body,
        name,
        half,
        (n_all,),
        [
            full((rows, width)),
            gain.spec,
            shift.spec,
            b.spec,
            full((rows, 128)),
            full((rows, 128)),
        ]
        + w.blocks(bn, number > 0),
        specs,
        outs,
        (x, gain.array, shift.array, b.array, cos, sin, *w.arrays),
        [pltpu.VMEM((rows, width), BF)],
        ride=ride,
        number=number,
        mirror=[(1 if has_q else 0, [(n_q + i, columns_at(i, bn)) for i in range(n_all - n_q)])],
    )


def two_heads(block):
    first = lax.broadcasted_iota(jnp.int32, block.shape, 1) < 64
    zero = jnp.zeros_like(block)
    return jnp.concatenate(
        [jnp.where(first, block, zero), jnp.where(first, zero, block)], axis=0
    )


def pick_heads(tall, rows):
    return jnp.concatenate([tall[:64, :rows], tall[64:, rows:]], axis=0)


def attend(half, q, kv, kvf, name, ride=(), number=0):
    rows, width = q.shape
    pairs = width // 128
    keys = 2 * rows

    def body(h, q_ref, ko_ref, vo_ref, kf_ref, vf_ref, p_ref, o_ref, mine, theirs, tall):
        q2 = two_heads(q_ref[...] * jnp.asarray(0.125, BF))
        k = jnp.concatenate([ko_ref[...], kf_ref[...]], axis=0)
        v = jnp.concatenate([vo_ref[...], vf_ref[...]], axis=0)
        vt = v.T
        pieces = []
        for c in range(0, 2 * rows, 256):
            s = mm(k, q2[c : c + 256], NT)
            e = jnp.exp(s - jnp.max(s, axis=0, keepdims=True))
            p = (e * (1.0 / jnp.sum(e, axis=0, keepdims=True))).astype(BF)
            p_ref[0, :, c : c + 256] = p
            pieces.append(mm(vt, p))
        t = pick_heads(jnp.concatenate(pieces, axis=1), rows)
        j = pl.program_id(0)
        tall[pl.ds(pl.multiple_of(j * 128, 128), 128), :] = t.astype(BF)
        o_ref[...] = t.T.astype(BF)

        @pl.when(j == pairs - 1)
        def _():
            deal(h, tall[...], mine, theirs)

    col = lambda j, h: (0, j)
    val = lambda j, h: (0, pairs + j)
    return call(
        body,
        name,
        half,
        (pairs,),
        [
            pl.BlockSpec((rows, 128), col),
            pl.BlockSpec((rows, 128), col),
            pl.BlockSpec((rows, 128), val),
            pl.BlockSpec((rows, 128), col),
            pl.BlockSpec((rows, 128), val),
        ],
        [
            pl.BlockSpec((1, keys, 2 * rows), lambda j, h: (j, 0, 0)),
            pl.BlockSpec((rows, 128), col),
            full((4, width // 8, rows)),
            full((4, width // 8, rows)),
        ],
        [
            sds((pairs, keys, 2 * rows), BF),
            sds((rows, width), BF),
            *dealt(width, rows),
        ],
        (q, kv, kv, kvf, kvf),
        [pltpu.VMEM((width, rows), BF)],
        ride=ride,
        number=number,
    )


def attend_back(half, q, kv, kvf, p, o, do, cos, sin, cos_all, sin_all, name, ride=(), number=0):
    rows, width = q.shape
    pairs = width // 128
    keys = 2 * rows

    def body(
        h, q_ref, ko_ref, vo_ref, kf_ref, vf_ref, p_ref, o_ref, do_ref, c_ref, s_ref, ca_ref, sa_ref,
        own_ref, ship_ref,
    ):
        q2 = two_heads(q_ref[...] * jnp.asarray(0.125, BF))
        k = jnp.concatenate([ko_ref[...], kf_ref[...]], axis=0)
        v = jnp.concatenate([vo_ref[...], vf_ref[...]], axis=0)
        kt = k.T
        do_low = do_ref[...]
        do2 = two_heads(do_low)
        prod = two_heads(do_low.astype(F32) * o_ref[...].astype(F32))
        inner = lax.dot_general(
            jnp.ones((8, 128), F32), prod, NT, precision=lax.Precision.HIGHEST,
            preferred_element_type=F32,
        )[:1]
        dk = jnp.zeros((keys, 128), F32)
        dv = jnp.zeros((keys, 128), F32)
        pieces = []
        for c in range(0, 2 * rows, 256):
            dp = mm(v, do2[c : c + 256], NT)
            pc = p_ref[0, :, c : c + 256]
            ds = (pc.astype(F32) * (dp - inner[:, c : c + 256])).astype(BF)
            dk += mm(ds, q2[c : c + 256])
            dv += mm(pc, do2[c : c + 256])
            pieces.append(mm(kt, ds))
        dq = pick_heads(jnp.concatenate(pieces, axis=1), rows).T * 0.125
        ship_ref[2] = turn(dq, c_ref[...], s_ref[...]).astype(BF)
        dk = turn(dk, ca_ref[...], sa_ref[...])
        own_ref[0] = dk[:rows]
        own_ref[1] = dv[:rows]
        ship_ref[0] = dk[rows:].astype(BF)
        ship_ref[1] = dv[rows:].astype(BF)

    col = lambda j, h: (0, j)
    val = lambda j, h: (0, pairs + j)
    return call(
        body,
        name,
        half,
        (pairs,),
        [
            pl.BlockSpec((rows, 128), col),
            pl.BlockSpec((rows, 128), col),
            pl.BlockSpec((rows, 128), val),
            pl.BlockSpec((rows, 128), col),
            pl.BlockSpec((rows, 128), val),
            pl.BlockSpec((1, keys, 2 * rows), lambda j, h: (j, 0, 0)),
            pl.BlockSpec((rows, 128), col),
            pl.BlockSpec((rows, 128), col),
            full((rows, 128)),
            full((rows, 128)),
            full((keys, 128)),
            full((keys, 128)),
        ],
        [
            pl.BlockSpec((2, rows, 128), lambda j, h: (0, 0, j)),
            pl.BlockSpec((3, rows, 128), lambda j, h: (0, 0, j)),
        ],
        [sds((2, rows, width), F32), sds((3, rows, width), BF)],
        (q, kv, kv, kvf, kvf, p, o, do, cos, sin, cos_all, sin_all),
        (),
        ride=ride,
        number=number,
        mirror=[(1, [(i, (slice(None), *columns_at(i, 128))) for i in range(pairs)])],
    )


def ffn_forward(half, o, resid, wo, bo, gain, shift, w_up, b_up, w_down, b_down, head, bn, name):
    rows, width = o.shape
    hidden = w_up.columns
    steps = hidden // bn
    n_w = len(wo.arrays)

    def body(h, o_ref, r_ref, bo_ref, g_ref, s_ref, bu_ref, bd_ref, *rest):
        wo_refs, up_refs, dn_refs, rest = rest[:n_w], rest[n_w : 2 * n_w], rest[2 * n_w : 3 * n_w], rest[3 * n_w :]
        if head:
            pj_ref, bp_ref, x1_ref, n_mine, n_theirs, a_mine, a_theirs, gp_ref, z_ref, *rest = rest
            x_mine, x_theirs, nrm, acc = rest
        else:
            x1_ref, n_mine, n_theirs, a_mine, a_theirs, gp_ref, z_ref, nrm, acc = rest
        j = pl.program_id(0)

        @pl.when(j == 0)
        def _():
            x1 = r_ref[...].astype(F32) + mm(o_ref[...], wo.read_whole(wo_refs, h)) + bo.get(bo_ref)
            x1_ref[...] = x1
            xhat, _ = norm_parts(x1)
            low = (xhat * gain.get(g_ref) + shift.get(s_ref)).astype(BF)
            nrm[...] = low
            deal(h, low.T, n_mine, n_theirs)
            acc[...] = x1 + b_down.get(bd_ref)

        u = mm(nrm[...], w_up.read(up_refs, h, j, bn)) + b_up.block(bu_ref, j, bn)
        act, slope = gelu_parts(u)
        act = act.astype(BF)
        gp_ref[...] = slope.astype(BF)
        deal(h, act.T, a_mine, a_theirs)
        acc[...] += mm(act, w_down.read_whole(dn_refs, h))

        @pl.when(j == steps - 1)
        def _():
            low = acc[...].astype(BF)
            if head:
                deal(h, low.T, x_mine, x_theirs)
                z_ref[...] = (mm(low, pj_ref[...]) + head[1].get(bp_ref)).astype(BF)
            else:
                z_ref[...] = low

    whole = full((rows, width))
    in_specs = (
        [whole, whole, bo.spec, gain.spec, shift.spec, b_up.spec, b_down.spec]
        + wo.whole()
        + w_up.blocks(bn)
        + w_down.whole(bn)
    )
    out_specs = [
        whole,
        full((4, width // 8, rows)),
        full((4, width // 8, rows)),
        pl.BlockSpec((bn * 4 // hidden, hidden // 8, rows), lambda j, h: (j, 0, 0)),
        pl.BlockSpec((bn * 4 // hidden, hidden // 8, rows), lambda j, h: (j, 0, 0)),
        pl.BlockSpec((rows, bn), lambda j, h: (0, j)),
    ]
    outs = [
        sds((rows, width), F32),
        *dealt(width, rows),
        *dealt(hidden, rows),
        sds((rows, hidden), BF),
    ]
    vectors = [row.array for row in (bo, gain, shift, b_up, b_down)]
    args = [o, resid, *vectors, *wo.arrays, *w_up.arrays, *w_down.arrays]
    if head:
        wide = head[0].shape[1]
        in_specs += [full((width, wide)), head[1].spec]
        args += [head[0], head[1].array]
        out_specs += [full((rows, wide)), full((4, width // 8, rows)), full((4, width // 8, rows))]
        outs += [sds((rows, wide), BF), *dealt(width, rows)]
    else:
        out_specs += [whole]
        outs += [sds((rows, width), BF)]
    return call(
        body,
        name,
        half,
        (steps,),
        in_specs,
        out_specs,
        outs,
        args,
        [pltpu.VMEM((rows, width), BF), pltpu.VMEM((rows, width), F32)],
        4 * rows * width * hidden + 2 * rows * width * width,
        4 * width * hidden + 4 * rows * hidden,
    )


def head_backward(half, grad, returned, proj, name, number):
    rows, wide = grad.shape
    width = proj.shape[0]

    part = wide // 4
    slot = -(-part // 128) * 128

    def body(h, g_ref, r_ref, s_ref, w_ref, low_ref, b_ref, gx_ref, gd_ref):
        back = jnp.concatenate([r_ref[...], s_ref[...]], axis=0)
        low = (g_ref[...] + back.astype(F32)).astype(BF)
        pad = jnp.zeros((rows, slot - part), BF)
        for t in range(4):
            piece = low[:, t * part : (t + 1) * part]
            low_ref[:, t * slot : (t + 1) * slot] = jnp.concatenate([piece, pad], axis=1)
        b_ref[...] = col_sum(low)
        gx = mm(low, w_ref[...], NT)
        gx_ref[...] = gx
        gd_ref[...] = gx.astype(BF)

    inside, outside = full((rows, wide)), full((rows, width))
    return call(
        body,
        name,
        half,
        (1,),
        [inside, full(returned[0].shape), full(returned[1].shape), full((width, wide))],
        [full((rows, 4 * slot)), full((1, wide)), outside, outside],
        [sds((rows, 4 * slot), BF), sds((1, wide), F32), sds((rows, width), F32), sds((rows, width), BF)],
        (grad, *returned, proj),
        number=number,
        mirror=[(0, [(0, ())]), (3, [(0, ())])],
    )


def ffn_backward(half, gd, base, w_down, slope, w_up, x, gain, wo, bn, name, ride=(), number=0):
    rows, width = x.shape
    hidden = w_up.columns
    steps = hidden // bn
    n_w = len(wo.arrays)
    has_base = base is not None

    def body(h, gd_ref, gp_ref, x_ref, g_ref, *refs):
        wo_refs, up_refs, dn_refs, refs = refs[:n_w], refs[n_w : 2 * n_w], refs[2 * n_w : 3 * n_w], refs[3 * n_w :]
        if has_base:
            base_ref, *refs = refs
        gu_ref, go_ref, gx_ref, do_ref, bd_ref, bu_ref, dg_ref, ds_ref, bo_ref, acc = refs
        j = pl.program_id(0)

        @pl.when(j == 0)
        def _():
            bd_ref[...] = col_sum(gd_ref[...])
            acc[...] = jnp.zeros_like(acc)

        da = mm(gd_ref[...], w_down.read_whole(dn_refs, h), NT)
        gu = (da * gp_ref[...].astype(F32)).astype(BF)
        gu_ref[...] = gu
        bu_ref[...] = col_sum(gu)
        acc[...] += mm(gu, w_up.read(up_refs, h, j, bn), NT)

        @pl.when(j == steps - 1)
        def _():
            dx, dg, ds = norm_back(acc[...], x_ref[...], gain.get(g_ref))
            dg_ref[...] = dg
            ds_ref[...] = ds
            total = (base_ref[...] if has_base else gd_ref[...].astype(F32)) + dx
            gx_ref[...] = total
            go = total.astype(BF)
            go_ref[...] = go
            bo_ref[...] = col_sum(go)
            do_ref[...] = mm(go, wo.read_whole(wo_refs, h), NT).astype(BF)

    vec, whole = full((1, width)), full((rows, width))
    row = sds((1, width), F32)
    return call(
        body,
        name,
        half,
        (steps,),
        [whole, pl.BlockSpec((rows, bn), lambda j, h: (0, j)), whole, gain.spec]
        + wo.whole()
        + w_up.blocks(bn, number > 0)
        + w_down.whole(bn)
        + ([whole] if has_base else []),
        [
            pl.BlockSpec((rows, bn), lambda j, h: (0, j)),
            whole,
            whole,
            whole,
            vec,
            pl.BlockSpec((1, bn), lambda j, h: (0, j)),
            vec,
            vec,
            vec,
        ],
        [
            sds((rows, hidden), BF),
            sds((rows, width), BF),
            sds((rows, width), F32),
            sds((rows, width), BF),
            row,
            sds((1, hidden), F32),
            row,
            row,
            row,
        ],
        [gd, slope, x, gain.array, *wo.arrays, *w_up.arrays, *w_down.arrays] + ([base] if has_base else []),
        [pltpu.VMEM((rows, width), F32)],
        ride=ride,
        number=number,
        mirror=[(0, [(i, columns_at(i, bn)) for i in range(steps)])],
    )


def mid_forward(half, o, resid, wo, bo, gain, shift, w, b, cos, sin, name):
    rows, width = o.shape

    def body(
        h, o_ref, r_ref, bo_ref, g_ref, s_ref, b_ref, c_ref, sn_ref, wo_own, wo_far, w_own, w_far,
        y_ref, q_ref, mine, theirs,
    ):
        y = r_ref[...].astype(F32) + mm(o_ref[...], wo.read_whole((wo_own, wo_far), h)) + bo.get(bo_ref)
        y_ref[...] = y
        xhat, _ = norm_parts(y)
        low = (xhat * gain.get(g_ref) + shift.get(s_ref)).astype(BF)
        deal(h, low.T, mine, theirs)
        q = mm(low, w.read_whole((w_own, w_far), h)) + b.get(b_ref)
        q_ref[...] = turn_cols(q, c_ref[...], sn_ref[...]).astype(BF)

    whole, table = full((rows, width)), full((rows, 128))
    return call(
        body,
        name,
        half,
        (1,),
        [whole, whole, bo.spec, gain.spec, shift.spec, b.spec, table, table] + wo.whole() + w.whole(),
        [whole, whole, full((4, width // 8, rows)), full((4, width // 8, rows))],
        [sds((rows, width), F32), sds((rows, width), BF), *dealt(width, rows)],
        (o, resid, bo.array, gain.array, shift.array, b.array, cos, sin, *wo.arrays, *w.arrays),
        (),
        4 * rows * width * width,
        4 * width * width,
    )


def mid_backward(half, gq, w, x, gain, above, wo, name, ride=(), number=0):
    rows, width = x.shape

    def body(
        h, gq_ref, x_ref, g_ref, a_ref, w_own, w_far, wo_own, wo_far,
        gx_ref, go_ref, do_ref, bq_ref, dg_ref, ds_ref, bo_ref,
    ):
        low = gq_ref[0]
        bq_ref[...] = col_sum(low)
        dx, dg, ds = norm_back(mm(low, w.read_whole((w_own, w_far), h), NT), x_ref[...], gain.get(g_ref))
        dg_ref[...] = dg
        ds_ref[...] = ds
        total = a_ref[...] + dx
        gx_ref[...] = total
        go = total.astype(BF)
        go_ref[...] = go
        bo_ref[...] = col_sum(go)
        do_ref[...] = mm(go, wo.read_whole((wo_own, wo_far), h), NT).astype(BF)

    whole, vec = full((rows, width)), full((1, width))
    row = sds((1, width), F32)
    return call(
        body,
        name,
        half,
        (1,),
        [pl.BlockSpec((1, rows, width), lambda j, h: (2, 0, 0)), whole, gain.spec, whole]
        + w.whole()
        + wo.whole(),
        [whole, whole, whole, vec, vec, vec, vec],
        [sds((rows, width), F32), sds((rows, width), BF), sds((rows, width), BF), row, row, row, row],
        (gq, x, gain.array, above, *w.arrays, *wo.arrays),
        ride=ride,
        number=number,
    )


def proj_backward(half, gq, own, back, w, x, gain, above, bn, name, ride=(), number=0):
    rows, width = x.shape
    steps, per = w.columns // bn, width // bn
    has_q, has_above = gq is not None, above is not None
    n_w = len(w.arrays)
    skip = per if has_q else 0

    def body(h, *refs):
        if has_q:
            gq_ref, *refs = refs
        own_ref, back_ref, x_ref, g_ref, *refs = refs
        w_refs, refs = refs[:n_w], refs[n_w:]
        if has_above:
            a_ref, *refs = refs
        g_out, b_ref, gx_ref, dg_ref, ds_ref, acc = refs
        j = pl.program_id(0)
        low = (own_ref[0] + back_ref[0].astype(F32)).astype(BF)
        if has_q:
            low = jnp.where(j < per, gq_ref[0], low)
        g_out[...] = low
        b_ref[...] = col_sum(low)
        piece = mm(low, w.read(w_refs, h, j, bn), NT)

        @pl.when(j == 0)
        def _():
            acc[...] = piece

        @pl.when(j > 0)
        def _():
            acc[...] += piece

        @pl.when(j == steps - 1)
        def _():
            dx, dg, ds = norm_back(acc[...], x_ref[...].astype(F32), gain.get(g_ref))
            dg_ref[...] = dg
            ds_ref[...] = ds
            gx_ref[...] = (a_ref[...] + dx if has_above else dx).astype(gx_ref.dtype)

    whole, vec = full((rows, width)), full((1, width))

    def part_index(j, h):
        i = jnp.maximum(j - skip, 0)
        return i // per, 0, i % per

    part = pl.BlockSpec((1, rows, bn), part_index)
    in_specs = [part, part, whole, gain.spec] + w.blocks(bn, number > 0)
    args = [own, back, x, gain.array, *w.arrays]
    if has_q:
        in_specs.insert(0, pl.BlockSpec((1, rows, bn), lambda j, h: (2, 0, jnp.minimum(j, per - 1))))
        args.insert(0, gq)
    if has_above:
        in_specs.append(whole)
        args.append(above)
    row = sds((1, width), F32)
    return call(
        body,
        name,
        half,
        (steps,),
        in_specs,
        [
            pl.BlockSpec((rows, bn), lambda j, h: (0, j)),
            pl.BlockSpec((1, bn), lambda j, h: (0, j)),
            whole,
            vec,
            vec,
        ],
        [
            sds((rows, w.columns), BF),
            sds((1, w.columns), F32),
            sds((rows, width), F32 if has_above and n_w == 2 else BF),
            row,
            row,
        ],
        args,
        [pltpu.VMEM((rows, width), F32)],
        ride=ride,
        number=number,
        mirror=[(0, [(i, columns_at(i, bn)) for i in range(steps)])],
    )


def weight_blocks(place, mine, far, g, g_far, nz, width, bn, name, base=None, at=0, total=None):
    _, rb, rows = mine.shape
    per = width // bn
    units = bn // 128
    total = total or width // 128 * rb
    group = max(1, 512 // rb)

    def body(place_ref, a_ref, b_ref, g_ref, gf_ref, *rest):
        out, lhs = rest[-2:]

        @pl.when((pl.program_id(0) == 0) & (pl.program_id(1) == 0))
        def _():
            for s in range(4):
                lhs[s * rb : (s + 1) * rb, :rows] = a_ref[place_ref[nz + s]]
                lhs[s * rb : (s + 1) * rb, rows:] = b_ref[place_ref[nz + s]]

        grad = jnp.concatenate([g_ref[...].reshape(rows, bn), gf_ref[...].reshape(rows, bn)], axis=0)
        for c in range(0, 4, group):
            n = min(4 - c, group)
            y = mm(lhs[c * rb : (c + n) * rb, :], grad).astype(BF)
            for s in range(n):
                for u in range(units):
                    out[c + s, 0, u * rb : (u + 1) * rb, :] = y[
                        s * rb : (s + 1) * rb, u * 128 : (u + 1) * 128
                    ]

    if g.ndim == 3:
        columns = pl.BlockSpec((1, rows, bn), lambda i, j, z: (2, 0, z[i] * per + j))
    else:
        columns = pl.BlockSpec((rows, bn), lambda i, j, z: (0, z[i] * per + j))
    skip = at // (units * rb)
    in_specs = [full((4, rb, rows)), full((4, rb, rows)), columns, columns]
    args, aliases = [mine, far, g, g_far], {}
    if base is not None:
        in_specs.append(pl.BlockSpec(memory_space=pl.ANY))
        args.append(base)
        aliases[5] = 0
    return pl.pallas_call(
        body,
        grid_spec=pltpu.PrefetchScalarGridSpec(
            num_scalar_prefetch=1,
            grid=(nz, per),
            in_specs=in_specs,
            out_specs=pl.BlockSpec((4, 1, units * rb, 128), lambda i, j, z: (0, i, skip + j, 0)),
            scratch_shapes=[pltpu.VMEM((4 * rb, 2 * rows), BF)],
        ),
        out_shape=sds((4, nz, total, 128), BF),
        name=name,
        input_output_aliases=aliases,
        compiler_params=pltpu.CompilerParams(vmem_limit_bytes=VMEM),
        cost_estimate=cost(name),
    )(place, *args)


def swap(value, axis, distance):
    size = lax.axis_size(axis)
    return lax.ppermute(value, axis, [(i, i ^ distance) for i in range(size)])


def plus(a, b):
    return (a.astype(F32) + b.astype(F32)).astype(BF)


def chip_sum(blocks):
    groups = [[0, 2, 4, 6], [1, 3, 5, 7]]
    flat = blocks.reshape(-1, 128)
    out = lax.psum_scatter(flat, "pair", scatter_dimension=0, axis_index_groups=groups, tiled=True)
    return out.reshape(blocks.shape[1:])


STAY = ((0, 2), (0, 1))
AWAY = ((1, 3), (2, 3))
BITS = (2, 4)


def final_sums(mains, stacks, pairs, added, layout, shapes, vectors, traded):
    arrays, chunks, base = [array for array, _ in mains], [], 0
    for k, (array, parts) in enumerate(mains):
        chunks += [(k, row, count, order, base + row, array.shape[1]) for row, count, order in parts]
        base += array.shape[2]
    n, l_main = len(chunks), base
    l_stack = sum(array.shape[1] for array in stacks)
    l_pair = sum(array.shape[1] for array in pairs)
    n_arr, ns, np, na = len(arrays), len(stacks), len(pairs), len(added)
    enc_vectors, dec_vectors = vectors
    nv = len(enc_vectors) + len(dec_vectors)
    enc_count, dec_count = [sum(v.shape[1] for v in group) // 128 for group in vectors]
    vector_enc = -(-enc_count // 8) * 8
    rows = vector_enc + -(-dec_count // 8) * 8
    gain_rows, dec_gain = 2 * DE // 128, 4 * DD // 128
    dec_bias = dec_count - dec_gain
    ahead = 4

    def body(*refs):
        m_refs, refs = refs[:n_arr], refs[n_arr:]
        s_refs, refs = refs[:ns], refs[ns:]
        p_refs, refs = refs[:np], refs[np:]
        a_refs, refs = refs[: 2 * na], refs[2 * na :]
        v_refs, refs = refs[:nv], refs[nv:]
        t_ref, *refs = refs
        outs, refs = refs[: len(shapes)], refs[len(shapes) :]
        (
            gains_out, biases_out, dec_gains_out, dec_biases_out, t_out, v_out, t_keep, t_in, t_send, t_recv,
            keep, got1, got2, got3, got4, s_keep, s_got3, s_got4, p_keep, p_got, a_keep, v_got,
            in_sem, send1, recv1, send2, recv2, send3, recv3, send4, recv4,
            s_in, s_send, s_recv, p_in, p_send, p_recv, a_in, v_send, v_recv,
        ) = refs
        core, x, y = across("pair", 1), across("pair", 2), across("pair", 4)
        z1, z2 = across("view", 1), across("view", 2)
        axes = (x, y)
        greet((core, x, y, z1, z2, slanted()))
        t_local = pltpu.make_async_copy(t_ref, t_keep, t_in)
        t_remote = pltpu.make_async_remote_copy(
            src_ref=t_ref, dst_ref=t_keep, send_sem=t_send, recv_sem=t_recv, device_id=slanted(),
            device_id_type=MESH,
        )

        @pl.when(stays())
        def _():
            t_local.start()

        @pl.when(jnp.logical_not(stays()))
        def _():
            t_remote.start()

        sent = []

        def send(src, dst, send_sem, recv_sem, device, late=True):
            copy = pltpu.make_async_remote_copy(
                src_ref=src, dst_ref=dst, send_sem=send_sem, recv_sem=recv_sem,
                device_id=device, device_id_type=MESH,
            )
            copy.start()
            if late:
                sent.append(copy)
            return copy

        def fetch(src, dst, sem):
            copy = pltpu.make_async_copy(src, dst, sem)
            copy.start()
            return copy

        def at(i):
            return pl.ds(chunks[i][4], chunks[i][2])

        def store(places, total):
            row = 0
            for count, out, column in places:
                outs[out][:, column : column + 128] = total[row : row + count]
                row += count

        one, two, three, four, loads = {}, {}, {}, {}, {}

        def start_one(i):
            k, row, count, order, _, nz = chunks[i]
            one[i] = [
                send(
                    m_refs[k].at[slot, :, pl.ds(row, count), :], got1.at[q, pl.ds(0, nz), at(i), :],
                    send1.at[i, q], recv1.at[i, q], axes[order],
                )
                for q, slot in enumerate(AWAY[order])
            ]

        def start_load(i):
            k, row, count, order, _, nz = chunks[i]
            loads[i] = [
                fetch(
                    m_refs[k].at[slot, :, pl.ds(row, count), :], keep.at[q, pl.ds(0, nz), at(i), :],
                    in_sem.at[i, q],
                )
                for q, slot in enumerate(STAY[order])
            ]

        def start_two(i):
            device = axes[1 - chunks[i][3]]
            nz = pl.ds(0, chunks[i][5])
            two[i] = send(
                keep.at[1, nz, at(i), :], got2.at[nz, at(i), :], send2.at[i], recv2.at[i], device
            )

        def start_three(i):
            three[i] = [
                send(keep.at[0, slot, at(i), :], got3.at[q, at(i), :], send3.at[i, q], recv3.at[i, q], z1)
                for q, slot in enumerate((1, 3)[: chunks[i][5] // 2])
            ]

        def start_four(i):
            four[i] = send(keep.at[0, 2, at(i), :], got4.at[at(i), :], send4.at[i], recv4.at[i], z2)

        for i in range(min(ahead, n)):
            start_one(i)
        for i in range(n):
            start_load(i)
        v_out[...] = jnp.zeros_like(v_out)
        row = 0
        for k, ref in enumerate(v_refs):
            row = vector_enc if k == len(enc_vectors) else row
            for u in range(ref.shape[1] // 128):
                v_out[row : row + 1, :] = ref[:, u * 128 : (u + 1) * 128]
                row += 1
        v_axes = (core, x, y, z1, z2)

        def start_vector(r):
            count = vector_enc if r == 4 else rows
            return send(
                v_out.at[pl.ds(0, count), :], v_got.at[r, pl.ds(0, count), :],
                v_send.at[r], v_recv.at[r], v_axes[r], late=False,
            )

        flying = start_vector(0)
        offset, s_moves = 0, []
        for k, ref in enumerate(s_refs):
            size = ref.shape[1]
            where = pl.ds(offset, size)
            s_moves.append(
                (
                    [
                        send(ref.at[slot], s_got3.at[q, where, :], s_send.at[k, q], s_recv.at[k, q], z1)
                        for q, slot in enumerate((1, 3))
                    ],
                    [
                        fetch(ref.at[slot], s_keep.at[q, where, :], s_in.at[k, q])
                        for q, slot in enumerate((0, 2))
                    ],
                    where,
                )
            )
            offset += size
        offset, a_moves = 0, []
        for k in range(na):
            size = a_refs[2 * k].shape[1]
            where = pl.ds(offset, size)
            a_moves.append((fetch(a_refs[2 * k].at[0], a_keep.at[where, :], a_in.at[k]), where))
            offset += size
        offset, p_moves = 0, []
        for k, ref in enumerate(p_refs):
            where = pl.ds(offset, ref.shape[1])
            p_moves.append(
                (
                    send(ref.at[1], p_got.at[where, :], p_send.at[k], p_recv.at[k], z2),
                    fetch(ref.at[0], p_keep.at[where, :], p_in.at[k]),
                    where,
                )
            )
            offset += ref.shape[1]

        mark = n // 2
        s_last = []
        for i in range(n + 6):
            if i < n:
                for copy in loads[i]:
                    copy.wait()
                for copy in one[i]:
                    copy.wait_recv()
                nz = pl.ds(0, chunks[i][5])
                keep[:, nz, at(i), :] = keep[:, nz, at(i), :] + got1[:, nz, at(i), :]
                start_two(i)
                if i + ahead < n:
                    start_one(i + ahead)
            j = i - 2
            if 0 <= j < n:
                two[j].wait_recv()
                nz = pl.ds(0, chunks[j][5])
                keep[0, nz, at(j), :] = keep[0, nz, at(j), :] + got2[nz, at(j), :]
                start_three(j)
            if i == mark:
                for k, (moves, reads, where) in enumerate(s_moves):
                    for copy in reads:
                        copy.wait()
                    for copy in moves:
                        copy.wait_recv()
                    for q in range(2):
                        s_keep[q, where, :] = s_keep[q, where, :] + s_got3[q, where, :]
                    s_last.append(
                        send(s_keep.at[1, where, :], s_got4.at[where, :], s_send.at[k, 2], s_recv.at[k, 2], z2)
                    )
            j = i - 4
            if 0 <= j < n:
                for copy in three[j]:
                    copy.wait_recv()
                if chunks[j][5] == 4:
                    keep[0, 0, at(j), :] = keep[0, 0, at(j), :] + got3[0, at(j), :]
                    keep[0, 2, at(j), :] = keep[0, 2, at(j), :] + got3[1, at(j), :]
                    start_four(j)
            j = i - 6
            if 0 <= j < n:
                row = chunks[j][4]
                if chunks[j][5] == 4:
                    four[j].wait_recv()
                    last = got4[at(j), :]
                else:
                    last = got3[0, at(j), :]
                total = keep[0, 0, at(j), :].astype(F32) + last.astype(F32)
                done = 0
                for count, out, column in main_places:
                    if done >= row and done < row + chunks[j][2]:
                        outs[out][:, column : column + 128] = total[done - row : done - row + count]
                    done += count
            if i % 2 == 1 and i // 2 < 5:
                r = i // 2
                flying.wait()
                count = vector_enc if r == 4 else rows
                v_out[pl.ds(0, count), :] = v_out[pl.ds(0, count), :] + v_got[r, pl.ds(0, count), :]
                if r < 4:
                    flying = start_vector(r + 1)
            if i == n - 1:
                for k in range(na):
                    read, where = a_moves[k]
                    read.wait()
                    total = a_keep[where, :].astype(F32) + a_refs[2 * k + 1][...].astype(F32)
                    store(layout[len(mains) + ns + np + k], total)
                for k, (move, read, where) in enumerate(p_moves):
                    read.wait()
                    move.wait_recv()
                    total = p_keep[where, :].astype(F32) + p_got[where, :].astype(F32)
                    store(layout[len(mains) + ns + k], total)
            if i == n + 3:
                for k, (copy, (_, _, where)) in enumerate(zip(s_last, s_moves)):
                    copy.wait_recv()
                    total = s_keep[0, where, :].astype(F32) + s_got4[where, :].astype(F32)
                    store(layout[len(mains) + k], total)
        gains_out[...] = v_out[:gain_rows]
        biases_out[...] = v_out[gain_rows:enc_count]
        first = lax.axis_index("view") % 2 == 0
        for out, base, count in ((dec_gains_out, 0, dec_gain), (dec_biases_out, dec_gain, dec_bias)):
            start, half = vector_enc + base, count // 2
            one, two_ = v_out[start : start + half], v_out[start + half : start + count]
            out[...] = jnp.where(first, one, two_)

        @pl.when(stays())
        def _():
            t_local.wait()

        @pl.when(jnp.logical_not(stays()))
        def _():
            t_remote.wait()

        t_out[...] = t_keep[...].astype(F32)
        for copy in sent:
            copy.wait_send()

    main_places = [place for part in layout[: len(mains)] for place in part]

    def vmem(*shape, dtype=BF):
        return pltpu.VMEM(shape, dtype)

    dma = pltpu.SemaphoreType.DMA
    hbm = pl.BlockSpec(memory_space=pl.ANY)
    inside = pl.BlockSpec(memory_space=pltpu.VMEM)
    return pl.pallas_call(
        body,
        in_specs=[hbm] * (n_arr + ns + np)
        + [hbm, inside] * na
        + [inside] * nv
        + [hbm],
        out_specs=[inside] * (len(shapes) + 5),
        out_shape=[sds(shape, F32) for shape in shapes]
        + [sds((count, 128), F32) for count in (gain_rows, enc_count - gain_rows, dec_gain // 2, dec_bias // 2)]
        + [sds(traded.shape, F32)],
        scratch_shapes=[
            pltpu.VMEM((rows, 128), F32),
            pltpu.VMEM(traded.shape, BF),
            pltpu.SemaphoreType.DMA,
            pltpu.SemaphoreType.DMA,
            pltpu.SemaphoreType.DMA,
            vmem(2, 4, l_main, 128),
            vmem(2, 4, l_main, 128),
            vmem(4, l_main, 128),
            vmem(2, l_main, 128),
            vmem(l_main, 128),
            vmem(2, l_stack, 128),
            vmem(2, l_stack, 128),
            vmem(l_stack, 128),
            vmem(l_pair, 128),
            vmem(l_pair, 128),
            vmem(sum(array.shape[1] for array, _ in added), 128),
            vmem(5, rows, 128, dtype=F32),
            dma((n, 2)),
            dma((n, 2)),
            dma((n, 2)),
            dma((n,)),
            dma((n,)),
            dma((n, 2)),
            dma((n, 2)),
            dma((n,)),
            dma((n,)),
            dma((ns, 2)),
            dma((ns, 3)),
            dma((ns, 3)),
            dma((np,)),
            dma((np,)),
            dma((np,)),
            dma((na,)),
            dma((5,)),
            dma((5,)),
        ],
        name="final_sums",
        compiler_params=pltpu.CompilerParams(
            vmem_limit_bytes=VMEM, collective_id=1, has_side_effects=True
        ),
        cost_estimate=pl.CostEstimate(flops=int(100 * SCALE), bytes_accessed=0, transcendentals=0),
    )(*arrays, *stacks, *pairs, *(a for pair in added for a in pair), *enc_vectors, *dec_vectors, traded)


def hand_over(arrays, vectors):
    ins = [*arrays, *vectors]
    shapes = [array.shape for array in ins]
    shapes[4] = (shapes[4][0], DD // 4)

    def body(*refs):
        for source, target in zip(refs[: len(ins)], refs[len(ins) :]):
            target[...] = source[:, : target.shape[1]]

    inside = pl.BlockSpec(memory_space=pltpu.VMEM)
    return pl.pallas_call(
        body,
        in_specs=[inside] * len(ins),
        out_specs=[inside] * len(ins),
        out_shape=[sds(shape, array.dtype) for shape, array in zip(shapes, ins)],
        name="hand_over",
        compiler_params=pltpu.CompilerParams(vmem_limit_bytes=VMEM),
    )(*ins)


def after(value, *deps):
    return lax.optimization_barrier((value, *deps))[0]


def spread(units):
    return jnp.transpose(units, (1, 0, 2)).reshape(units.shape[1], -1)


def tables(place):
    lane = jnp.arange(128)
    frequency = 100.0 ** (-(lane % 16).astype(F32) * 2.0 / 32.0)
    position = jnp.where((lane % 64 < 32)[None, :], place[0][:, None], place[1][:, None])
    angle = position * frequency[None, :]
    sin = jnp.sin(angle)
    return jnp.cos(angle), jnp.where((lane % 32 < 16)[None, :], -sin, sin)


def local(
    tokens,
    out_grad,
    masks,
    coords,
    enc_qkv,
    enc_out,
    enc_up,
    enc_down,
    enc_gains,
    enc_biases,
    proj,
    dec_in,
    dec_outs,
    dec_down,
    dec_gains,
    dec_biases,
):
    n_pair, n_view = lax.axis_size("pair"), lax.axis_size("view")
    quarter, pair_id = lax.axis_index("view"), lax.axis_index("pair")
    half_id, view_id, core = quarter % 2, quarter // 2, pair_id % 2
    half = jnp.stack([half_id, core]).astype(jnp.int32)
    rows = tokens.shape[1]
    tokens = tokens[0]
    d_gd = (out_grad[0].astype(F32) * masks[0].astype(F32)[:, None]).astype(BF)
    chip_plan = n_pair == 8 and n_view == 4

    def trade(value):
        moves = []
        for p in range(n_pair):
            for t in range(n_view):
                moves.append((p * n_view + t, (p - p % 2 + t % 2) * n_view + t - t % 2 + p % 2))
        return lax.ppermute(value, ("pair", "view"), moves)

    tokens = trade(tokens)
    far_coords = swap(coords[:, 0], "pair", 1)
    far_small = swap(jnp.concatenate([dec_gains, dec_biases]), "view", 1)
    place = jnp.where(core == half_id, coords[:, 0], far_coords).astype(F32)

    def seg(view, half_of):
        return lax.dynamic_slice_in_dim(place, (view * 2 + half_of) * rows, rows, 1)

    cos_all, sin_all = tables(jnp.concatenate([seg(view_id, core), seg(view_id, 1 - core)], axis=1))
    cos_oth, sin_oth = tables(
        jnp.concatenate([seg(1 - view_id, core), seg(1 - view_id, 1 - core)], axis=1)
    )
    back_all, back_oth = -sin_all, -sin_oth

    def join_row(mine, theirs):
        return jnp.where(
            half_id == 0, jnp.concatenate([mine, theirs]), jnp.concatenate([theirs, mine])
        ).astype(F32)[None]

    n_gains = dec_gains.shape[0]
    dec_scale = join_row(dec_gains, far_small[:n_gains])
    dec_shift = join_row(dec_biases, far_small[n_gains:])
    enc_scale, enc_shift = enc_gains.astype(F32)[None], enc_biases.astype(F32)[None]
    tokens = after(
        tokens, cos_all, sin_all, cos_oth, sin_oth, back_all, back_oth, dec_scale, dec_shift, d_gd,
        enc_scale, enc_shift,
    )

    s3 = 3 * DD

    def share(array):
        if not chip_plan:
            return array
        count = array.shape[0] // n_pair
        return lax.dynamic_slice_in_dim(array, pair_id * count, count, 0)

    def gather(array):
        return lax.all_gather(array, "pair", axis=0, tiled=True) if chip_plan else array

    s1 = s3 // 2
    own_in = share(dec_in)
    first_piece = own_in[:, :s1]
    second_piece = jnp.concatenate([own_in[:, s1:s3], share(dec_outs)], axis=1)
    third_piece = jnp.concatenate(
        [own_in[:, s3:], share(dec_down).reshape(own_in.shape[0], -1)], axis=1
    )

    start = 4 * DE + FE
    g1, g2 = Row(enc_scale, 0, DE), Row(enc_scale, DE, DE)
    sh1, sh2 = Row(enc_shift, start + DE, DE), Row(enc_shift, start + 2 * DE, DE)
    own_tables = (cos_all, sin_all)
    deps = []

    def pend(*values):
        deps.extend(values)

    def tie(value):
        out = after(value, *deps) if deps else value
        deps.clear()
        return out

    def core_ride(*arrays):
        return [(array, [()], "pair", 1) for array in arrays]

    e_q, e_kv, *e_n1, first_piece, e_kvf = lnproj(
        half, tokens, g1, sh1, Whole(enc_qkv), Row(enc_shift, 0, 3 * DE), *own_tables, 1, 2, 3,
        "enc_qkv", ride=[(first_piece, [()], "view", 1)], number=9,
    )
    far_first = gather(first_piece[0])
    e_p, e_o, *e_ot, second_piece, third_piece = attend(
        half, e_q, e_kv, e_kvf, "enc_attend",
        ride=[(second_piece, [()], "view", 1), (third_piece, [()], "view", 1)], number=16,
    )
    far_second = gather(second_piece[0])
    e_x1, e_n2, e_nt, e_am, e_at, e_slope, z, e_xm, e_xt = ffn_forward(
        half, e_o, tokens, Whole(enc_out), Row(enc_shift, 3 * DE, DE), g2, sh2, Whole(enc_up),
        Row(enc_shift, 4 * DE, FE), Whole(enc_down), Row(enc_shift, start, DE),
        (proj, Row(enc_shift, start + 3 * DE, DD)), 1024, "enc_ffn",
    )
    far_third = gather(after(third_piece[0], z))
    cut = rows // 48 * 16 + 16
    upper, lower = (slice(0, cut),), (slice(cut, rows),)

    w_sqkv = Halves((dec_in, 0), (far_first, 0), 3 * DD // 2)
    w_cq = Halves((dec_in, s1), (far_second, 0), DD // 2)
    w_ckv = Halves((dec_in, 2 * DD), (far_second, DD // 2), DD)
    w_so = Halves((dec_outs, 0), (far_second, s1), DD // 2)
    w_co = Halves((dec_outs, DD // 2), (far_second, 2 * DD), DD // 2)
    ga, gb, gc, gd = [Row(dec_scale, i * DD, DD) for i in range(4)]
    sa, sb, sc, sd = [Row(dec_shift, i * DD, DD) for i in range(4)]
    bias = lambda i, n=1: Row(dec_shift, i * DD, n * DD)
    tied = lambda row: Row(tie(row.array), row.start, row.size)
    s_q, s_kv, *s_nt, z_one, s_kvf = lnproj(
        half, z, ga, sa, w_sqkv, bias(4, 3), *own_tables, 2, 4, 6,
        "dec_qkv", ride=[(z, [upper], "view", 2)], number=6,
    )
    s_p, s_o, *s_ot, z_two, f_n1, f_ot, f_nt, f_at, f_xt = attend(
        half, s_q, s_kv, s_kvf, "self_attend",
        ride=[(z, [lower], "view", 2)] + core_ride(e_n1[1], e_ot[1], e_nt, e_at, e_xt), number=7,
    )
    e_n1, e_ot, e_nt, e_at, e_xt = [
        (mine, far[0], theirs)
        for mine, far, theirs in (
            (e_n1[0], f_n1, e_n1[1]), (e_ot[0], f_ot, e_ot[1]), (e_n2, f_nt, e_nt), (e_am, f_at, e_at),
            (e_xm, f_xt, e_xt),
        )
    ]
    other_z = jnp.concatenate([z_one[0], z_two[0]])
    far_third = after(far_third, s_o)
    far_down = far_third[:, FD // 2 :].reshape(dec_down.shape)
    w_up = Halves((dec_in, s3), (far_third, 0), FD // 2)
    w_down = Halves((dec_down, 0), (far_down, 0), DD // 2)
    y1, c_q, *b_nt = mid_forward(
        half, s_o, z, w_so, bias(7), gb, sb, w_cq, bias(8), *own_tables, "dec_mid",
    )
    pend(y1)
    c_kv, *c_nt, c_kvf = lnproj(
        half, other_z, tied(gc), sc, w_ckv, bias(9, 2), cos_oth, sin_oth, 0, 2, 4, "dec_ckv", number=10,
    )
    c_p, c_o, *c_ot, d_gd, f_sn, f_so, f_bn, f_cn = attend(
        half, c_q, c_kv, c_kvf, "cross_attend",
        ride=[(d_gd, [()], "trade", 0)] + core_ride(s_nt[1], s_ot[1], b_nt[1], c_nt[1]), number=11,
    )
    d_gd = d_gd[0]
    s_nt, s_ot, b_nt, c_nt = [
        (mine, far[0], theirs)
        for (mine, theirs), far in zip((s_nt, s_ot, b_nt, c_nt), (f_sn, f_so, f_bn, f_cn))
    ]
    y2, d_nm, d_nt, d_am, d_at, d_slope, mixed = ffn_forward(
        half, c_o, y1, w_co, bias(11), gd, sd, w_up, Row(dec_shift, 12 * DD, FD), w_down,
        Row(dec_shift, 12 * DD + FD, DD), None, 768, "dec_ffn",
    )

    chip = pair_id // 2
    pack = lambda *ids: jnp.stack([jnp.asarray(i, jnp.int32) for i in ids])
    dec_z = pack(half_id, 1 - half_id, 0, 1, 2, 3)
    dec_near = pack(half_id, 1 - half_id, chip, chip ^ 1, chip ^ 2, chip ^ 3)
    enc_z = pack(quarter, quarter ^ 1, quarter ^ 2, quarter ^ 3, 0, 1, 2, 3)
    enc_near = pack(
        quarter, quarter ^ 1, quarter ^ 2, quarter ^ 3, chip, chip ^ 1, chip ^ 2, chip ^ 3
    )

    def blocks(plan, a, g, far, width, bn, name, **rest):
        if not chip_plan:
            return None
        nz = plan.shape[0] - 4
        out = weight_blocks(tie(plan), a[0], a[1], g, far, nz, width, bn, name, **rest)
        pend(out)
        return out

    def summed(out):
        return chip_sum(out) if chip_plan else None

    d_gu, d_gco, grad_y2, d_doc, vb_down, vb_up, vg_d, vs_d, vb_co, f_at, f_nt, f_ot, far_gd, far_gu = (
        ffn_backward(
            half, d_gd, None, w_down, d_slope, w_up, y2, gd, w_co, 768, "dec_ffn_back",
            ride=core_ride(d_at, d_nt, c_ot[1], d_gd), number=12,
        )
    )
    d_at, d_nt, c_ot = (d_am, f_at[0], d_at), (d_nm, f_nt[0], d_nt), (c_ot[0], f_ot[0], c_ot[1])
    ffn = blocks(dec_z, d_at, d_gd, far_gd[0], 384, 384, "dw_dec_down", total=2304)
    t_ffn = summed(
        blocks(dec_z, d_nt, d_gu, far_gu, 1536, 768, "dw_dec_up", base=ffn, at=1152, total=2304)
    )
    c_own, c_ship, mixed, far_gco, c_back = attend_back(
        half, c_q, c_kv, c_kvf, c_p, c_o, tie(d_doc), cos_all, back_all, cos_oth, back_oth,
        "cross_back", ride=[(mixed, [()], "trade", 0)] + core_ride(d_gco), number=13,
    )
    mixed = mixed[0]
    g_ckv, vb_ckv, grad_other, vg_c, vs_c, far_ckv = proj_backward(
        half, None, c_own, c_back, w_ckv, other_z, gc, None, 384, "ckv_back", number=14
    )
    pend(g_ckv)
    grad_y1, d_gso, d_dos, vb_cq, vg_b, vs_b, vb_so = mid_backward(
        half, c_ship, w_cq, y1, tied(gb), grad_y2, w_so, "mid_back"
    )
    cross = blocks(dec_z, c_ot, d_gco, far_gco[0], 384, 384, "dw_co", total=1152)
    cross = blocks(dec_z, b_nt, c_ship, c_back, 384, 384, "dw_cq", base=cross, at=288, total=1152)
    t_cross = summed(
        blocks(dec_z, c_nt, g_ckv, far_ckv, 768, 768, "dw_ckv", base=cross, at=576, total=1152)
    )
    s_own, s_ship, returned, far_gso, s_back = attend_back(
        half, s_q, s_kv, s_kvf, s_p, s_o, tie(d_dos), cos_all, back_all, cos_all, back_all, "self_back",
        ride=[(grad_other, [lower], "view", 2)] + core_ride(d_gso), number=2,
    )
    g_sqkv, vb_sqkv, grad_own, vg_a, vs_a, returned_up, far_sqkv = proj_backward(
        half, s_ship, s_own, s_back, w_sqkv, z, ga, grad_y1, 384, "qkv_back",
        ride=[(grad_other, [upper], "view", 2)], number=8,
    )
    returned = (returned_up[0], returned[0])
    e_gp, ub_proj, grad_x2, e_gd, far_gp, far_egd = head_backward(
        half, grad_own, returned, proj, "proj_back", 15
    )
    t_enc_down = summed(blocks(enc_z, e_at, e_gd, far_egd, 256, 256, "dw_enc_down"))
    selfs = blocks(dec_near, s_ot, d_gso, far_gso[0], 384, 384, "dw_so", total=1152)
    selfs = blocks(dec_near, s_nt, g_sqkv, far_sqkv, 1152, 384, "dw_sqkv", base=selfs, at=288, total=1152)
    e_gu, e_go, grad_x1, e_do, ub_down, ub_up, ug_2, us_2, ub_out, *dec_got, far_egu = ffn_backward(
        half, e_gd, grad_x2, Whole(enc_down), e_slope, Whole(enc_up), e_x1, tied(g2), Whole(enc_out),
        1024, "enc_ffn_back", ride=[(t_ffn, [(1,)], "view", 1)] if chip_plan else (),
        number=3,
    )
    pend(e_do)
    t_enc_up = summed(blocks(enc_z, e_nt, e_gu, far_egu, 1024, 1024, "dw_enc_up"))
    e_three = blocks(enc_near, e_xt, e_gp, far_gp, 256, 256, "dw_proj", at=1024, total=1280)
    rides = [(t_cross, [(1,)], "view", 1)] if chip_plan else []
    e_own, e_ship, *rode, far_go, e_back = attend_back(
        half, e_q, e_kv, e_kvf, e_p, e_o, tie(e_do), cos_all, back_all, cos_all, back_all, "enc_back",
        ride=rides + core_ride(e_go), number=4,
    )
    if chip_plan:
        ffn_got, cross_got = [got[0] for got in (*dec_got, *rode)]
    pend(e_own)
    e_three = blocks(
        enc_near, e_ot, e_go, far_go[0], 256, 256, "dw_out", base=e_three, at=768, total=1280
    )
    rides = [(t_enc_down, [(1,), (3,)], "view", 1)] if chip_plan else []
    g_eqkv, ub_qkv, tokens_grad, ug_1, us_1, *rode, far_eqkv = proj_backward(
        half, e_ship, e_own, e_back, Whole(enc_qkv), tokens, tied(g1), grad_x1, 1024, "enc_qkv_back",
        ride=rides, number=5,
    )
    e_three = blocks(
        enc_near, e_n1, g_eqkv, far_eqkv, 768, 768, "dw_enc_qkv", base=e_three, total=1280
    )

    if chip_plan:
        vectors = (
            [ug_1, ug_2, ub_qkv, ub_out, ub_up, ub_down, us_1, us_2, ub_proj],
            [
                vg_a, vg_b, vg_c, vg_d, vs_a, vs_b, vs_c, vs_d,
                vb_sqkv, vb_so, vb_cq, vb_ckv, vb_co, vb_up, vb_down,
            ],
        )
        t_enc_down = after(t_enc_down, g_eqkv)
        t_enc_down = plus(jnp.stack([t_enc_down[0], t_enc_down[2]]), rode[0])
        mains = [
            (e_three, [(128 * c, 128, c % 2) for c in range(10)]),
            (selfs, [(288 * c, 288, c % 2) for c in range(4)]),
        ]
        added = [(t_ffn, ffn_got), (t_cross, cross_got)]
        shapes = [
            (DE // 8, 3 * DE // 4), (DE // 8, DE // 4), (DE // 8, FE // 4), (FE // 8, DE // 4),
            (DE // 8, 256), (DD // 8, 3 * DD + FD // 2), (DD // 8, DD), (FD // 8, DD // 2),
        ]

        def run(count, units, out, column):
            return [(count, out, column + 128 * u) for u in range(units)]

        layout = [
            run(128, 6, 0, 0) + run(128, 2, 1, 0) + run(128, 2, 4, 0),
            run(96, 3, 6, 0) + run(96, 9, 5, 0),
            run(128, 8, 2, 0),
            run(512, 2, 3, 0),
            run(384, 3, 7, 0) + run(96, 12, 5, 3 * DD),
            run(96, 3, 6, DD // 2) + run(96, 3, 5, 3 * DD // 2) + run(96, 6, 5, 2 * DD),
        ]
        results = final_sums(
            mains, [t_enc_up], [t_enc_down], added, layout, shapes, vectors, tokens_grad
        )
        (
            enc_qkv_grad, enc_out_grad, enc_up_grad, enc_down_grad, proj_grad, dec_in_grad,
            dec_outs_grad, dec_down_grad, tokens_grad, mixed, *vectors,
        ) = hand_over([*results[:8], results[12], mixed], results[8:12])
        enc_gains_grad, enc_biases_grad, dec_gains_grad, dec_biases_grad = [
            v.reshape(-1) for v in vectors
        ]
    else:
        def tall(pieces):
            mine, _, theirs = pieces
            even, odd = jnp.where(core == 0, mine, theirs), jnp.where(core == 0, theirs, mine)
            return jnp.stack([even, odd], axis=1).reshape(-1, rows)

        def scatter(value, axis, dim):
            return lax.psum_scatter(value.astype(BF), axis, scatter_dimension=dim, tiled=True)

        def enc_sum(a, g):
            return scatter(scatter(mm(tall(a), g), "pair", 0), "view", 1).astype(F32)

        def halves(value, which):
            width = value.shape[1] // 2
            return lax.dynamic_slice_in_dim(value, which * width, width, 1)

        def dec_sum(*pairs):
            blocks = [mm(tall(a), g) for a, g in pairs]
            mine = jnp.concatenate([halves(b, half_id) for b in blocks], axis=1)
            other = jnp.concatenate([halves(b, 1 - half_id) for b in blocks], axis=1)
            both = mine + swap(other.astype(BF), "view", 1).astype(F32)
            return scatter(both, "pair", 0).astype(F32)

        dec_in_grad = dec_sum((s_nt, g_sqkv), (b_nt, c_ship[2]), (c_nt, g_ckv), (d_nt, d_gu))
        dec_outs_grad = dec_sum((s_ot, d_gso), (c_ot, d_gco))
        dec_down_grad = dec_sum((d_at, d_gd))
        enc_qkv_grad, enc_out_grad = enc_sum(e_n1, g_eqkv), enc_sum(e_ot, e_go)
        enc_up_grad, enc_down_grad = enc_sum(e_nt, e_gu), enc_sum(e_at, e_gd)
        proj_grad = enc_sum(e_xt, e_gp.reshape(rows, 4, -1)[:, :, : DD // 4].reshape(rows, DD))

    if not chip_plan:
        tokens_grad = trade(tokens_grad).astype(F32)
        dec_vec = jnp.concatenate(
            [
                vg_a, vg_b, vg_c, vg_d, vs_a, vs_b, vs_c, vs_d,
                vb_sqkv, vb_so, vb_cq, vb_ckv, vb_co, vb_up, vb_down,
            ],
            axis=1,
        )[0]
        empty = jnp.zeros_like(dec_vec)
        enc_parts = [ug_1, ug_2, ub_qkv, ub_out, ub_up, ub_down, us_1, us_2, ub_proj]
        enc_vec, dec_one, dec_two = lax.psum(
            (
                jnp.concatenate(enc_parts, axis=1)[0],
                jnp.where(view_id == 0, dec_vec, empty),
                jnp.where(view_id == 0, empty, dec_vec),
            ),
            ("pair", "view"),
        )
        dec_vec = jnp.where(view_id == 0, dec_one, dec_two)
        enc_gains_grad, enc_biases_grad = enc_vec[: 2 * DE], enc_vec[2 * DE :]
        gain_all, bias_all = dec_vec[: 4 * DD], dec_vec[4 * DD :]
        gain_part, bias_part = gain_all.shape[0] // 2, bias_all.shape[0] // 2
        dec_gains_grad = lax.dynamic_slice_in_dim(gain_all, half_id * gain_part, gain_part, 0)
        dec_biases_grad = lax.dynamic_slice_in_dim(bias_all, half_id * bias_part, bias_part, 0)
    return (
        mixed[None],
        tokens_grad[None],
        enc_qkv_grad,
        enc_out_grad,
        enc_up_grad,
        enc_down_grad,
        enc_gains_grad,
        enc_biases_grad,
        proj_grad,
        dec_in_grad,
        dec_outs_grad,
        dec_down_grad,
        dec_gains_grad,
        dec_biases_grad,
    )


def solution(mesh):
    both = P("pair", "view")
    return jax.shard_map(
        local,
        mesh=mesh,
        in_specs=(
            P("pair", "view", None),
            P("pair", "view", None),
            both,
            P(None, "pair", None),
            P(),
            P(),
            P(),
            P(),
            P(),
            P(),
            P(),
            P(None, "view"),
            P(None, "view"),
            P(None, "view"),
            P("view"),
            P("view"),
        ),
        out_specs=(
            P("pair", "view", None),
            P("pair", "view", None),
            both,
            both,
            both,
            both,
            P(),
            P(),
            both,
            both,
            both,
            both,
            P("view"),
            P("view"),
        ),
        check_vma=False,
    )
```

```python
from functools import partial

import jax
import jax.numpy as jnp
from jax import lax
from jax.experimental import pallas as pl
from jax.experimental.pallas import tpu as pltpu
from jax.sharding import PartitionSpec as P

DE = 1024
HE = 16
FE = 4096
DD = 768
HD = 12
FD = 3072

norm_eps = 1e-06
BF = jnp.bfloat16
F32 = jnp.float32
VMEM = 58 * 1024 * 1024

NN = (((1,), (0,)), ((), ()))
NT = (((1,), (1,)), ((), ()))
TN = (((0,), (0,)), ((), ()))


def mm(a, b, dims=NN):
    return lax.dot_general(a, b, dims, preferred_element_type=F32)


def full(shape):
    zeros = (0,) * len(shape)
    return pl.BlockSpec(shape, lambda *_: zeros)


def sds(shape, dtype):
    return jax.ShapeDtypeStruct(shape, dtype)


MESH = pl.DeviceIdType.MESH


def across(axis, bit):
    here = lax.axis_index(axis)
    return {axis: here + bit - 2 * bit * ((here // bit) % 2)}


def greet(devices):
    barrier = pltpu.get_barrier_semaphore()
    for device in devices:
        pl.semaphore_signal(barrier, inc=1, device_id=device, device_id_type=MESH)
    pl.semaphore_wait(barrier, len(devices))


def slanted():
    return {**across("pair", 1), **across("view", 1)}


def stays():
    return lax.axis_index("pair") % 2 == lax.axis_index("view") % 2


def part(ref, index):
    if not index:
        return ref
    return ref.at[
        tuple(pl.ds(i.start, i.stop - i.start) if isinstance(i, slice) and i.stop else i for i in index)
    ]


def carry(body, name, number, ride, mirror, grid, in_specs, out_specs, out_shape, args, scratch):
    landing, moves = [], []
    for k, (array, indices, axis, bit) in enumerate(ride):
        shape = jax.eval_shape(lambda a, i=indices[0]: a[i], array).shape if indices[0] else array.shape
        landing.append(sds((len(indices), *shape), array.dtype))
        moves += [(k, place, index, axis, bit) for place, index in enumerate(indices)]
    partners = {(axis, bit) for _, _, axis, bit in ride}
    if mirror:
        partners.add(("pair", 1))
    partners = sorted(partners)
    landing += [out_shape[k] for k, _ in mirror]
    n_in, n_out, n_ride, n_mirror = len(in_specs), len(out_specs), len(ride), len(mirror)
    n_scratch = len(scratch)
    traded = [array for array, _, axis, _ in ride if axis == "trade"]
    n_trade = len(traded)
    last = grid[0] - 1

    def plain(spec):
        return pl.BlockSpec(spec.block_shape, lambda j, index=spec.index_map: index(j, None))

    def shell(*refs):
        ins, refs = refs[:n_in], refs[n_in:]
        sources, refs = refs[:n_ride], refs[n_ride:]
        outs, refs = refs[:n_out], refs[n_out:]
        targets, refs = refs[:n_ride], refs[n_ride:]
        fars, refs = refs[:n_mirror], refs[n_mirror:]
        rest, refs = refs[:n_scratch], refs[n_scratch:]
        held, refs = refs[:n_mirror], refs[n_mirror:]
        bounce, refs = refs[:n_trade], refs[n_trade:]
        sems = list(refs)
        j = pl.program_id(0)

        def device(axis, bit):
            return slanted() if axis == "trade" else across(axis, bit)

        def remote(source, target, send, recv, to):
            return pltpu.make_async_remote_copy(
                src_ref=source, dst_ref=target, send_sem=send, recv_sem=recv, device_id=to,
                device_id_type=MESH,
            )

        def rides(act):
            for m, (k, place, index, axis, bit) in enumerate(moves):
                source, target = part(sources[k], index), targets[k].at[place]
                send, recv = sems[0].at[m], sems[1].at[m]
                copy = remote(source, target, send, recv, device(axis, bit))
                if axis == "trade":
                    pl.when(jnp.logical_not(stays()))(lambda copy=copy: act(copy))
                else:
                    act(copy)

        def keeps(out):
            found = [m for m, (_, _, _, axis, _) in enumerate(moves) if axis == "trade"]
            for i, m in enumerate(found):
                if out:
                    yield pltpu.make_async_copy(bounce[i], targets[moves[m][0]].at[0], sems[0].at[m])
                else:
                    yield pltpu.make_async_copy(sources[moves[m][0]], bounce[i], sems[1].at[m])

        def mirrored(m, n, index):
            send, recv = sems[2 * (m + 1)].at[n], sems[2 * (m + 1) + 1].at[n]
            return remote(part(held[m], index), part(fars[m], index), send, recv, across("pair", 1))

        @pl.when(j == 0)
        def _():
            greet([device(axis, bit) for axis, bit in partners])
            rides(lambda copy: copy.start())
            if traded:

                @pl.when(stays())
                def _():
                    for copy in keeps(False):
                        copy.start()

        if traded:

            @pl.when((j == 1) & stays())
            def _():
                for copy in keeps(False):
                    copy.wait()
                for copy in keeps(True):
                    copy.start()

        body((lax.axis_index("view") % 2, lax.axis_index("pair") % 2), *ins, *outs, *rest)

        for m, (k, steps) in enumerate(mirror):
            for n, (step, index) in enumerate(steps):

                @pl.when(j == step)
                def _(m=m, n=n, k=k, index=index):
                    part(held[m], index)[...] = outs[k][...]
                    mirrored(m, n, index).start()

        @pl.when(j == last)
        def _():
            for m, (_, steps) in enumerate(mirror):
                for n, (_, index) in enumerate(steps):
                    mirrored(m, n, index).wait()
            rides(lambda copy: copy.wait())
            if traded:

                @pl.when(stays())
                def _():
                    for copy in keeps(True):
                        copy.wait()

    hbm = pl.BlockSpec(memory_space=pl.ANY)
    dma = pltpu.SemaphoreType.DMA
    counts = [max(1, len(moves))] + [len(steps) for _, steps in mirror]
    return pl.pallas_call(
        shell,
        grid=grid,
        in_specs=[plain(spec) for spec in in_specs] + [hbm] * n_ride,
        out_specs=[plain(spec) for spec in out_specs] + [hbm] * (n_ride + n_mirror),
        out_shape=list(out_shape) + landing,
        scratch_shapes=list(scratch)
        + [pltpu.VMEM(out_shape[k].shape, out_shape[k].dtype) for k, _ in mirror]
        + [pltpu.VMEM(array.shape, array.dtype) for array in traded]
        + [dma((count,)) for count in counts for _ in range(2)],
        name=name,
        compiler_params=pltpu.CompilerParams(
            vmem_limit_bytes=VMEM, collective_id=number, has_side_effects=True
        ),
        cost_estimate=cost(name),
    )(*args, *(array for array, *_ in ride))


def call(
    body, name, half, grid, in_specs, out_specs, out_shape, args, scratch=(), flops=0, nbytes=0,
    ride=(), number=0, mirror=(),
):
    if number:
        return carry(body, name, number, ride, mirror, grid, in_specs, out_specs, out_shape, args, scratch)
    return pl.pallas_call(
        body,
        grid_spec=pltpu.PrefetchScalarGridSpec(
            num_scalar_prefetch=1,
            grid=grid,
            in_specs=in_specs,
            out_specs=out_specs,
            scratch_shapes=list(scratch),
        ),
        out_shape=out_shape,
        name=name,
        compiler_params=pltpu.CompilerParams(vmem_limit_bytes=VMEM),
        cost_estimate=cost(name),
    )(half, *args)


SCALE = 0.2e9

TIMES = {
    "enc_qkv": 8, "enc_attend": 19, "enc_ffn": 20, "dec_qkv": 8, "self_attend": 15, "dec_mid": 5,
    "dec_ckv": 7, "cross_attend": 15, "dec_ffn": 15, "dec_ffn_back": 13, "cross_back": 15,
    "mid_back": 5, "ckv_back": 7, "self_back": 15, "qkv_back": 10, "proj_back": 4,
    "enc_ffn_back": 18, "enc_back": 18, "enc_qkv_back": 11, "dw_dec_down": 6, "dw_dec_up": 6,
    "dw_co": 4, "dw_cq": 4, "dw_ckv": 4, "dw_so": 4, "dw_sqkv": 6, "dw_enc_down": 8, "dw_proj": 5,
    "dw_enc_up": 8, "dw_out": 5, "dw_enc_qkv": 7,
}


def cost(name):
    flops = int(TIMES[name] * SCALE)
    return pl.CostEstimate(flops=flops, bytes_accessed=0, transcendentals=0)


class Row:
    def __init__(self, array, start, size):
        self.array, self.start, self.size = array, start, size

    @property
    def spec(self):
        return full(self.array.shape)

    def get(self, ref):
        return ref[:, self.start : self.start + self.size]

    def block(self, ref, j, bn):
        return ref[:, pl.ds(pl.multiple_of(self.start + j * bn, 128), bn)]


class Whole:
    def __init__(self, array):
        self.arrays, self.columns = [array], array.shape[1]
        self.rows = array.shape[0]

    def blocks(self, bn, fixed=False):
        return [pl.BlockSpec((self.rows, bn), lambda j, h: (0, j))]

    def whole(self, bn=None):
        if bn is None:
            return [full(self.arrays[0].shape)]
        return [pl.BlockSpec((bn, self.columns), lambda j, h: (j, 0))]

    def read(self, refs, h, j, bn):
        return refs[0][...]

    def read_whole(self, refs, h):
        return refs[0][...]


class Halves:
    def __init__(self, own, far, width):
        self.arrays = [own[0], far[0]]
        self.starts, self.width = (own[1], far[1]), width
        self.rows, self.columns = own[0].shape[0], 2 * width

    def blocks(self, bn, fixed=False):
        per = self.width // bn
        specs = []
        for which, start in enumerate(self.starts):

            def index(j, h, which=which, start=start):
                if fixed:
                    return 0, start // bn + j % per
                half = h[0] ^ which
                hold = jnp.where(half == 0, per - 1, 0)
                return 0, start // bn + jnp.where(j // per == half, j % per, hold)

            specs.append(pl.BlockSpec((self.rows, bn), index))
        return specs

    def whole(self, bn=None):
        specs = []
        for start in self.starts:
            col = start // self.width
            if bn is None:
                specs.append(pl.BlockSpec((self.rows, self.width), lambda j, h, col=col: (0, col)))
            else:
                specs.append(pl.BlockSpec((bn, self.width), lambda j, h, col=col: (j, col)))
        return specs

    def read(self, refs, h, j, bn):
        return jnp.where(j // (self.width // bn) == h[0], refs[0][...], refs[1][...])

    def read_whole(self, refs, h):
        own, far = refs[0][...], refs[1][...]
        first = h[0] == 0
        return jnp.concatenate([jnp.where(first, own, far), jnp.where(first, far, own)], axis=1)


def norm_parts(x):
    centred = x - jnp.mean(x, axis=-1, keepdims=True)
    rstd = lax.rsqrt(jnp.mean(centred * centred, axis=-1, keepdims=True) + norm_eps)
    return centred * rstd, rstd


def norm_back(dy, x, gain):
    xhat, rstd = norm_parts(x)
    dgain = jnp.sum(dy * xhat, axis=0, keepdims=True)
    dshift = jnp.sum(dy, axis=0, keepdims=True)
    dxh = dy * gain
    mean_one = jnp.mean(dxh, axis=-1, keepdims=True)
    mean_two = jnp.mean(dxh * xhat, axis=-1, keepdims=True)
    return rstd * (dxh - mean_one - xhat * mean_two), dgain, dshift


def turn(u, cos, sin):
    lane = lax.broadcasted_iota(jnp.int32, u.shape, 1)
    other = jnp.where(lane % 32 < 16, pltpu.roll(u, 112, 1), pltpu.roll(u, 16, 1))
    return u * cos + other * sin


def turn_cols(y, cos, sin):
    return jnp.concatenate(
        [turn(y[:, i : i + 128], cos, sin) for i in range(0, y.shape[1], 128)], axis=1
    )


def gelu_parts(u):
    phi = 0.5 + 0.5 * lax.erf(u * 0.7071067811865476)
    return u * phi, phi + u * jnp.exp(-0.5 * u * u) * 0.3989422804014327


def col_sum(g):
    return jnp.sum(g.astype(F32), axis=0, keepdims=True)


def deal(h, tall, mine, theirs, at=None):
    rb = mine.shape[1]
    for s in range(tall.shape[0] // (2 * rb)):
        even, odd = tall[2 * s * rb : (2 * s + 1) * rb], tall[(2 * s + 1) * rb : (2 * s + 2) * rb]
        first = h[1] == 0
        mine[s] = jnp.where(first, even, odd)
        theirs[s] = jnp.where(first, odd, even)


def dealt(width, rows):
    return [sds((4, width // 8, rows), BF)] * 2


def columns_at(i, bn):
    return slice(None), slice(i * bn, i * bn + bn)


def lnproj(half, x, gain, shift, w, b, cos, sin, n_q, n_turn, n_all, name, ride=(), number=0):
    rows, width = x.shape
    bn = w.columns // n_all
    n_w = len(w.arrays)
    has_q = n_q > 0

    def body(h, x_ref, g_ref, s_ref, b_ref, c_ref, sn_ref, *rest):
        w_refs, rest = rest[:n_w], rest[n_w:]
        if has_q:
            q_ref, kv_ref, mine, theirs, nrm = rest
        else:
            kv_ref, mine, theirs, nrm = rest
        j = pl.program_id(0)

        @pl.when(j == 0)
        def _():
            xhat, _ = norm_parts(x_ref[...].astype(F32))
            low = (xhat * gain.get(g_ref) + shift.get(s_ref)).astype(BF)
            nrm[...] = low
            deal(h, low.T, mine, theirs)

        y = mm(nrm[...], w.read(w_refs, h, j, bn)) + b.block(b_ref, j, bn)

        @pl.when(j < n_turn)
        def _():
            out = turn_cols(y, c_ref[...], sn_ref[...]).astype(BF)
            if has_q:

                @pl.when(j < n_q)
                def _():
                    q_ref[...] = out

                @pl.when(j >= n_q)
                def _():
                    kv_ref[...] = out

            else:
                kv_ref[...] = out

        @pl.when(j >= n_turn)
        def _():
            kv_ref[...] = y.astype(BF)

    outs = [
        sds((rows, bn * (n_all - n_q)), BF),
        *dealt(width, rows),
    ]
    specs = [
        pl.BlockSpec((rows, bn), lambda j, h: (0, jnp.maximum(j - n_q, 0))),
        full((4, width // 8, rows)),
        full((4, width // 8, rows)),
    ]
    if has_q:
        outs.insert(0, sds((rows, bn * n_q), BF))
        specs.insert(0, pl.BlockSpec((rows, bn), lambda j, h: (0, jnp.minimum(j, n_q - 1))))
    return call(
        body,
        name,
        half,
        (n_all,),
        [
            full((rows, width)),
            gain.spec,
            shift.spec,
            b.spec,
            full((rows, 128)),
            full((rows, 128)),
        ]
        + w.blocks(bn, number > 0),
        specs,
        outs,
        (x, gain.array, shift.array, b.array, cos, sin, *w.arrays),
        [pltpu.VMEM((rows, width), BF)],
        ride=ride,
        number=number,
        mirror=[(1 if has_q else 0, [(n_q + i, columns_at(i, bn)) for i in range(n_all - n_q)])],
    )


def two_heads(block):
    first = lax.broadcasted_iota(jnp.int32, block.shape, 1) < 64
    zero = jnp.zeros_like(block)
    return jnp.concatenate(
        [jnp.where(first, block, zero), jnp.where(first, zero, block)], axis=0
    )


def pick_heads(tall, rows):
    return jnp.concatenate([tall[:64, :rows], tall[64:, rows:]], axis=0)


def attend(half, q, kv, kvf, name, ride=(), number=0):
    rows, width = q.shape
    pairs = width // 128
    keys = 2 * rows

    def body(h, q_ref, ko_ref, vo_ref, kf_ref, vf_ref, p_ref, l_ref, o_ref, mine, theirs, tall):
        q2 = two_heads(q_ref[...] * jnp.asarray(0.125, BF))
        k = jnp.concatenate([ko_ref[...], kf_ref[...]], axis=0)
        v = jnp.concatenate([vo_ref[...], vf_ref[...]], axis=0)
        vt = v.T
        s = mm(k, q2, NT)
        e = jnp.exp(s - jnp.max(s, axis=0, keepdims=True))
        p = e.astype(BF)
        share = 1.0 / jnp.sum(e, axis=0, keepdims=True)
        p_ref[0] = p
        l_ref[0] = share
        t = pick_heads(mm(vt, p) * share, rows)
        j = pl.program_id(0)
        tall[pl.ds(pl.multiple_of(j * 128, 128), 128), :] = t.astype(BF)
        o_ref[...] = t.T.astype(BF)

        @pl.when(j == pairs - 1)
        def _():
            deal(h, tall[...], mine, theirs)

    col = lambda j, h: (0, j)
    val = lambda j, h: (0, pairs + j)
    return call(
        body,
        name,
        half,
        (pairs,),
        [
            pl.BlockSpec((rows, 128), col),
            pl.BlockSpec((rows, 128), col),
            pl.BlockSpec((rows, 128), val),
            pl.BlockSpec((rows, 128), col),
            pl.BlockSpec((rows, 128), val),
        ],
        [
            pl.BlockSpec((1, keys, 2 * rows), lambda j, h: (j, 0, 0)),
            pl.BlockSpec((1, 1, 2 * rows), lambda j, h: (j, 0, 0)),
            pl.BlockSpec((rows, 128), col),
            full((4, width // 8, rows)),
            full((4, width // 8, rows)),
        ],
        [
            sds((pairs, keys, 2 * rows), BF),
            sds((pairs, 1, 2 * rows), F32),
            sds((rows, width), BF),
            *dealt(width, rows),
        ],
        (q, kv, kv, kvf, kvf),
        [pltpu.VMEM((width, rows), BF)],
        ride=ride,
        number=number,
    )


def attend_back(half, q, kv, kvf, p, share, o, do, cos, sin, cos_all, sin_all, name, ride=(), number=0):
    rows, width = q.shape
    pairs = width // 128
    keys = 2 * rows

    def body(
        h, q_ref, ko_ref, vo_ref, kf_ref, vf_ref, p_ref, l_ref, o_ref, do_ref, c_ref, s_ref, ca_ref, sa_ref,
        own_ref, ship_ref,
    ):
        q2 = two_heads(q_ref[...] * jnp.asarray(0.125, BF))
        k = jnp.concatenate([ko_ref[...], kf_ref[...]], axis=0)
        v = jnp.concatenate([vo_ref[...], vf_ref[...]], axis=0)
        kt = k.T
        do_low = do_ref[...]
        share = l_ref[0]
        column = jnp.broadcast_to(share, (128, 2 * rows)).T
        do2 = (two_heads(do_low).astype(F32) * column).astype(BF)
        prod = two_heads(do_low.astype(F32) * o_ref[...].astype(F32))
        inner = lax.dot_general(
            jnp.ones((8, 128), F32), prod, NT, precision=lax.Precision.HIGHEST,
            preferred_element_type=F32,
        )[:1]
        p = p_ref[0]
        ds = (p.astype(F32) * (mm(v, do2, NT) - inner * share)).astype(BF)
        dk = mm(ds, q2)
        dv = mm(p, do2)
        dq = pick_heads(mm(kt, ds), rows).T * 0.125
        ship_ref[2] = turn(dq, c_ref[...], s_ref[...]).astype(BF)
        dk = turn(dk, ca_ref[...], sa_ref[...])
        own_ref[0] = dk[:rows]
        own_ref[1] = dv[:rows]
        ship_ref[0] = dk[rows:].astype(BF)
        ship_ref[1] = dv[rows:].astype(BF)

    col = lambda j, h: (0, j)
    val = lambda j, h: (0, pairs + j)
    return call(
        body,
        name,
        half,
        (pairs,),
        [
            pl.BlockSpec((rows, 128), col),
            pl.BlockSpec((rows, 128), col),
            pl.BlockSpec((rows, 128), val),
            pl.BlockSpec((rows, 128), col),
            pl.BlockSpec((rows, 128), val),
            pl.BlockSpec((1, keys, 2 * rows), lambda j, h: (j, 0, 0)),
            pl.BlockSpec((1, 1, 2 * rows), lambda j, h: (j, 0, 0)),
            pl.BlockSpec((rows, 128), col),
            pl.BlockSpec((rows, 128), col),
            full((rows, 128)),
            full((rows, 128)),
            full((keys, 128)),
            full((keys, 128)),
        ],
        [
            pl.BlockSpec((2, rows, 128), lambda j, h: (0, 0, j)),
            pl.BlockSpec((3, rows, 128), lambda j, h: (0, 0, j)),
        ],
        [sds((2, rows, width), F32), sds((3, rows, width), BF)],
        (q, kv, kv, kvf, kvf, p, share, o, do, cos, sin, cos_all, sin_all),
        (),
        ride=ride,
        number=number,
        mirror=[(1, [(i, (slice(None), *columns_at(i, 128))) for i in range(pairs)])],
    )


def ffn_forward(half, o, resid, wo, bo, gain, shift, w_up, b_up, w_down, b_down, head, bn, name, ride=(), number=0):
    rows, width = o.shape
    hidden = w_up.columns
    steps = hidden // bn
    n_w = len(wo.arrays)

    def body(h, o_ref, r_ref, bo_ref, g_ref, s_ref, bu_ref, bd_ref, *rest):
        wo_refs, up_refs, dn_refs, rest = rest[:n_w], rest[n_w : 2 * n_w], rest[2 * n_w : 3 * n_w], rest[3 * n_w :]
        if head:
            pj_ref, bp_ref, x1_ref, n_mine, n_theirs, a_mine, a_theirs, gp_ref, z_ref, *rest = rest
            x_mine, x_theirs, nrm, acc = rest
        else:
            x1_ref, n_mine, n_theirs, a_mine, a_theirs, gp_ref, z_ref, nrm, acc = rest
        j = pl.program_id(0)

        @pl.when(j == 0)
        def _():
            x1 = r_ref[...].astype(F32) + mm(o_ref[...], wo.read_whole(wo_refs, h)) + bo.get(bo_ref)
            x1_ref[...] = x1
            xhat, _ = norm_parts(x1)
            low = (xhat * gain.get(g_ref) + shift.get(s_ref)).astype(BF)
            nrm[...] = low
            deal(h, low.T, n_mine, n_theirs)
            acc[...] = x1 + b_down.get(bd_ref)

        u = mm(nrm[...], w_up.read(up_refs, h, j, bn)) + b_up.block(bu_ref, j, bn)
        act, slope = gelu_parts(u)
        act = act.astype(BF)
        gp_ref[...] = slope.astype(BF)
        deal(h, act.T, a_mine, a_theirs)
        acc[...] += mm(act, w_down.read_whole(dn_refs, h))

        @pl.when(j == steps - 1)
        def _():
            low = acc[...].astype(BF)
            if head:
                deal(h, low.T, x_mine, x_theirs)
                z_ref[...] = (mm(low, pj_ref[...]) + head[1].get(bp_ref)).astype(BF)
            else:
                z_ref[...] = low

    whole = full((rows, width))
    in_specs = (
        [whole, whole, bo.spec, gain.spec, shift.spec, b_up.spec, b_down.spec]
        + wo.whole()
        + w_up.blocks(bn)
        + w_down.whole(bn)
    )
    out_specs = [
        whole,
        full((4, width // 8, rows)),
        full((4, width // 8, rows)),
        pl.BlockSpec((bn * 4 // hidden, hidden // 8, rows), lambda j, h: (j, 0, 0)),
        pl.BlockSpec((bn * 4 // hidden, hidden // 8, rows), lambda j, h: (j, 0, 0)),
        pl.BlockSpec((rows, bn), lambda j, h: (0, j)),
    ]
    outs = [
        sds((rows, width), F32),
        *dealt(width, rows),
        *dealt(hidden, rows),
        sds((rows, hidden), BF),
    ]
    vectors = [row.array for row in (bo, gain, shift, b_up, b_down)]
    args = [o, resid, *vectors, *wo.arrays, *w_up.arrays, *w_down.arrays]
    if head:
        wide = head[0].shape[1]
        in_specs += [full((width, wide)), head[1].spec]
        args += [head[0], head[1].array]
        out_specs += [full((rows, wide)), full((4, width // 8, rows)), full((4, width // 8, rows))]
        outs += [sds((rows, wide), BF), *dealt(width, rows)]
    else:
        out_specs += [whole]
        outs += [sds((rows, width), BF)]
    return call(
        body,
        name,
        half,
        (steps,),
        in_specs,
        out_specs,
        outs,
        args,
        [pltpu.VMEM((rows, width), BF), pltpu.VMEM((rows, width), F32)],
        ride=ride,
        number=number,
    )


def head_backward(half, grad, returned, proj, name, number):
    rows, wide = grad.shape
    width = proj.shape[0]

    part = wide // 4
    slot = -(-part // 128) * 128

    def body(h, g_ref, r_ref, s_ref, w_ref, low_ref, b_ref, gx_ref, gd_ref):
        back = jnp.concatenate([r_ref[...], s_ref[...]], axis=0)
        low = (g_ref[...] + back.astype(F32)).astype(BF)
        pad = jnp.zeros((rows, slot - part), BF)
        for t in range(4):
            piece = low[:, t * part : (t + 1) * part]
            low_ref[:, t * slot : (t + 1) * slot] = jnp.concatenate([piece, pad], axis=1)
        b_ref[...] = col_sum(low)
        gx = mm(low, w_ref[...], NT)
        gx_ref[...] = gx
        gd_ref[...] = gx.astype(BF)

    inside, outside = full((rows, wide)), full((rows, width))
    return call(
        body,
        name,
        half,
        (1,),
        [inside, full(returned[0].shape), full(returned[1].shape), full((width, wide))],
        [full((rows, 4 * slot)), full((1, wide)), outside, outside],
        [sds((rows, 4 * slot), BF), sds((1, wide), F32), sds((rows, width), F32), sds((rows, width), BF)],
        (grad, *returned, proj),
        number=number,
        mirror=[(0, [(0, ())]), (3, [(0, ())])],
    )


def ffn_backward(half, gd, base, w_down, slope, w_up, x, gain, wo, bn, name, ride=(), number=0):
    rows, width = x.shape
    hidden = w_up.columns
    steps = hidden // bn
    n_w = len(wo.arrays)
    has_base = base is not None

    def body(h, gd_ref, gp_ref, x_ref, g_ref, *refs):
        wo_refs, up_refs, dn_refs, refs = refs[:n_w], refs[n_w : 2 * n_w], refs[2 * n_w : 3 * n_w], refs[3 * n_w :]
        if has_base:
            base_ref, *refs = refs
        gu_ref, go_ref, gx_ref, do_ref, bd_ref, bu_ref, dg_ref, ds_ref, bo_ref, acc = refs
        j = pl.program_id(0)

        @pl.when(j == 0)
        def _():
            bd_ref[...] = col_sum(gd_ref[...])
            acc[...] = jnp.zeros_like(acc)

        da = mm(gd_ref[...], w_down.read_whole(dn_refs, h), NT)
        gu = (da * gp_ref[...].astype(F32)).astype(BF)
        gu_ref[...] = gu
        bu_ref[...] = col_sum(gu)
        acc[...] += mm(gu, w_up.read(up_refs, h, j, bn), NT)

        @pl.when(j == steps - 1)
        def _():
            dx, dg, ds = norm_back(acc[...], x_ref[...], gain.get(g_ref))
            dg_ref[...] = dg
            ds_ref[...] = ds
            total = (base_ref[...] if has_base else gd_ref[...].astype(F32)) + dx
            gx_ref[...] = total
            go = total.astype(BF)
            go_ref[...] = go
            bo_ref[...] = col_sum(go)
            do_ref[...] = mm(go, wo.read_whole(wo_refs, h), NT).astype(BF)

    vec, whole = full((1, width)), full((rows, width))
    row = sds((1, width), F32)
    return call(
        body,
        name,
        half,
        (steps,),
        [whole, pl.BlockSpec((rows, bn), lambda j, h: (0, j)), whole, gain.spec]
        + wo.whole()
        + w_up.blocks(bn, number > 0)
        + w_down.whole(bn)
        + ([whole] if has_base else []),
        [
            pl.BlockSpec((rows, bn), lambda j, h: (0, j)),
            whole,
            whole,
            whole,
            vec,
            pl.BlockSpec((1, bn), lambda j, h: (0, j)),
            vec,
            vec,
            vec,
        ],
        [
            sds((rows, hidden), BF),
            sds((rows, width), BF),
            sds((rows, width), F32),
            sds((rows, width), BF),
            row,
            sds((1, hidden), F32),
            row,
            row,
            row,
        ],
        [gd, slope, x, gain.array, *wo.arrays, *w_up.arrays, *w_down.arrays] + ([base] if has_base else []),
        [pltpu.VMEM((rows, width), F32)],
        ride=ride,
        number=number,
        mirror=[(0, [(i, columns_at(i, bn)) for i in range(steps)])],
    )


def mid_forward(half, o, resid, wo, bo, gain, shift, w, b, cos, sin, name):
    rows, width = o.shape

    def body(
        h, o_ref, r_ref, bo_ref, g_ref, s_ref, b_ref, c_ref, sn_ref, wo_own, wo_far, w_own, w_far,
        y_ref, q_ref, mine, theirs,
    ):
        y = r_ref[...].astype(F32) + mm(o_ref[...], wo.read_whole((wo_own, wo_far), h)) + bo.get(bo_ref)
        y_ref[...] = y
        xhat, _ = norm_parts(y)
        low = (xhat * gain.get(g_ref) + shift.get(s_ref)).astype(BF)
        deal(h, low.T, mine, theirs)
        q = mm(low, w.read_whole((w_own, w_far), h)) + b.get(b_ref)
        q_ref[...] = turn_cols(q, c_ref[...], sn_ref[...]).astype(BF)

    whole, table = full((rows, width)), full((rows, 128))
    return call(
        body,
        name,
        half,
        (1,),
        [whole, whole, bo.spec, gain.spec, shift.spec, b.spec, table, table] + wo.whole() + w.whole(),
        [whole, whole, full((4, width // 8, rows)), full((4, width // 8, rows))],
        [sds((rows, width), F32), sds((rows, width), BF), *dealt(width, rows)],
        (o, resid, bo.array, gain.array, shift.array, b.array, cos, sin, *wo.arrays, *w.arrays),
        (),
        4 * rows * width * width,
        4 * width * width,
    )


def mid_backward(half, gq, w, x, gain, above, wo, name, ride=(), number=0):
    rows, width = x.shape

    def body(
        h, gq_ref, x_ref, g_ref, a_ref, w_own, w_far, wo_own, wo_far,
        gx_ref, go_ref, do_ref, bq_ref, dg_ref, ds_ref, bo_ref,
    ):
        low = gq_ref[0]
        bq_ref[...] = col_sum(low)
        dx, dg, ds = norm_back(mm(low, w.read_whole((w_own, w_far), h), NT), x_ref[...], gain.get(g_ref))
        dg_ref[...] = dg
        ds_ref[...] = ds
        total = a_ref[...] + dx
        gx_ref[...] = total
        go = total.astype(BF)
        go_ref[...] = go
        bo_ref[...] = col_sum(go)
        do_ref[...] = mm(go, wo.read_whole((wo_own, wo_far), h), NT).astype(BF)

    whole, vec = full((rows, width)), full((1, width))
    row = sds((1, width), F32)
    return call(
        body,
        name,
        half,
        (1,),
        [pl.BlockSpec((1, rows, width), lambda j, h: (2, 0, 0)), whole, gain.spec, whole]
        + w.whole()
        + wo.whole(),
        [whole, whole, whole, vec, vec, vec, vec],
        [sds((rows, width), F32), sds((rows, width), BF), sds((rows, width), BF), row, row, row, row],
        (gq, x, gain.array, above, *w.arrays, *wo.arrays),
        ride=ride,
        number=number,
    )


def proj_backward(half, gq, own, back, w, x, gain, above, bn, name, ride=(), number=0):
    rows, width = x.shape
    steps, per = w.columns // bn, width // bn
    has_q, has_above = gq is not None, above is not None
    n_w = len(w.arrays)
    skip = per if has_q else 0

    def body(h, *refs):
        if has_q:
            gq_ref, *refs = refs
        own_ref, back_ref, x_ref, g_ref, *refs = refs
        w_refs, refs = refs[:n_w], refs[n_w:]
        if has_above:
            a_ref, *refs = refs
        g_out, b_ref, gx_ref, dg_ref, ds_ref, acc = refs
        j = pl.program_id(0)
        low = (own_ref[0] + back_ref[0].astype(F32)).astype(BF)
        if has_q:
            low = jnp.where(j < per, gq_ref[0], low)
        g_out[...] = low
        b_ref[...] = col_sum(low)
        piece = mm(low, w.read(w_refs, h, j, bn), NT)

        @pl.when(j == 0)
        def _():
            acc[...] = piece

        @pl.when(j > 0)
        def _():
            acc[...] += piece

        @pl.when(j == steps - 1)
        def _():
            dx, dg, ds = norm_back(acc[...], x_ref[...].astype(F32), gain.get(g_ref))
            dg_ref[...] = dg
            ds_ref[...] = ds
            gx_ref[...] = (a_ref[...] + dx if has_above else dx).astype(gx_ref.dtype)

    whole, vec = full((rows, width)), full((1, width))

    def part_index(j, h):
        i = jnp.maximum(j - skip, 0)
        return i // per, 0, i % per

    part = pl.BlockSpec((1, rows, bn), part_index)
    in_specs = [part, part, whole, gain.spec] + w.blocks(bn, number > 0)
    args = [own, back, x, gain.array, *w.arrays]
    if has_q:
        in_specs.insert(0, pl.BlockSpec((1, rows, bn), lambda j, h: (2, 0, jnp.minimum(j, per - 1))))
        args.insert(0, gq)
    if has_above:
        in_specs.append(whole)
        args.append(above)
    row = sds((1, width), F32)
    return call(
        body,
        name,
        half,
        (steps,),
        in_specs,
        [
            pl.BlockSpec((rows, bn), lambda j, h: (0, j)),
            pl.BlockSpec((1, bn), lambda j, h: (0, j)),
            whole,
            vec,
            vec,
        ],
        [
            sds((rows, w.columns), BF),
            sds((1, w.columns), F32),
            sds((rows, width), F32 if has_above and n_w == 2 else BF),
            row,
            row,
        ],
        args,
        [pltpu.VMEM((rows, width), F32)],
        ride=ride,
        number=number,
        mirror=[(0, [(i, columns_at(i, bn)) for i in range(steps)])],
    )


def weight_blocks(place, mine, far, g, g_far, nz, width, bn, name, base=None, at=0, total=None):
    _, rb, rows = mine.shape
    per = width // bn
    units = bn // 128
    total = total or width // 128 * rb
    group = max(1, 512 // rb)

    def body(place_ref, a_ref, b_ref, g_ref, gf_ref, *rest):
        out, lhs = rest[-2:]

        @pl.when((pl.program_id(0) == 0) & (pl.program_id(1) == 0))
        def _():
            for s in range(4):
                lhs[s * rb : (s + 1) * rb, :rows] = a_ref[place_ref[nz + s]]
                lhs[s * rb : (s + 1) * rb, rows:] = b_ref[place_ref[nz + s]]

        grad = jnp.concatenate([g_ref[...].reshape(rows, bn), gf_ref[...].reshape(rows, bn)], axis=0)
        for c in range(0, 4, group):
            n = min(4 - c, group)
            y = mm(lhs[c * rb : (c + n) * rb, :], grad).astype(BF)
            for s in range(n):
                for u in range(units):
                    out[c + s, 0, u * rb : (u + 1) * rb, :] = y[
                        s * rb : (s + 1) * rb, u * 128 : (u + 1) * 128
                    ]

    if g.ndim == 3:
        columns = pl.BlockSpec((1, rows, bn), lambda i, j, z: (2, 0, z[i] * per + j))
    else:
        columns = pl.BlockSpec((rows, bn), lambda i, j, z: (0, z[i] * per + j))
    skip = at // (units * rb)
    in_specs = [full((4, rb, rows)), full((4, rb, rows)), columns, columns]
    args, aliases = [mine, far, g, g_far], {}
    if base is not None:
        in_specs.append(pl.BlockSpec(memory_space=pl.ANY))
        args.append(base)
        aliases[5] = 0
    return pl.pallas_call(
        body,
        grid_spec=pltpu.PrefetchScalarGridSpec(
            num_scalar_prefetch=1,
            grid=(nz, per),
            in_specs=in_specs,
            out_specs=pl.BlockSpec((4, 1, units * rb, 128), lambda i, j, z: (0, i, skip + j, 0)),
            scratch_shapes=[pltpu.VMEM((4 * rb, 2 * rows), BF)],
        ),
        out_shape=sds((4, nz, total, 128), BF),
        name=name,
        input_output_aliases=aliases,
        compiler_params=pltpu.CompilerParams(vmem_limit_bytes=VMEM),
        cost_estimate=cost(name),
    )(place, *args)


def swap(value, axis, distance):
    size = lax.axis_size(axis)
    return lax.ppermute(value, axis, [(i, i ^ distance) for i in range(size)])


def plus(a, b):
    return (a.astype(F32) + b.astype(F32)).astype(BF)


def chip_sum(blocks):
    groups = [[0, 2, 4, 6], [1, 3, 5, 7]]
    flat = blocks.reshape(-1, 128)
    out = lax.psum_scatter(flat, "pair", scatter_dimension=0, axis_index_groups=groups, tiled=True)
    return out.reshape(blocks.shape[1:])


STAY = ((0, 2), (0, 1))
AWAY = ((1, 3), (2, 3))
BITS = (2, 4)
AHEAD, LAGS, MARK = 4, (2, 4, 6), 4


def final_sums(mains, stacks, pairs, added, layout, shapes, vectors, traded):
    arrays, chunks, base = [array for array, _ in mains], [], 0
    for k, (array, parts) in enumerate(mains):
        chunks += [(k, row, count, order, base + row, array.shape[1]) for row, count, order in parts]
        base += array.shape[2]
    n, l_main = len(chunks), base
    l_stack = sum(array.shape[1] for array in stacks)
    l_pair = sum(array.shape[1] for array in pairs)
    n_arr, ns, np, na = len(arrays), len(stacks), len(pairs), len(added)
    enc_vectors, dec_vectors = vectors
    nv = len(enc_vectors) + len(dec_vectors)
    enc_count, dec_count = [sum(v.shape[1] for v in group) // 128 for group in vectors]
    vector_enc = -(-enc_count // 8) * 8
    rows = vector_enc + -(-dec_count // 8) * 8
    gain_rows, dec_gain = 2 * DE // 128, 4 * DD // 128
    dec_bias = dec_count - dec_gain
    ahead, (lag_two, lag_three, lag_four), mark = AHEAD, LAGS, MARK

    def body(*refs):
        m_refs, refs = refs[:n_arr], refs[n_arr:]
        s_refs, refs = refs[:ns], refs[ns:]
        p_refs, refs = refs[:np], refs[np:]
        a_refs, refs = refs[: 2 * na], refs[2 * na :]
        v_refs, refs = refs[:nv], refs[nv:]
        t_ref, *refs = refs
        outs, refs = refs[: len(shapes)], refs[len(shapes) :]
        (
            gains_out, biases_out, dec_gains_out, dec_biases_out, t_out, v_out, t_keep, t_in, t_send, t_recv,
            keep, got1, got2, got3, got4, s_keep, s_got3, s_got4, p_keep, p_got, a_keep, v_got,
            in_sem, send1, recv1, send2, recv2, send3, recv3, send4, recv4,
            s_in, s_send, s_recv, p_in, p_send, p_recv, a_in, v_send, v_recv,
        ) = refs
        core, x, y = across("pair", 1), across("pair", 2), across("pair", 4)
        z1, z2 = across("view", 1), across("view", 2)
        axes = (x, y)
        greet((core, x, y, z1, z2, slanted()))
        t_local = pltpu.make_async_copy(t_ref, t_keep, t_in)
        t_remote = pltpu.make_async_remote_copy(
            src_ref=t_ref, dst_ref=t_keep, send_sem=t_send, recv_sem=t_recv, device_id=slanted(),
            device_id_type=MESH,
        )

        @pl.when(stays())
        def _():
            t_local.start()

        @pl.when(jnp.logical_not(stays()))
        def _():
            t_remote.start()

        sent = []

        def send(src, dst, send_sem, recv_sem, device, late=True):
            copy = pltpu.make_async_remote_copy(
                src_ref=src, dst_ref=dst, send_sem=send_sem, recv_sem=recv_sem,
                device_id=device, device_id_type=MESH,
            )
            copy.start()
            if late:
                sent.append(copy)
            return copy

        def fetch(src, dst, sem):
            copy = pltpu.make_async_copy(src, dst, sem)
            copy.start()
            return copy

        def at(i):
            return pl.ds(chunks[i][4], chunks[i][2])

        def store(places, total):
            row = 0
            for count, out, column in places:
                outs[out][:, column : column + 128] = total[row : row + count]
                row += count

        one, two, three, four, loads = {}, {}, {}, {}, {}

        def start_one(i):
            k, row, count, order, _, nz = chunks[i]
            one[i] = [
                send(
                    m_refs[k].at[slot, :, pl.ds(row, count), :], got1.at[q, pl.ds(0, nz), at(i), :],
                    send1.at[i, q], recv1.at[i, q], axes[order],
                )
                for q, slot in enumerate(AWAY[order])
            ]

        def start_load(i):
            k, row, count, order, _, nz = chunks[i]
            loads[i] = [
                fetch(
                    m_refs[k].at[slot, :, pl.ds(row, count), :], keep.at[q, pl.ds(0, nz), at(i), :],
                    in_sem.at[i, q],
                )
                for q, slot in enumerate(STAY[order])
            ]

        def start_two(i):
            device = axes[1 - chunks[i][3]]
            nz = pl.ds(0, chunks[i][5])
            two[i] = send(
                keep.at[1, nz, at(i), :], got2.at[nz, at(i), :], send2.at[i], recv2.at[i], device
            )

        def start_three(i):
            three[i] = [
                send(keep.at[0, slot, at(i), :], got3.at[q, at(i), :], send3.at[i, q], recv3.at[i, q], z1)
                for q, slot in enumerate((1, 3)[: chunks[i][5] // 2])
            ]

        def start_four(i):
            four[i] = send(keep.at[0, 2, at(i), :], got4.at[at(i), :], send4.at[i], recv4.at[i], z2)

        for i in range(min(ahead, n)):
            start_one(i)
        for i in range(n):
            start_load(i)
        v_out[...] = jnp.zeros_like(v_out)
        row = 0
        for k, ref in enumerate(v_refs):
            row = vector_enc if k == len(enc_vectors) else row
            for u in range(ref.shape[1] // 128):
                v_out[row : row + 1, :] = ref[:, u * 128 : (u + 1) * 128]
                row += 1
        v_axes = (core, z1, z2, x, y)
        v_waits = {2: 0, 5: 1, 8: 2, n - 2: 3, n + 2: 4}

        def start_vector(r):
            count = vector_enc if r == 2 else rows
            return send(
                v_out.at[pl.ds(0, count), :], v_got.at[r, pl.ds(0, count), :],
                v_send.at[r], v_recv.at[r], v_axes[r], late=False,
            )

        flying = start_vector(0)
        offset, s_moves = 0, []
        for k, ref in enumerate(s_refs):
            size = ref.shape[1]
            where = pl.ds(offset, size)
            s_moves.append(
                (
                    [
                        send(ref.at[slot], s_got3.at[q, where, :], s_send.at[k, q], s_recv.at[k, q], z1)
                        for q, slot in enumerate((1, 3))
                    ],
                    [
                        fetch(ref.at[slot], s_keep.at[q, where, :], s_in.at[k, q])
                        for q, slot in enumerate((0, 2))
                    ],
                    where,
                )
            )
            offset += size
        offset, a_moves = 0, []
        for k in range(na):
            size = a_refs[2 * k].shape[1]
            where = pl.ds(offset, size)
            a_moves.append((fetch(a_refs[2 * k].at[0], a_keep.at[where, :], a_in.at[k]), where))
            offset += size
        offset, p_moves = 0, []
        for k, ref in enumerate(p_refs):
            where = pl.ds(offset, ref.shape[1])
            p_moves.append(
                (
                    send(ref.at[1], p_got.at[where, :], p_send.at[k], p_recv.at[k], z2),
                    fetch(ref.at[0], p_keep.at[where, :], p_in.at[k]),
                    where,
                )
            )
            offset += ref.shape[1]

        s_last = []
        for i in range(n + lag_four):
            if i < n:
                for copy in loads[i]:
                    copy.wait()
                for copy in one[i]:
                    copy.wait_recv()
                nz = pl.ds(0, chunks[i][5])
                keep[:, nz, at(i), :] = keep[:, nz, at(i), :] + got1[:, nz, at(i), :]
                start_two(i)
                if i + ahead < n:
                    start_one(i + ahead)
            j = i - lag_two
            if 0 <= j < n:
                two[j].wait_recv()
                nz = pl.ds(0, chunks[j][5])
                keep[0, nz, at(j), :] = keep[0, nz, at(j), :] + got2[nz, at(j), :]
                start_three(j)
            if i == mark:
                for k, (moves, reads, where) in enumerate(s_moves):
                    for copy in reads:
                        copy.wait()
                    for copy in moves:
                        copy.wait_recv()
                    for q in range(2):
                        s_keep[q, where, :] = s_keep[q, where, :] + s_got3[q, where, :]
                    s_last.append(
                        send(s_keep.at[1, where, :], s_got4.at[where, :], s_send.at[k, 2], s_recv.at[k, 2], z2)
                    )
            j = i - lag_three
            if 0 <= j < n:
                for copy in three[j]:
                    copy.wait_recv()
                if chunks[j][5] == 4:
                    keep[0, 0, at(j), :] = keep[0, 0, at(j), :] + got3[0, at(j), :]
                    keep[0, 2, at(j), :] = keep[0, 2, at(j), :] + got3[1, at(j), :]
                    start_four(j)
            j = i - lag_four
            if 0 <= j < n:
                row = chunks[j][4]
                if chunks[j][5] == 4:
                    four[j].wait_recv()
                    last = got4[at(j), :]
                else:
                    last = got3[0, at(j), :]
                total = keep[0, 0, at(j), :].astype(F32) + last.astype(F32)
                done = 0
                for count, out, column in main_places:
                    if done >= row and done < row + chunks[j][2]:
                        outs[out][:, column : column + 128] = total[done - row : done - row + count]
                    done += count
            if i in v_waits:
                r = v_waits[i]
                flying.wait()
                count = vector_enc if r == 2 else rows
                v_out[pl.ds(0, count), :] = v_out[pl.ds(0, count), :] + v_got[r, pl.ds(0, count), :]
                if r < 4:
                    flying = start_vector(r + 1)
            if i == n - 1:
                for k in range(na):
                    read, where = a_moves[k]
                    read.wait()
                    total = a_keep[where, :].astype(F32) + a_refs[2 * k + 1][...].astype(F32)
                    store(layout[len(mains) + ns + np + k], total)
                for k, (move, read, where) in enumerate(p_moves):
                    read.wait()
                    move.wait_recv()
                    total = p_keep[where, :].astype(F32) + p_got[where, :].astype(F32)
                    store(layout[len(mains) + ns + k], total)
            if i == n + lag_four - 1:
                for k, (copy, (_, _, where)) in enumerate(zip(s_last, s_moves)):
                    copy.wait_recv()
                    total = s_keep[0, where, :].astype(F32) + s_got4[where, :].astype(F32)
                    store(layout[len(mains) + k], total)
        gains_out[...] = v_out[:gain_rows]
        biases_out[...] = v_out[gain_rows:enc_count]
        first = lax.axis_index("view") % 2 == 0
        for out, base, count in ((dec_gains_out, 0, dec_gain), (dec_biases_out, dec_gain, dec_bias)):
            start, half = vector_enc + base, count // 2
            one, two_ = v_out[start : start + half], v_out[start + half : start + count]
            out[...] = jnp.where(first, one, two_)

        @pl.when(stays())
        def _():
            t_local.wait()

        @pl.when(jnp.logical_not(stays()))
        def _():
            t_remote.wait()

        t_out[...] = t_keep[...].astype(F32)
        for copy in sent:
            copy.wait_send()

    main_places = [place for part in layout[: len(mains)] for place in part]

    def vmem(*shape, dtype=BF):
        return pltpu.VMEM(shape, dtype)

    dma = pltpu.SemaphoreType.DMA
    hbm = pl.BlockSpec(memory_space=pl.ANY)
    inside = pl.BlockSpec(memory_space=pltpu.VMEM)
    return pl.pallas_call(
        body,
        in_specs=[hbm] * (n_arr + ns + np)
        + [hbm, inside] * na
        + [inside] * nv
        + [hbm],
        out_specs=[inside] * (len(shapes) + 5),
        out_shape=[sds(shape, F32) for shape in shapes]
        + [sds((count, 128), F32) for count in (gain_rows, enc_count - gain_rows, dec_gain // 2, dec_bias // 2)]
        + [sds(traded.shape, F32)],
        scratch_shapes=[
            pltpu.VMEM((rows, 128), F32),
            pltpu.VMEM(traded.shape, BF),
            pltpu.SemaphoreType.DMA,
            pltpu.SemaphoreType.DMA,
            pltpu.SemaphoreType.DMA,
            vmem(2, 4, l_main, 128),
            vmem(2, 4, l_main, 128),
            vmem(4, l_main, 128),
            vmem(2, l_main, 128),
            vmem(l_main, 128),
            vmem(2, l_stack, 128),
            vmem(2, l_stack, 128),
            vmem(l_stack, 128),
            vmem(l_pair, 128),
            vmem(l_pair, 128),
            vmem(sum(array.shape[1] for array, _ in added), 128),
            vmem(5, rows, 128, dtype=F32),
            dma((n, 2)),
            dma((n, 2)),
            dma((n, 2)),
            dma((n,)),
            dma((n,)),
            dma((n, 2)),
            dma((n, 2)),
            dma((n,)),
            dma((n,)),
            dma((ns, 2)),
            dma((ns, 3)),
            dma((ns, 3)),
            dma((np,)),
            dma((np,)),
            dma((np,)),
            dma((na,)),
            dma((5,)),
            dma((5,)),
        ],
        name="final_sums",
        compiler_params=pltpu.CompilerParams(
            vmem_limit_bytes=VMEM, collective_id=1, has_side_effects=True
        ),
        cost_estimate=pl.CostEstimate(flops=int(100 * SCALE), bytes_accessed=0, transcendentals=0),
    )(*arrays, *stacks, *pairs, *(a for pair in added for a in pair), *enc_vectors, *dec_vectors, traded)


def hand_over(arrays, vectors):
    ins = [*arrays, *vectors]
    shapes = [array.shape for array in ins]
    shapes[4] = (DD // 4, shapes[4][0])

    def body(*refs):
        for k, (source, target) in enumerate(zip(refs[: len(ins)], refs[len(ins) :])):
            target[...] = source[...].T[: DD // 4] if k == 4 else source[...]

    inside = pl.BlockSpec(memory_space=pltpu.VMEM)
    return pl.pallas_call(
        body,
        in_specs=[inside] * len(ins),
        out_specs=[inside] * len(ins),
        out_shape=[sds(shape, array.dtype) for shape, array in zip(shapes, ins)],
        name="hand_over",
        compiler_params=pltpu.CompilerParams(vmem_limit_bytes=VMEM),
    )(*ins)


def after(value, *deps):
    return lax.optimization_barrier((value, *deps))[0]


def spread(units):
    return jnp.transpose(units, (1, 0, 2)).reshape(units.shape[1], -1)


def tables(place):
    lane = jnp.arange(128)
    frequency = 100.0 ** (-(lane % 16).astype(F32) * 2.0 / 32.0)
    position = jnp.where((lane % 64 < 32)[None, :], place[0][:, None], place[1][:, None])
    angle = position * frequency[None, :]
    sin = jnp.sin(angle)
    return jnp.cos(angle), jnp.where((lane % 32 < 16)[None, :], -sin, sin)


def local(
    tokens,
    out_grad,
    masks,
    coords,
    enc_qkv,
    enc_out,
    enc_up,
    enc_down,
    enc_gains,
    enc_biases,
    proj,
    dec_in,
    dec_outs,
    dec_down,
    dec_gains,
    dec_biases,
):
    n_pair, n_view = lax.axis_size("pair"), lax.axis_size("view")
    quarter, pair_id = lax.axis_index("view"), lax.axis_index("pair")
    half_id, view_id, core = quarter % 2, quarter // 2, pair_id % 2
    half = jnp.stack([half_id, core]).astype(jnp.int32)
    rows = tokens.shape[1]
    tokens = tokens[0]
    d_gd = (out_grad[0].astype(F32) * masks[0].astype(F32)[:, None]).astype(BF)
    chip_plan = n_pair == 8 and n_view == 4

    def trade(value):
        moves = []
        for p in range(n_pair):
            for t in range(n_view):
                moves.append((p * n_view + t, (p - p % 2 + t % 2) * n_view + t - t % 2 + p % 2))
        return lax.ppermute(value, ("pair", "view"), moves)

    tokens = trade(tokens)
    far_coords = swap(coords[:, 0], "pair", 1)
    far_small = swap(jnp.concatenate([dec_gains, dec_biases]), "view", 1)
    place = jnp.where(core == half_id, coords[:, 0], far_coords).astype(F32)

    def seg(view, half_of):
        return lax.dynamic_slice_in_dim(place, (view * 2 + half_of) * rows, rows, 1)

    cos_all, sin_all = tables(jnp.concatenate([seg(view_id, core), seg(view_id, 1 - core)], axis=1))
    cos_oth, sin_oth = tables(
        jnp.concatenate([seg(1 - view_id, core), seg(1 - view_id, 1 - core)], axis=1)
    )
    back_all, back_oth = -sin_all, -sin_oth

    def join_row(mine, theirs):
        return jnp.where(
            half_id == 0, jnp.concatenate([mine, theirs]), jnp.concatenate([theirs, mine])
        ).astype(F32)[None]

    n_gains = dec_gains.shape[0]
    dec_scale = join_row(dec_gains, far_small[:n_gains])
    dec_shift = join_row(dec_biases, far_small[n_gains:])
    enc_scale, enc_shift = enc_gains.astype(F32)[None], enc_biases.astype(F32)[None]
    tokens = after(
        tokens, cos_all, sin_all, cos_oth, sin_oth, back_all, back_oth, dec_scale, dec_shift, d_gd,
        enc_scale, enc_shift,
    )

    s3 = 3 * DD

    def share(array):
        if not chip_plan:
            return array
        count = array.shape[0] // n_pair
        return lax.dynamic_slice_in_dim(array, pair_id * count, count, 0)

    def gather(array):
        return lax.all_gather(array, "pair", axis=0, tiled=True) if chip_plan else array

    s1 = s3 // 2
    own_in = share(dec_in)
    first_piece = own_in[:, :s1]
    second_piece = jnp.concatenate([own_in[:, s1:s3], share(dec_outs)], axis=1)
    third_piece = jnp.concatenate(
        [own_in[:, s3:], share(dec_down).reshape(own_in.shape[0], -1)], axis=1
    )

    start = 4 * DE + FE
    g1, g2 = Row(enc_scale, 0, DE), Row(enc_scale, DE, DE)
    sh1, sh2 = Row(enc_shift, start + DE, DE), Row(enc_shift, start + 2 * DE, DE)
    own_tables = (cos_all, sin_all)
    deps = []

    def pend(*values):
        deps.extend(values)

    def tie(value):
        out = after(value, *deps) if deps else value
        deps.clear()
        return out

    def core_ride(*arrays):
        return [(array, [()], "pair", 1) for array in arrays]

    e_q, e_kv, *e_n1, first_piece, e_kvf = lnproj(
        half, tokens, g1, sh1, Whole(enc_qkv), Row(enc_shift, 0, 3 * DE), *own_tables, 1, 2, 3,
        "enc_qkv", ride=[(first_piece, [()], "view", 1)], number=9,
    )
    far_first = gather(first_piece[0])
    e_p, e_l, e_o, *e_ot, second_piece = attend(
        half, e_q, e_kv, e_kvf, "enc_attend", ride=[(second_piece, [()], "view", 1)], number=16
    )
    far_second = gather(second_piece[0])
    e_x1, e_n2, e_nt, e_am, e_at, e_slope, z, e_xm, e_xt, third_piece = ffn_forward(
        half, e_o, tokens, Whole(enc_out), Row(enc_shift, 3 * DE, DE), g2, sh2, Whole(enc_up),
        Row(enc_shift, 4 * DE, FE), Whole(enc_down), Row(enc_shift, start, DE),
        (proj, Row(enc_shift, start + 3 * DE, DD)), 1024, "enc_ffn",
        ride=[(third_piece, [()], "view", 1)], number=17,
    )
    far_third = gather(third_piece[0])
    cut = rows // 48 * 16 + 16
    upper, lower = (slice(0, cut),), (slice(cut, rows),)

    w_sqkv = Halves((dec_in, 0), (far_first, 0), 3 * DD // 2)
    w_cq = Halves((dec_in, s1), (far_second, 0), DD // 2)
    w_ckv = Halves((dec_in, 2 * DD), (far_second, DD // 2), DD)
    w_so = Halves((dec_outs, 0), (far_second, s1), DD // 2)
    w_co = Halves((dec_outs, DD // 2), (far_second, 2 * DD), DD // 2)
    ga, gb, gc, gd = [Row(dec_scale, i * DD, DD) for i in range(4)]
    sa, sb, sc, sd = [Row(dec_shift, i * DD, DD) for i in range(4)]
    bias = lambda i, n=1: Row(dec_shift, i * DD, n * DD)
    tied = lambda row: Row(tie(row.array), row.start, row.size)
    s_q, s_kv, *s_nt, z_one, s_kvf = lnproj(
        half, z, ga, sa, w_sqkv, bias(4, 3), *own_tables, 2, 4, 6,
        "dec_qkv", ride=[(z, [upper], "view", 2)], number=6,
    )
    s_p, s_l, s_o, *s_ot, z_two, f_n1, f_ot, f_nt, f_at, f_xt = attend(
        half, s_q, s_kv, s_kvf, "self_attend",
        ride=[(z, [lower], "view", 2)] + core_ride(e_n1[1], e_ot[1], e_nt, e_at, e_xt), number=7,
    )
    e_n1, e_ot, e_nt, e_at, e_xt = [
        (mine, far[0], theirs)
        for mine, far, theirs in (
            (e_n1[0], f_n1, e_n1[1]), (e_ot[0], f_ot, e_ot[1]), (e_n2, f_nt, e_nt), (e_am, f_at, e_at),
            (e_xm, f_xt, e_xt),
        )
    ]
    other_z = jnp.concatenate([z_one[0], z_two[0]])
    far_third = after(far_third, s_o)
    far_down = far_third[:, FD // 2 :].reshape(dec_down.shape)
    w_up = Halves((dec_in, s3), (far_third, 0), FD // 2)
    w_down = Halves((dec_down, 0), (far_down, 0), DD // 2)
    y1, c_q, *b_nt = mid_forward(
        half, s_o, z, w_so, bias(7), gb, sb, w_cq, bias(8), *own_tables, "dec_mid",
    )
    pend(y1)
    c_kv, *c_nt, c_kvf = lnproj(
        half, other_z, tied(gc), sc, w_ckv, bias(9, 2), cos_oth, sin_oth, 0, 2, 4, "dec_ckv", number=10,
    )
    c_p, c_l, c_o, *c_ot, d_gd, f_sn, f_so, f_bn, f_cn = attend(
        half, c_q, c_kv, c_kvf, "cross_attend",
        ride=[(d_gd, [()], "trade", 0)] + core_ride(s_nt[1], s_ot[1], b_nt[1], c_nt[1]), number=11,
    )
    d_gd = d_gd[0]
    s_nt, s_ot, b_nt, c_nt = [
        (mine, far[0], theirs)
        for (mine, theirs), far in zip((s_nt, s_ot, b_nt, c_nt), (f_sn, f_so, f_bn, f_cn))
    ]
    y2, d_nm, d_nt, d_am, d_at, d_slope, mixed = ffn_forward(
        half, c_o, y1, w_co, bias(11), gd, sd, w_up, Row(dec_shift, 12 * DD, FD), w_down,
        Row(dec_shift, 12 * DD + FD, DD), None, 768, "dec_ffn",
    )

    chip = pair_id // 2
    pack = lambda *ids: jnp.stack([jnp.asarray(i, jnp.int32) for i in ids])
    dec_z = pack(half_id, 1 - half_id, 0, 1, 2, 3)
    dec_near = pack(half_id, 1 - half_id, chip, chip ^ 1, chip ^ 2, chip ^ 3)
    enc_z = pack(quarter, quarter ^ 1, quarter ^ 2, quarter ^ 3, 0, 1, 2, 3)
    enc_near = pack(
        quarter, quarter ^ 1, quarter ^ 2, quarter ^ 3, chip, chip ^ 1, chip ^ 2, chip ^ 3
    )

    def blocks(plan, a, g, far, width, bn, name, **rest):
        if not chip_plan:
            return None
        nz = plan.shape[0] - 4
        out = weight_blocks(tie(plan), a[0], a[1], g, far, nz, width, bn, name, **rest)
        pend(out)
        return out

    def summed(out):
        return chip_sum(out) if chip_plan else None

    d_gu, d_gco, grad_y2, d_doc, vb_down, vb_up, vg_d, vs_d, vb_co, f_at, f_nt, f_ot, far_gd, far_gu = (
        ffn_backward(
            half, d_gd, None, w_down, d_slope, w_up, y2, gd, w_co, 768, "dec_ffn_back",
            ride=core_ride(d_at, d_nt, c_ot[1], d_gd), number=12,
        )
    )
    d_at, d_nt, c_ot = (d_am, f_at[0], d_at), (d_nm, f_nt[0], d_nt), (c_ot[0], f_ot[0], c_ot[1])
    ffn = blocks(dec_z, d_at, d_gd, far_gd[0], 384, 384, "dw_dec_down", total=2304)
    t_ffn = summed(
        blocks(dec_z, d_nt, d_gu, far_gu, 1536, 1536, "dw_dec_up", base=ffn, at=1152, total=2304)
    )
    c_own, c_ship, mixed, far_gco, c_back = attend_back(
        half, c_q, c_kv, c_kvf, c_p, c_l, c_o, tie(d_doc), cos_all, back_all, cos_oth, back_oth,
        "cross_back", ride=[(mixed, [()], "trade", 0)] + core_ride(d_gco), number=13,
    )
    mixed = mixed[0]
    g_ckv, vb_ckv, grad_other, vg_c, vs_c, far_ckv = proj_backward(
        half, None, c_own, c_back, w_ckv, other_z, gc, None, 384, "ckv_back", number=14
    )
    pend(g_ckv)
    grad_y1, d_gso, d_dos, vb_cq, vg_b, vs_b, vb_so = mid_backward(
        half, c_ship, w_cq, y1, tied(gb), grad_y2, w_so, "mid_back"
    )
    cross = blocks(dec_z, c_ot, d_gco, far_gco[0], 384, 384, "dw_co", total=1152)
    cross = blocks(dec_z, b_nt, c_ship, c_back, 384, 384, "dw_cq", base=cross, at=288, total=1152)
    t_cross = summed(
        blocks(dec_z, c_nt, g_ckv, far_ckv, 768, 768, "dw_ckv", base=cross, at=576, total=1152)
    )
    s_own, s_ship, returned, far_gso, s_back = attend_back(
        half, s_q, s_kv, s_kvf, s_p, s_l, s_o, tie(d_dos), cos_all, back_all, cos_all, back_all, "self_back",
        ride=[(grad_other, [lower], "view", 2)] + core_ride(d_gso), number=2,
    )
    g_sqkv, vb_sqkv, grad_own, vg_a, vs_a, returned_up, far_sqkv = proj_backward(
        half, s_ship, s_own, s_back, w_sqkv, z, ga, grad_y1, 384, "qkv_back",
        ride=[(grad_other, [upper], "view", 2)], number=8,
    )
    returned = (returned_up[0], returned[0])
    e_gp, ub_proj, grad_x2, e_gd, far_gp, far_egd = head_backward(
        half, grad_own, returned, proj, "proj_back", 15
    )
    t_enc_down = summed(blocks(enc_z, e_at, e_gd, far_egd, 256, 256, "dw_enc_down"))
    selfs = blocks(dec_near, s_ot, d_gso, far_gso[0], 384, 384, "dw_so", total=1152)
    selfs = blocks(dec_near, s_nt, g_sqkv, far_sqkv, 1152, 384, "dw_sqkv", base=selfs, at=288, total=1152)
    e_gu, e_go, grad_x1, e_do, ub_down, ub_up, ug_2, us_2, ub_out, *dec_got, far_egu = ffn_backward(
        half, e_gd, grad_x2, Whole(enc_down), e_slope, Whole(enc_up), e_x1, tied(g2), Whole(enc_out),
        1024, "enc_ffn_back", ride=[(t_ffn, [(1,)], "view", 1)] if chip_plan else (),
        number=3,
    )
    pend(e_do)
    t_enc_up = summed(blocks(enc_z, e_nt, e_gu, far_egu, 1024, 1024, "dw_enc_up"))
    e_three = blocks(enc_near, e_xt, e_gp, far_gp, 256, 256, "dw_proj", at=1024, total=1280)
    rides = [(t_cross, [(1,)], "view", 1)] if chip_plan else []
    e_own, e_ship, *rode, far_go, e_back = attend_back(
        half, e_q, e_kv, e_kvf, e_p, e_l, e_o, tie(e_do), cos_all, back_all, cos_all, back_all, "enc_back",
        ride=rides + core_ride(e_go), number=4,
    )
    if chip_plan:
        ffn_got, cross_got = [got[0] for got in (*dec_got, *rode)]
    pend(e_own)
    e_three = blocks(
        enc_near, e_ot, e_go, far_go[0], 256, 256, "dw_out", base=e_three, at=768, total=1280
    )
    rides = [(t_enc_down, [(1,), (3,)], "view", 1)] if chip_plan else []
    g_eqkv, ub_qkv, tokens_grad, ug_1, us_1, *rode, far_eqkv = proj_backward(
        half, e_ship, e_own, e_back, Whole(enc_qkv), tokens, tied(g1), grad_x1, 1024, "enc_qkv_back",
        ride=rides, number=5,
    )
    e_three = blocks(
        enc_near, e_n1, g_eqkv, far_eqkv, 768, 768, "dw_enc_qkv", base=e_three, total=1280
    )

    if chip_plan:
        vectors = (
            [ug_1, ug_2, ub_qkv, ub_out, ub_up, ub_down, us_1, us_2, ub_proj],
            [
                vg_a, vg_b, vg_c, vg_d, vs_a, vs_b, vs_c, vs_d,
                vb_sqkv, vb_so, vb_cq, vb_ckv, vb_co, vb_up, vb_down,
            ],
        )
        t_enc_down = after(t_enc_down, g_eqkv)
        t_enc_down = plus(jnp.stack([t_enc_down[0], t_enc_down[2]]), rode[0])
        mains = [
            (e_three, [(128 * c, 128, c % 2) for c in range(10)]),
            (selfs, [(288 * c, 288, c % 2) for c in range(4)]),
        ]
        added = [(t_ffn, ffn_got), (t_cross, cross_got)]
        shapes = [
            (DE // 8, 3 * DE // 4), (DE // 8, DE // 4), (DE // 8, FE // 4), (FE // 8, DE // 4),
            (DE // 8, 256), (DD // 8, 3 * DD + FD // 2), (DD // 8, DD), (FD // 8, DD // 2),
        ]

        def run(count, units, out, column):
            return [(count, out, column + 128 * u) for u in range(units)]

        layout = [
            run(128, 6, 0, 0) + run(128, 2, 1, 0) + run(128, 2, 4, 0),
            run(96, 3, 6, 0) + run(96, 9, 5, 0),
            run(128, 8, 2, 0),
            run(512, 2, 3, 0),
            run(384, 3, 7, 0) + run(96, 12, 5, 3 * DD),
            run(96, 3, 6, DD // 2) + run(96, 3, 5, 3 * DD // 2) + run(96, 6, 5, 2 * DD),
        ]
        results = final_sums(
            mains, [t_enc_up], [t_enc_down], added, layout, shapes, vectors, tokens_grad
        )
        (
            enc_qkv_grad, enc_out_grad, enc_up_grad, enc_down_grad, proj_grad, dec_in_grad,
            dec_outs_grad, dec_down_grad, tokens_grad, mixed, *vectors,
        ) = hand_over([*results[:8], results[12], mixed], results[8:12])
        proj_grad = proj_grad.T
        enc_gains_grad, enc_biases_grad, dec_gains_grad, dec_biases_grad = [
            v.reshape(-1) for v in vectors
        ]
    else:
        def tall(pieces):
            mine, _, theirs = pieces
            even, odd = jnp.where(core == 0, mine, theirs), jnp.where(core == 0, theirs, mine)
            return jnp.stack([even, odd], axis=1).reshape(-1, rows)

        def scatter(value, axis, dim):
            return lax.psum_scatter(value.astype(BF), axis, scatter_dimension=dim, tiled=True)

        def enc_sum(a, g):
            return scatter(scatter(mm(tall(a), g), "pair", 0), "view", 1).astype(F32)

        def halves(value, which):
            width = value.shape[1] // 2
            return lax.dynamic_slice_in_dim(value, which * width, width, 1)

        def dec_sum(*pairs):
            blocks = [mm(tall(a), g) for a, g in pairs]
            mine = jnp.concatenate([halves(b, half_id) for b in blocks], axis=1)
            other = jnp.concatenate([halves(b, 1 - half_id) for b in blocks], axis=1)
            both = mine + swap(other.astype(BF), "view", 1).astype(F32)
            return scatter(both, "pair", 0).astype(F32)

        dec_in_grad = dec_sum((s_nt, g_sqkv), (b_nt, c_ship[2]), (c_nt, g_ckv), (d_nt, d_gu))
        dec_outs_grad = dec_sum((s_ot, d_gso), (c_ot, d_gco))
        dec_down_grad = dec_sum((d_at, d_gd))
        enc_qkv_grad, enc_out_grad = enc_sum(e_n1, g_eqkv), enc_sum(e_ot, e_go)
        enc_up_grad, enc_down_grad = enc_sum(e_nt, e_gu), enc_sum(e_at, e_gd)
        proj_grad = enc_sum(e_xt, e_gp.reshape(rows, 4, -1)[:, :, : DD // 4].reshape(rows, DD))

    if not chip_plan:
        tokens_grad = trade(tokens_grad).astype(F32)
        dec_vec = jnp.concatenate(
            [
                vg_a, vg_b, vg_c, vg_d, vs_a, vs_b, vs_c, vs_d,
                vb_sqkv, vb_so, vb_cq, vb_ckv, vb_co, vb_up, vb_down,
            ],
            axis=1,
        )[0]
        empty = jnp.zeros_like(dec_vec)
        enc_parts = [ug_1, ug_2, ub_qkv, ub_out, ub_up, ub_down, us_1, us_2, ub_proj]
        enc_vec, dec_one, dec_two = lax.psum(
            (
                jnp.concatenate(enc_parts, axis=1)[0],
                jnp.where(view_id == 0, dec_vec, empty),
                jnp.where(view_id == 0, empty, dec_vec),
            ),
            ("pair", "view"),
        )
        dec_vec = jnp.where(view_id == 0, dec_one, dec_two)
        enc_gains_grad, enc_biases_grad = enc_vec[: 2 * DE], enc_vec[2 * DE :]
        gain_all, bias_all = dec_vec[: 4 * DD], dec_vec[4 * DD :]
        gain_part, bias_part = gain_all.shape[0] // 2, bias_all.shape[0] // 2
        dec_gains_grad = lax.dynamic_slice_in_dim(gain_all, half_id * gain_part, gain_part, 0)
        dec_biases_grad = lax.dynamic_slice_in_dim(bias_all, half_id * bias_part, bias_part, 0)
    return (
        mixed[None],
        tokens_grad[None],
        enc_qkv_grad,
        enc_out_grad,
        enc_up_grad,
        enc_down_grad,
        enc_gains_grad,
        enc_biases_grad,
        proj_grad,
        dec_in_grad,
        dec_outs_grad,
        dec_down_grad,
        dec_gains_grad,
        dec_biases_grad,
    )


def solution(mesh):
    both = P("pair", "view")
    return jax.shard_map(
        local,
        mesh=mesh,
        in_specs=(
            P("pair", "view", None),
            P("pair", "view", None),
            both,
            P(None, "pair", None),
            P(),
            P(),
            P(),
            P(),
            P(),
            P(),
            P(),
            P(None, "view"),
            P(None, "view"),
            P(None, "view"),
            P("view"),
            P("view"),
        ),
        out_specs=(
            P("pair", "view", None),
            P("pair", "view", None),
            both,
            both,
            both,
            both,
            P(),
            P(),
            both,
            both,
            both,
            both,
            P("view"),
            P("view"),
        ),
        check_vma=False,
    )
```
